32 devices in a mesh: rows: 8 (over z, x), lat: 4 (over y, core).
Axes of the slice: x: 2, y: 2, z: 4, core: 2. Of those that a mesh axis runs over, the one named last changes fastest.
Arguments:
- token_ids: int32 [32768], P('rows'), may hold values from 0 to 50303
- token_mask: int32 [32768], P('rows'), may hold values from 0 to 1
- scale_index: int32 [32768], P('rows'), may hold values from 0 to 7
- embed: bfloat16 [50304, 512], P('lat'), may hold values from -6 to 6
- norm_params: float32 [4, 512], replicated
- frozen_bias: float32 [4608], replicated, may hold values from -2 to 2
- w_joined: bfloat16 [512, 1536], replicated, may hold values from -0.25 to 0.25
- w_attn_out: bfloat16 [512, 512], replicated, may hold values from -1 to 1
- w_mlp_in: bfloat16 [512, 2048], replicated, may hold values from -0.25 to 0.25
- w_mlp_out: bfloat16 [2048, 512], replicated, may hold values from -0.1875 to 0.1875
- enc_weight: float32 [512, 16384], P('rows', 'lat'), may hold values from -0.25 to 0.25
- enc_moment: float32 [512, 16384], P('rows', 'lat'), may hold values from -6.1035156e-05 to 6.1035156e-05
- enc_second: float32 [512, 16384], P('rows', 'lat'), may hold values from 7.2759577e-13 to 1.1641532e-11
- dec_weight: float32 [16384, 512], P('lat', 'rows')
- dec_moment: float32 [16384, 512], P('lat', 'rows'), may hold values from -0.00048828125 to 0.00048828125
- dec_second: float32 [16384, 512], P('lat', 'rows'), may hold values from 5.960465e-11 to 9.536744e-10
- enc_bias: float32 [16384], P('lat')
- enc_bias_moment: float32 [16384], P('lat'), may hold values from -0.0034179688 to 0.0034179688
- enc_bias_second: float32 [16384], P('lat'), may hold values from 2.1457671e-09 to 3.4332274e-08
- dec_bias: float32 [512], replicated, may hold values from -6 to 6
- dec_bias_moment: float32 [512], replicated, may hold values from -0.01171875 to 0.01171875
- dec_bias_second: float32 [512], replicated, may hold values from 2.384186e-10 to 3.8146974e-09
Outputs:
- enc_weight_new: float32 [512, 16384], P('rows', 'lat')
- enc_moment_new: float32 [512, 16384], P('rows', 'lat')
- enc_second_new: float32 [512, 16384], P('rows', 'lat')
- dec_weight_new: float32 [16384, 512], P('lat', 'rows')
- dec_moment_new: float32 [16384, 512], P('lat', 'rows')
- dec_second_new: float32 [16384, 512], P('lat', 'rows')
- enc_bias_new: float32 [16384], P('lat')
- enc_bias_moment_new: float32 [16384], P('lat')
- enc_bias_second_new: float32 [16384], P('lat')
- dec_bias_new: float32 [512], replicated
- dec_bias_moment_new: float32 [512], replicated
- dec_bias_second_new: float32 [512], replicated
- grad_norm: float32 [], replicated
- loss_sum: float32 [], replicated
- token_count: float32 [], replicated
The draws below stay inside these ranges and needn't reach their ends.
All inputs are finite; a program needn't handle non-finite values.
Results may differ from the reference program's by a relative error of at most 0.0003.
The reference program's roundings to bfloat16 on the way count: a program that leaves them out, or rounds other values in their place, can miss the bound.
Values may be sent and summed in bfloat16 or wider, within the bound.
A program may use at most 256 MiB of HBM per device.

```python
import math
import jax
import jax.numpy as jnp
import numpy as np
from jax import lax

D = 512
HEADS = 8
ROT = 16
FF = 2048
VOCAB = 50304
LAT = 16384
STEP = 10
TOK_DEV = 1024
TOKENS = 32768


def draw_token_mask(key, part):
    key = jax.random.fold_in(key, 2)
    places = jnp.arange(TOKENS, dtype=jnp.int32)
    threshold = 250 + 500 * places // TOKENS
    picks = jax.random.randint(key, (TOKENS,), 0, 1000, dtype=jnp.int32)
    return (picks < threshold).astype(jnp.int32)


def draw_norm_params(key, part):
    key = jax.random.fold_in(key, 1)
    first, second = jax.random.split(key)
    gains = 1.0 + 0.1 * jax.random.normal(first, (2, D), jnp.float32)
    shifts = 0.2 * jax.random.normal(second, (2, D), jnp.float32)
    return jnp.stack([gains[0], shifts[0], gains[1], shifts[1]])


def draw_dec_weight(key, part):
    key = jax.random.fold_in(key, 3)
    first, second = jax.random.split(key)
    base = jax.random.normal(first, (LAT, D), jnp.float32) * LAT ** (-0.5)
    growth = 3.0
    ramp = growth ** (jnp.arange(LAT, dtype=jnp.float32) / LAT)
    row_factor = jnp.exp(jax.random.uniform(second, (LAT, 1), jnp.float32, -0.35, 0.35))
    return base * ramp[:, None] * row_factor


def draw_enc_bias(key, part):
    key = jax.random.fold_in(key, 4)
    lowest = -2.75
    rise = 1.5
    ramp = lowest + rise * jnp.arange(LAT, dtype=jnp.float32) / LAT
    return ramp + jax.random.uniform(key, (LAT,), jnp.float32, -0.75, 0.75)


def set_ends(array, key, smallest, top_value):
    spot = [jax.random.randint(jax.random.fold_in(key, axis), (), 0, length) for axis, length in enumerate(array.shape)]
    longest = array.shape.index(max(array.shape))
    neighbour = spot[:longest] + [(spot[longest] + 1) % array.shape[longest]] + spot[longest + 1:]
    return array.at[tuple(spot)].set(smallest).at[tuple(neighbour)].set(top_value)


def level_of(rng, shape, cuts, least, top_value):
    level, own = 1.0, jax.random.fold_in(rng, 6)
    for position, parts in cuts:
        heights = jnp.exp(jax.random.uniform(jax.random.fold_in(own, position), (parts,), jnp.float32, least / len(cuts), top_value / len(cuts)))
        level = level * jnp.repeat(heights, shape[position] // parts).reshape([-1 if axis == position else 1 for axis in range(len(shape))])
    return level


def rank_table(count, skew):
    loads = [(1 << 20) // math.isqrt(grade ** skew) + 1 for grade in range(1, count + 1)]
    scale = 1 + sum(loads) // (1 << 30)
    return np.cumsum(np.array([max(1, weight // scale) for weight in loads]))


def ranked_ids(stream_key, shape, count, skew):
    table = rank_table(count, skew)
    ticket = jax.random.randint(jax.random.fold_in(stream_key, 1), shape, 0, int(table[count - 1]))
    grade = jnp.searchsorted(jnp.asarray(table, jnp.int32), ticket, side="right")
    return jax.random.permutation(jax.random.fold_in(stream_key, 2), count)[grade].astype(jnp.int32)


def noise(stream_key, shape, deviation, bound, shards=(), kind=jnp.bfloat16):
    entries = deviation * jax.random.normal(stream_key, shape, jnp.float32)
    if shards:
        entries = entries * level_of(stream_key, shape, shards, -0.22, 0.18)
    return jnp.clip(entries, -bound, bound).astype(kind)


def setup_inputs(seed: int = 0) -> dict:
    splits = jax.random.split(jax.random.key(seed), 23)
    token_ids = set_ends(ranked_ids(splits[0], (TOKENS,), VOCAB, 2), jax.random.fold_in(splits[0], 3), 0, VOCAB - 1).astype(jnp.int32)
    token_mask = draw_token_mask(jax.random.fold_in(splits[22], 71), 0)
    scale_index = set_ends(jax.random.randint(splits[2], (TOKENS,), 0, 8), jax.random.fold_in(splits[2], 1), 0, 7).astype(jnp.int32)
    embed = noise(splits[3], (VOCAB, D), 1.0, 6.0, ((0, 4),))
    norm_params = draw_norm_params(jax.random.fold_in(splits[22], 71), 0)
    frozen_bias = noise(splits[5], (5 * D + FF,), 0.3, 2.0, (), jnp.float32)
    w_joined = noise(splits[6], (D, 3 * D), D ** -0.5, 0.25)
    w_attn_out = noise(splits[7], (D, D), (D // 16) ** -0.5, 1.0)
    w_mlp_in = noise(splits[8], (D, FF), D ** -0.5, 0.25)
    w_mlp_out = noise(splits[9], (FF, D), (FF // 2) ** -0.5, 0.1875)
    enc_weight = noise(splits[10], (D, LAT), D ** -0.5, 0.25, ((0, 8), (1, 4)), jnp.float32)
    enc_moment = noise(splits[11], (D, LAT), (0.11 * (D * LAT) ** -0.5 * min(1, 20 * TOKENS ** -0.5)), 6.103515625e-05, ((0, 8), (1, 4)), jnp.float32)
    enc_second = jnp.clip(jnp.exp(math.log(1.1641532356165829e-11) - 2.7725887 * jax.random.uniform(splits[12], (D, LAT), jnp.float32) ** level_of(splits[12], (D, LAT), ((0, 8), (1, 4)), -0.2, 0.2)), 7.275957722603643e-13, 1.1641532356165829e-11)
    dec_weight = draw_dec_weight(jax.random.fold_in(splits[22], 71), 0)
    dec_moment = noise(splits[14], (LAT, D), (0.11 * (D * LAT) ** -0.5), 0.00048828125, ((0, 4), (1, 8)), jnp.float32)
    dec_second = jnp.clip(jnp.exp(math.log(9.536743617033494e-10) - 2.7725887 * jax.random.uniform(splits[15], (LAT, D), jnp.float32) ** level_of(splits[15], (LAT, D), ((0, 4), (1, 8)), -0.2, 0.2)), 5.960464760645934e-11, 9.536743617033494e-10)
    enc_bias = draw_enc_bias(jax.random.fold_in(splits[22], 71), 0)
    enc_bias_moment = noise(splits[17], (LAT,), (0.66 * (D * LAT) ** -0.5), 0.0034179688, ((0, 4),), jnp.float32)
    enc_bias_second = jnp.clip(jnp.exp(math.log(3.433227391269611e-08) - 2.7725887 * jax.random.uniform(splits[18], (LAT,), jnp.float32) ** level_of(splits[18], (LAT,), ((0, 4),), -0.2, 0.2)), 2.145767119543507e-09, 3.433227391269611e-08)
    dec_bias = noise(splits[19], (D,), 1.0, 6.0, (), jnp.float32)
    dec_bias_moment = noise(splits[20], (D,), (2.2 * (D * LAT) ** -0.5), 0.01171875, (), jnp.float32)
    dec_bias_second = jnp.clip(jnp.exp(jax.random.uniform(splits[21], (D,), jnp.float32, math.log(2.3841859042583735e-10), math.log(3.814697446813398e-09))), 2.3841859042583735e-10, 3.814697446813398e-09)
    return dict(token_ids=token_ids, token_mask=token_mask, scale_index=scale_index, embed=embed, norm_params=norm_params, frozen_bias=frozen_bias, w_joined=w_joined, w_attn_out=w_attn_out, w_mlp_in=w_mlp_in, w_mlp_out=w_mlp_out, enc_weight=enc_weight, enc_moment=enc_moment, enc_second=enc_second, dec_weight=dec_weight, dec_moment=dec_moment, dec_second=dec_second, enc_bias=enc_bias, enc_bias_moment=enc_bias_moment, enc_bias_second=enc_bias_second, dec_bias=dec_bias, dec_bias_moment=dec_bias_moment, dec_bias_second=dec_bias_second)


highest = lax.Precision.HIGHEST
lasso_coef = 5.0
clip_bound = 1.0
learn_rate = 0.03
beta_one = 0.9
beta_two = 0.999
adam_eps = 1e-08
weight_decay = 0.01

@jax.custom_vjp
def low(v):
    return lax.optimization_barrier(v.astype(jnp.bfloat16)).astype(jnp.float32)

@jax.custom_vjp
def low_back(v):
    return v

def low_keep(v):
    return (low(v), None)

def low_pass(kept, grad):
    return (grad,)

def back_keep(v):
    return (v, None)

def back_low(kept, grad):
    return (low(grad),)
low.defvjp(low_keep, low_pass)
low_back.defvjp(back_keep, back_low)

def layer_norm(values, gain, shift):
    centred = values - lax.optimization_barrier(jnp.mean(values, axis=-1, keepdims=True))
    spread = lax.optimization_barrier(jnp.mean(centred * centred, axis=-1, keepdims=True))
    return centred * lax.rsqrt(spread + 1e-05) * gain + shift

def rotary(values, rotated):
    length = values.shape[0]
    half = rotated // 2
    freqs = 10000.0 ** (-2.0 * jnp.arange(half, dtype=jnp.float32) / rotated)
    angles = jnp.arange(length, dtype=jnp.float32)[:, None] * freqs[None, :]
    cosines = jnp.concatenate([jnp.cos(angles), jnp.cos(angles)], -1)[:, None, :]
    sines = jnp.concatenate([jnp.sin(angles), jnp.sin(angles)], -1)[:, None, :]
    head = values[..., :rotated]
    turned = jnp.concatenate([-head[..., half:], head[..., :half]], -1)
    return jnp.concatenate([head * cosines + turned * sines, values[..., rotated:]], -1)

def frozen_layer(embedded, norm_params, frozen_bias, w_joined, w_attn_out, w_mlp_in, w_mlp_out):
    length, width = embedded.shape
    head_dim = width // HEADS
    hidden_units = w_mlp_in.shape[1]
    attn_in = low(layer_norm(embedded, norm_params[0], norm_params[1]))
    joined = jnp.dot(attn_in, w_joined, precision=highest) + frozen_bias[:3 * width]
    queries = low(rotary(joined[:, :width].reshape(length, HEADS, head_dim), ROT))
    keys = low(rotary(joined[:, width:2 * width].reshape(length, HEADS, head_dim), ROT))
    values = low(joined[:, 2 * width:].reshape(length, HEADS, head_dim))
    scores = jnp.einsum('qhd,khd->hqk', queries, keys, precision=highest) * head_dim ** (-0.5)
    places = jnp.arange(length)
    causal = places[None, :, None] >= places[None, None, :]
    scores = jnp.where(causal, scores, -1e+30)
    probs = low(jax.nn.softmax(scores, axis=-1))
    context = low(jnp.einsum('hqk,khd->qhd', probs, values, precision=highest).reshape(length, width))
    attended = jnp.dot(context, w_attn_out, precision=highest) + frozen_bias[3 * width:4 * width]
    mlp_in = low(layer_norm(embedded, norm_params[2], norm_params[3]))
    inner = jnp.dot(mlp_in, w_mlp_in, precision=highest) + frozen_bias[4 * width:4 * width + hidden_units]
    inner = low(jax.nn.gelu(inner, approximate=False))
    mlp_out = jnp.dot(inner, w_mlp_out, precision=highest) + frozen_bias[4 * width + hidden_units:]
    return embedded + attended + mlp_out

def sae_loss(params, inputs, weights_mask, count):
    enc_weight, dec_weight, enc_bias, dec_bias = params
    preact = low_back(jnp.dot(inputs, low(enc_weight), precision=highest) + enc_bias)
    active = jax.nn.softplus(preact)
    norms = jnp.sqrt(lax.optimization_barrier(jnp.sum(dec_weight * dec_weight, axis=1)))
    recon = low_back(jnp.dot(low(active), low(dec_weight), precision=highest) + dec_bias)
    error_rows = recon - inputs
    per_token = lax.optimization_barrier(jnp.sum(error_rows * error_rows, axis=1)) + lasso_coef * jnp.dot(active, norms, precision=highest)
    total = jnp.sum(weights_mask * per_token)
    return (total / count, total)

def adam_update(weight, moment, second, grad, decay):
    moment_new = beta_one * moment + (1.0 - beta_one) * grad
    second_new = beta_two * second + (1.0 - beta_two) * grad * grad
    corrected = moment_new / (1.0 - beta_one ** STEP)
    scaled = jnp.sqrt(second_new / (1.0 - beta_two ** STEP)) + adam_eps
    weight_new = weight - learn_rate * (corrected / scaled + decay * weight)
    return (weight_new, moment_new, second_new)

def reference(token_ids, token_mask, scale_index, embed, norm_params, frozen_bias, w_joined, w_attn_out, w_mlp_in, w_mlp_out, enc_weight, enc_moment, enc_second, dec_weight, dec_moment, dec_second, enc_bias, enc_bias_moment, enc_bias_second, dec_bias, dec_bias_moment, dec_bias_second):
    sequences = TOKENS // TOK_DEV
    table = embed.astype(jnp.float32)
    joined_w = w_joined.astype(jnp.float32)
    attn_w = w_attn_out.astype(jnp.float32)
    inner_w = w_mlp_in.astype(jnp.float32)
    outer_w = w_mlp_out.astype(jnp.float32)

    def one_sequence(sequence_ids):
        return frozen_layer(table[sequence_ids], norm_params, frozen_bias, joined_w, attn_w, inner_w, outer_w)
    hidden = lax.map(one_sequence, token_ids.reshape(sequences, TOK_DEV)).reshape(TOKENS, D)
    scales = 0.5 + 0.25 * scale_index.astype(jnp.float32)
    inputs = low(hidden * scales[:, None])
    mask_float = token_mask.astype(jnp.float32)
    count = jnp.sum(mask_float)
    group = 4 if sequences % 4 == 0 else 1
    blocks = sequences // group
    params = (enc_weight, dec_weight, enc_bias, dec_bias)

    def accumulate(carry, pieces):
        grads, total = carry
        block_inputs, block_mask = pieces
        loss, pull, block_total = jax.vjp(lambda p: sae_loss(p, block_inputs, block_mask, count), params, has_aux=True)
        block_grads, = pull(jnp.ones_like(loss))
        return ((jax.tree.map(jnp.add, grads, block_grads), total + block_total), None)
    zeros = jax.tree.map(jnp.zeros_like, params)
    (grads, loss_sum), _ = lax.scan(accumulate, (zeros, jnp.zeros((), jnp.float32)), (inputs.reshape(blocks, group * TOK_DEV, D), mask_float.reshape(blocks, group * TOK_DEV)))
    squares = jnp.sum(grads[0] * grads[0]) + jnp.sum(grads[1] * grads[1]) + jnp.sum(grads[2] * grads[2]) + jnp.sum(grads[3] * grads[3])
    grad_norm = jnp.sqrt(squares)
    factor = clip_bound / jnp.maximum(grad_norm, clip_bound)
    enc_new = adam_update(enc_weight, enc_moment, enc_second, grads[0] * factor, weight_decay)
    dec_new = adam_update(dec_weight, dec_moment, dec_second, grads[1] * factor, weight_decay)
    enc_bias_new = adam_update(enc_bias, enc_bias_moment, enc_bias_second, grads[2] * factor, 0.0)
    dec_bias_new = adam_update(dec_bias, dec_bias_moment, dec_bias_second, grads[3] * factor, 0.0)
    return (enc_new[0], enc_new[1], enc_new[2], dec_new[0], dec_new[1], dec_new[2], enc_bias_new[0], enc_bias_new[1], enc_bias_new[2], dec_bias_new[0], dec_bias_new[1], dec_bias_new[2], grad_norm, loss_sum, count)
```

```python
import functools
import jax
import jax.numpy as jnp
from jax import lax
from jax.experimental import pallas as pl
from jax.experimental.pallas import tpu as pltpu
from jax.sharding import PartitionSpec as P

HEADS = 8
ROT = 16
STEP = 10
Z_CHIPS = 4
CORES = 2
SLOTS = 6
CHUNK = 1024
MESH = pl.DeviceIdType.MESH
f32 = jnp.float32
bf16 = jnp.bfloat16


lasso_coef = 5.0
clip_bound = 1.0
learn_rate = 0.03
beta_one = 0.9
beta_two = 0.999
adam_eps = 1e-08
weight_decay = 0.01


def layer_norm(values, gain, shift):
    centred = values - jnp.mean(values, axis=-1, keepdims=True)
    spread = jnp.mean(centred * centred, axis=-1, keepdims=True)
    return centred * lax.rsqrt(spread + 1e-05) * gain + shift


def rotary(values, rotated):
    length = values.shape[0]
    half = rotated // 2
    freqs = 10000.0 ** (-2.0 * jnp.arange(half, dtype=jnp.float32) / rotated)
    angles = jnp.arange(length, dtype=jnp.float32)[:, None] * freqs[None, :]
    cosines = jnp.concatenate([jnp.cos(angles), jnp.cos(angles)], -1)[:, None, :]
    sines = jnp.concatenate([jnp.sin(angles), jnp.sin(angles)], -1)[:, None, :]
    head = values[..., :rotated]
    turned = jnp.concatenate([-head[..., half:], head[..., :half]], -1)
    return jnp.concatenate([head * cosines + turned * sines, values[..., rotated:]], -1)


def frozen_layer(embedded, norm_params, frozen_bias, w_joined, w_attn_out, w_mlp_in, w_mlp_out):
    length, width = embedded.shape
    head_dim = width // HEADS
    hidden_units = w_mlp_in.shape[1]
    attn_in = layer_norm(embedded, norm_params[0], norm_params[1]).astype(jnp.bfloat16)
    joined = (
        jnp.dot(attn_in, w_joined, preferred_element_type=jnp.float32) + frozen_bias[: 3 * width]
    )
    queries = rotary(joined[:, :width].reshape(length, HEADS, head_dim), ROT).astype(jnp.bfloat16)
    keys = rotary(joined[:, width : 2 * width].reshape(length, HEADS, head_dim), ROT).astype(
        jnp.bfloat16
    )
    values = joined[:, 2 * width :].reshape(length, HEADS, head_dim).astype(jnp.bfloat16)
    block_rows = min(512, length)
    key_places = jnp.arange(length)

    def attend(block_start):
        block_queries = lax.dynamic_slice_in_dim(queries, block_start, block_rows, 0)
        scores = jnp.einsum(
            "qhd,khd->hqk", block_queries, keys, preferred_element_type=jnp.float32
        ) * head_dim ** (-0.5)
        query_places = block_start + jnp.arange(block_rows)
        causal = query_places[None, :, None] >= key_places[None, None, :]
        probs = jax.nn.softmax(jnp.where(causal, scores, -1e30), axis=-1).astype(jnp.bfloat16)
        return jnp.einsum("hqk,khd->qhd", probs, values, preferred_element_type=jnp.float32)

    starts = jnp.arange(0, length, block_rows)
    context = lax.map(attend, starts).reshape(length, width).astype(jnp.bfloat16)
    attended = (
        jnp.dot(context, w_attn_out, preferred_element_type=jnp.float32)
        + frozen_bias[3 * width : 4 * width]
    )
    mlp_in = layer_norm(embedded, norm_params[2], norm_params[3]).astype(jnp.bfloat16)
    inner = (
        jnp.dot(mlp_in, w_mlp_in, preferred_element_type=jnp.float32)
        + frozen_bias[4 * width : 4 * width + hidden_units]
    )
    inner = jax.nn.gelu(inner, approximate=False).astype(jnp.bfloat16)
    mlp_out = (
        jnp.dot(inner, w_mlp_out, preferred_element_type=jnp.float32)
        + frozen_bias[4 * width + hidden_units :]
    )
    return embedded + attended + mlp_out


def adam_update(weight, moment, second, grad, decay):
    moment_new = beta_one * moment + (1.0 - beta_one) * grad
    second_new = beta_two * second + (1.0 - beta_two) * grad * grad
    corrected = moment_new / (1.0 - beta_one**STEP)
    scaled = jnp.sqrt(second_new / (1.0 - beta_two**STEP)) + adam_eps
    weight_new = weight - learn_rate * (corrected / scaled + decay * weight)
    return (weight_new, moment_new, second_new)


def softplus_parts(value):
    power = jnp.exp(value)
    grown = jnp.log(1.0 + power)
    grown = jnp.where(power < 2.0**-8, power * (1.0 - 0.5 * power), grown)
    active = jnp.where(value > 30.0, value, grown)
    return active, jnp.exp(value - active)


def forward_kernel(
    lat_size,
    inputs_ref, enc_ref, dec_ref, enc_bias_ref, mask_ref, dec_bias_ref, scale_ref,
    active_hbm, slope_hbm, mass_out, back_out, stats_out,
    active_buf, slope_buf, product, partial, own, send_two, recv_one, recv_two,
    active_sem, slope_sem, out_one, in_one, out_two, in_two, out_three, in_three, out_four, in_four,
):
    tokens, depth = inputs_ref.shape
    latents = enc_ref.shape[1]
    chunk, span = product.shape[1:]
    width = active_hbm.shape[2]
    chunks, spans = tokens // chunk, latents // span
    y_size = lat_size // CORES
    share = chunk // lat_size
    strip = 16
    row = lax.axis_index("rows")
    lat = lax.axis_index("lat")
    my_y, core = lat // CORES, lax.rem(lat, CORES)
    other = 1 - core

    def y_peer(step):
        return lax.rem(my_y + step, y_size)

    def share_rows(y, which_core):
        return pl.multiple_of((y * CORES + which_core) * share, share)

    def token_rows(block, y, which_core):
        return pl.ds(pl.multiple_of(block * chunk + (y * CORES + which_core) * share, share), share)

    def remote(src, dst, send, recv, target):
        return pltpu.make_async_remote_copy(
            src_ref=src, dst_ref=dst, send_sem=send, recv_sem=recv,
            device_id=(row, target), device_id_type=MESH)

    def copy_one(block, y):
        slot = lax.rem(block, 2)
        return remote(
            partial.at[slot, pl.ds(share_rows(y, other), share)], recv_one.at[block, y],
            out_one.at[slot, y], in_one.at[block, y], my_y * CORES + other)

    def copy_two(block, step):
        slot = lax.rem(block, 2)
        return remote(
            send_two.at[slot, step - 1], recv_two.at[block, step - 1],
            out_two.at[slot, step - 1], in_two.at[block, step - 1], y_peer(step) * CORES + core)

    def copy_three(block, step):
        mine = back_out.at[token_rows(block, my_y, core)]
        return remote(
            mine, mine, out_three.at[block, step - 1], in_three.at[block, step - 1], y_peer(step) * CORES + core)

    def copy_four(block, y):
        mine = back_out.at[token_rows(block, y, core)]
        return remote(mine, mine, out_four.at[block, y], in_four.at[block, y], my_y * CORES + other)

    def stores(block, at, slot):
        rows = pl.ds(pl.multiple_of(block * chunk, chunk), chunk)
        copies = []
        for part in range(span // width):
            lanes = pl.ds(part * width, width)
            copies.append(pltpu.make_async_copy(
                active_buf.at[slot, :, lanes], active_hbm.at[at * (span // width) + part, rows], active_sem.at[slot, part]))
            copies.append(pltpu.make_async_copy(
                slope_buf.at[slot, :, lanes], slope_hbm.at[at * (span // width) + part, rows], slope_sem.at[slot, part]))
        return copies

    barrier = pltpu.get_barrier_semaphore()
    pl.semaphore_signal(barrier, inc=1, device_id=(row, my_y * CORES + other), device_id_type=MESH)
    for step in range(1, y_size):
        pl.semaphore_signal(barrier, inc=1, device_id=(row, y_peer(step) * CORES + core), device_id_type=MESH)
    mass_out[...] = jnp.zeros_like(mass_out)
    stats_out[...] = jnp.zeros_like(stats_out)
    pl.semaphore_wait(barrier, y_size)

    def compute(block):
        place = lax.rem(block, 2)
        first = pl.multiple_of(block * chunk, chunk)

        @pl.when(block >= 2)
        def _():
            for y in range(y_size):
                copy_one(block - 2, y).wait_send()

        for at in range(spans):
            slot = at % 2
            if at >= 2:
                for copy in stores(block, at - 2, slot):
                    copy.wait()
            else:
                @pl.when(block > 0)
                def _():
                    for copy in stores(block - 1, spans - 2 + at, slot):
                        copy.wait()

            product[slot] = jnp.dot(
                inputs_ref[pl.ds(first, chunk), :], enc_ref[:, at * span : (at + 1) * span], preferred_element_type=f32)
            for left in range(0, span, width):
                lanes = pl.ds(left, width)
                cols = pl.ds(at * span + left, width)
                shift = enc_bias_ref[:, cols]
                total = mass_out[:, cols]
                for top in range(0, chunk, strip):
                    rows = pl.ds(top, strip)
                    mask = mask_ref[pl.ds(first + top, strip), :]
                    mask = jnp.concatenate([mask] * (width // 128), axis=1)
                    active, slope = softplus_parts(product[slot, rows, lanes] + shift)
                    active_buf[slot, rows, lanes] = active.astype(bf16)
                    slope_buf[slot, rows, lanes] = slope * mask
                    total = total + (active * mask).reshape(strip // 8, 8, width).sum(0)
                mass_out[:, cols] = total
            for copy in stores(block, at, slot):
                copy.start()
            part = lax.dot_general(
                active_buf[slot], dec_ref[:, at * span : (at + 1) * span], (((1,), (1,)), ((), ())),
                preferred_element_type=f32)
            partial[place] = part if at == 0 else partial[place] + part

    def exchange(block):
        slot = lax.rem(block, 2)
        for y in range(y_size):
            copy_one(block, y).start()
        for y in range(y_size):
            copy_one(block, y).wait_recv()
        for step in list(range(1, y_size)) + [0]:
            y = y_peer(step)
            total = partial[slot, pl.ds(share_rows(y, core), share), :] + recv_one[block, y]
            if step == 0:
                own[slot] = total
            else:
                @pl.when(block >= 2)
                def _():
                    copy_two(block - 2, step).wait_send()

                send_two[slot, step - 1] = total
                copy_two(block, step).start()

    def settle(block):
        slot = lax.rem(block, 2)
        rows = token_rows(block, my_y, core)
        total = own[slot]
        for step in range(1, y_size):
            copy_two(block, step).wait_recv()
            total = total + recv_two[block, step - 1]
        error = total + dec_bias_ref[...] - inputs_ref[rows, :].astype(f32)
        mask = jnp.concatenate([mask_ref[rows, :]] * (depth // 128), axis=1)
        low = (scale_ref[...] * mask * error).astype(bf16)
        back_out[rows, :] = low
        stats_out[0:8, :] += (mask * error * error).reshape(share // 8, 8, depth).sum(0)
        stats_out[8:16, :] += low.astype(f32).reshape(share // 8, 8, depth).sum(0)
        for step in range(1, y_size):
            copy_three(block, step).start()

    def spread(block):
        for step in range(1, y_size):
            copy_three(block, step).wait_recv()
        for y in range(y_size):
            copy_four(block, y).start()

    def turn(block, carry):
        @pl.when(block < chunks)
        def _():
            compute(block)
            exchange(block)

        @pl.when((block >= 1) & (block <= chunks))
        def _():
            settle(block - 1)

        @pl.when(block >= 2)
        def _():
            spread(block - 2)

        return carry

    lax.fori_loop(0, chunks + 2, turn, 0)
    for slot in range(2):
        for copy in stores(chunks - 1, spans - 2 + slot, slot):
            copy.wait()
    for block in range(chunks - 2, chunks):
        for y in range(y_size):
            copy_one(block, y).wait_send()
        for step in range(1, y_size):
            copy_two(block, step).wait_send()

    def drain(block, carry):
        for step in range(1, y_size):
            copy_three(block, step).wait_send()
        for y in range(y_size):
            copy_four(block, y).wait_send()
            copy_four(block, y).wait_recv()
        return carry

    lax.fori_loop(0, chunks, drain, 0)


def forward(lat_size, inputs, enc_low, dec_cols, enc_bias_row, mask_lanes, dec_bias_row, scale_row):
    tokens, depth = inputs.shape
    latents = enc_low.shape[1]
    chunk, span, width = 512, 1024, (512 if tokens <= 4096 else 256)
    chunks = tokens // chunk
    y_size = lat_size // CORES
    share = chunk // lat_size
    dma = pltpu.SemaphoreType.DMA
    vmem = pl.BlockSpec(memory_space=pltpu.VMEM)
    hbm = pl.BlockSpec(memory_space=pl.ANY)
    return pl.pallas_call(
        functools.partial(forward_kernel, lat_size),
        out_shape=[
            jax.ShapeDtypeStruct((latents // width, tokens, width), bf16),
            jax.ShapeDtypeStruct((latents // width, tokens, width), f32),
            jax.ShapeDtypeStruct((8, latents), f32),
            jax.ShapeDtypeStruct((tokens, depth), bf16),
            jax.ShapeDtypeStruct((16, depth), f32),
        ],
        in_specs=[vmem] * 7,
        out_specs=[hbm, hbm, vmem, vmem, vmem],
        scratch_shapes=[
            pltpu.VMEM((2, chunk, span), bf16),
            pltpu.VMEM((2, chunk, span), f32),
            pltpu.VMEM((2, chunk, span), f32),
            pltpu.VMEM((2, chunk, depth), f32),
            pltpu.VMEM((2, share, depth), f32),
            pltpu.VMEM((2, y_size - 1, share, depth), f32),
            pltpu.VMEM((chunks, y_size, share, depth), f32),
            pltpu.VMEM((chunks, y_size - 1, share, depth), f32),
            dma((2, span // width)), dma((2, span // width)),
            dma((2, y_size)), dma((chunks, y_size)),
            dma((2, y_size - 1)), dma((chunks, y_size - 1)),
            dma((chunks, y_size - 1)), dma((chunks, y_size - 1)),
            dma((chunks, y_size)), dma((chunks, y_size)),
        ],
        compiler_params=pltpu.CompilerParams(
            collective_id=1, has_side_effects=True, vmem_limit_bytes=60 * 2**20),
        name="forward",
    )(inputs, enc_low, dec_cols, enc_bias_row, mask_lanes, dec_bias_row, scale_row)


def encode(value):
    top = jnp.max(jnp.abs(value), axis=0, keepdims=True)
    unit = jnp.where(top > 0.0, 32766.0 / top, 0.0)
    shifted = value * unit + 12582912.0
    return (shifted - 12582912.0).astype(jnp.int32).astype(jnp.int16), top * (1.0 / 32766.0)


def decode(code, unit):
    return code.astype(jnp.int32).astype(f32) * unit


def put_units(ref, index, unit):
    for piece in range(unit.shape[1] // 128):
        ref[index + (pl.ds(piece, 1), slice(None))] = unit[:, piece * 128 : piece * 128 + 128]


def get_units(ref, index, width):
    return jnp.concatenate(
        [ref[index + (pl.ds(piece, 1), slice(None))] for piece in range(width // 128)], axis=1)


def backward_kernel(
    rows_size,
    inputs_ref, back_ref, dec_ref, lasso_ref, active_hbm, slope_hbm,
    enc_out, dec_out, bias_out,
    grad_low, active_buf, slope_buf, sums,
    send_one, units_one, recv_one, got_one,
    send_two, units_two, recv_two, got_two,
    active_sem, slope_sem,
    out_one, in_one, outu_one, inu_one, out_two, in_two, outu_two, inu_two,
):
    blocks, tokens, width = active_hbm.shape
    chunk = slope_buf.shape[1]
    chunks = tokens // chunk
    shard = enc_out.shape[0]
    x_size = rows_size // Z_CHIPS
    row = lax.axis_index("rows")
    lat = lax.axis_index("lat")
    my_z, my_x = row // x_size, lax.rem(row, x_size)

    def x_peer(step):
        return lax.rem(my_x + step, x_size)

    def z_peer(step):
        return lax.rem(my_z + step, Z_CHIPS)

    def active_copy(block):
        slot = lax.rem(block, 2)
        return pltpu.make_async_copy(active_hbm.at[block], active_buf.at[slot], active_sem.at[slot])

    def slope_copy(index):
        slot = lax.rem(index, slope_buf.shape[0])
        return pltpu.make_async_copy(
            slope_hbm.at[index // chunks, pl.ds(pl.multiple_of(lax.rem(index, chunks) * chunk, chunk), chunk)],
            slope_buf.at[slot],
            slope_sem.at[slot],
        )

    def copies(stage, block, which, step):
        slot = lax.rem(block, 2)
        if stage == 0:
            target = (my_z * x_size + x_peer(step), lat)
            refs = (send_one, recv_one, out_one, in_one, units_one, got_one, outu_one, inu_one)
        else:
            target = (z_peer(step) * x_size + my_x, lat)
            refs = (send_two, recv_two, out_two, in_two, units_two, got_two, outu_two, inu_two)
        return [
            pltpu.make_async_remote_copy(
                src_ref=refs[at].at[slot, which, step - 1], dst_ref=refs[at + 1].at[block, which, step - 1],
                send_sem=refs[at + 2].at[slot, which, step - 1], recv_sem=refs[at + 3].at[block, which, step - 1],
                device_id=target, device_id_type=MESH)
            for at in (0, 4)
        ]

    barrier = pltpu.get_barrier_semaphore()
    for step in range(1, x_size):
        pl.semaphore_signal(barrier, inc=1, device_id=(my_z * x_size + x_peer(step), lat), device_id_type=MESH)
    for step in range(1, Z_CHIPS):
        pl.semaphore_signal(barrier, inc=1, device_id=(z_peer(step) * x_size + my_x, lat), device_id_type=MESH)
    active_copy(0).start()
    ahead = slope_buf.shape[0] - 1
    for index in range(ahead):
        slope_copy(index).start()
    pl.semaphore_wait(barrier, x_size + Z_CHIPS - 2)

    def columns(block):
        return pl.ds(pl.multiple_of(block * width, width), width)

    over_tokens = (((0,), (0,)), ((), ()))

    def compute_dec(block):
        slot = lax.rem(block, 2)

        @pl.when(block + 1 < blocks)
        def _():
            active_copy(block + 1).start()

        active_copy(block).wait()
        sums[slot, 1] = lax.dot_general(back_ref[...], active_buf[slot], over_tokens, preferred_element_type=f32)

    def compute_enc(block):
        slot = lax.rem(block, 2)
        cols = columns(block)

        def piece(index, total):
            at = block * chunks + index

            @pl.when(at + ahead < blocks * chunks)
            def _():
                slope_copy(at + ahead).start()

            slope_copy(at).wait()
            rows = pl.ds(pl.multiple_of(index * chunk, chunk), chunk)
            back = jnp.dot(back_ref[rows, :], dec_ref[:, cols], preferred_element_type=f32)
            low = ((back + lasso_ref[:, cols]) * slope_buf[lax.rem(at, ahead + 1)]).astype(bf16)
            grad_low[rows, :] = low
            return total + low.astype(f32).reshape(chunk // 8, 8, width).sum(0)

        bias_out[:, cols] = lax.fori_loop(0, chunks, piece, jnp.zeros((8, width), f32))
        sums[slot, 0] = lax.dot_general(inputs_ref[...], grad_low[...], over_tokens, preferred_element_type=f32)

    def send_x(block, which):
        slot = lax.rem(block, 2)
        for step in range(1, x_size):
            @pl.when(block >= 2)
            def _():
                for copy in copies(0, block - 2, which, step):
                    copy.wait_send()

            parts = []
            for z in range(Z_CHIPS):
                first = pl.multiple_of((z * x_size + x_peer(step)) * shard, shard)
                parts.append(sums[slot, which, pl.ds(first, shard), :])
            code, unit = encode(jnp.concatenate(parts, axis=0))
            for z in range(Z_CHIPS):
                send_one[slot, which, step - 1, z] = code[z * shard : (z + 1) * shard]
            put_units(units_one, (slot, which, step - 1), unit)
            for copy in copies(0, block, which, step):
                copy.start()

    def send_z(block, which):
        slot = lax.rem(block, 2)
        for step in range(1, x_size):
            for copy in copies(0, block, which, step):
                copy.wait_recv()
        for step in range(Z_CHIPS):
            z = z_peer(step)
            if step:
                @pl.when(block >= 2)
                def _():
                    for copy in copies(1, block - 2, which, step):
                        copy.wait_send()

            first = pl.multiple_of((z * x_size + my_x) * shard, shard)
            total = sums[slot, which, pl.ds(first, shard), :]
            for x_step in range(1, x_size):
                total = total + decode(
                    recv_one[block, which, x_step - 1, z], get_units(got_one, (block, which, x_step - 1), width))
            if step == 0:
                (enc_out, dec_out)[which][:, columns(block)] = total
            else:
                code, unit = encode(total)
                send_two[slot, which, step - 1] = code
                put_units(units_two, (slot, which, step - 1), unit)
                for copy in copies(1, block, which, step):
                    copy.start()

    def finish(block, which):
        slot = lax.rem(block, 2)
        for step in range(1, Z_CHIPS):
            for copy in copies(1, block, which, step):
                copy.wait_recv()
        out, cols = (enc_out, dec_out)[which], columns(block)
        total = out[:, cols]
        for step in range(1, Z_CHIPS):
            total = total + decode(
                recv_two[block, which, step - 1], get_units(got_two, (block, which, step - 1), width))
        out[:, cols] = total

    def turn(block, carry):
        for which, compute in ((1, compute_dec), (0, compute_enc)):
            @pl.when(block < blocks)
            def _():
                compute(block)
                send_x(block, which)

            @pl.when((block >= 1) & (block <= blocks))
            def _():
                send_z(block - 1, which)

            @pl.when(block >= 2)
            def _():
                finish(block - 2, which)

        return carry

    lax.fori_loop(0, blocks + 2, turn, 0)
    for block in range(max(blocks - 2, 0), blocks):
        for which in range(2):
            for stage, size in ((0, x_size), (1, Z_CHIPS)):
                for step in range(1, size):
                    for copy in copies(stage, block, which, step):
                        copy.wait_send()


def backward(rows_size, inputs, back, dec_cols, lasso_row, active, slope):
    blocks, tokens, width = active.shape
    depth = inputs.shape[1]
    shard = depth // rows_size
    latents = dec_cols.shape[1]
    x_size = rows_size // Z_CHIPS
    chunk = min(CHUNK, tokens)
    i16 = jnp.int16
    dma = pltpu.SemaphoreType.DMA
    vmem = pl.BlockSpec(memory_space=pltpu.VMEM)
    hbm = pl.BlockSpec(memory_space=pl.ANY)
    return pl.pallas_call(
        functools.partial(backward_kernel, rows_size),
        out_shape=[
            jax.ShapeDtypeStruct((shard, latents), f32),
            jax.ShapeDtypeStruct((shard, latents), f32),
            jax.ShapeDtypeStruct((8, latents), f32),
        ],
        in_specs=[vmem] * 4 + [hbm] * 2,
        out_specs=[vmem] * 3,
        scratch_shapes=[
            pltpu.VMEM((tokens, width), bf16),
            pltpu.VMEM((2, tokens, width), bf16),
            pltpu.VMEM((SLOTS, chunk, width), f32),
            pltpu.VMEM((2, 2, depth, width), f32),
            pltpu.VMEM((2, 2, x_size - 1, Z_CHIPS, shard, width), i16),
            pltpu.VMEM((2, 2, x_size - 1, 8, 128), f32),
            pltpu.VMEM((blocks, 2, x_size - 1, Z_CHIPS, shard, width), i16),
            pltpu.VMEM((blocks, 2, x_size - 1, 8, 128), f32),
            pltpu.VMEM((2, 2, Z_CHIPS - 1, shard, width), i16),
            pltpu.VMEM((2, 2, Z_CHIPS - 1, 8, 128), f32),
            pltpu.VMEM((blocks, 2, Z_CHIPS - 1, shard, width), i16),
            pltpu.VMEM((blocks, 2, Z_CHIPS - 1, 8, 128), f32),
            dma((2,)), dma((SLOTS,)),
            dma((2, 2, x_size - 1)), dma((blocks, 2, x_size - 1)),
            dma((2, 2, x_size - 1)), dma((blocks, 2, x_size - 1)),
            dma((2, 2, Z_CHIPS - 1)), dma((blocks, 2, Z_CHIPS - 1)),
            dma((2, 2, Z_CHIPS - 1)), dma((blocks, 2, Z_CHIPS - 1)),
        ],
        compiler_params=pltpu.CompilerParams(
            collective_id=2, has_side_effects=True, vmem_limit_bytes=60 * 2**20),
        name="backward",
    )(inputs, back, dec_cols, lasso_row, active, slope)


def body(
    token_ids,
    token_mask,
    scale_index,
    embed,
    norm_params,
    frozen_bias,
    w_joined,
    w_attn_out,
    w_mlp_in,
    w_mlp_out,
    enc_weight,
    enc_moment,
    enc_second,
    dec_weight,
    dec_moment,
    dec_second,
    enc_bias,
    enc_bias_moment,
    enc_bias_second,
    dec_bias,
    dec_bias_moment,
    dec_bias_second,
):
    lat_size = lax.axis_size("lat")
    lat_index = lax.axis_index("lat")
    group_tokens = token_ids.shape[0]
    tok_local = group_tokens // lat_size
    rows_size = lax.axis_size("rows")
    depth = enc_weight.shape[0] * rows_size
    mask_float = token_mask.astype(f32)
    dec_master = dec_weight.T
    enc_low = lax.all_gather(enc_weight.astype(bf16), "rows", axis=0, tiled=True)
    dec_cols = lax.all_gather(dec_master.astype(bf16), "rows", axis=0, tiled=True)
    count = lax.psum(jnp.sum(mask_float), "rows")
    norms = jnp.sqrt(lax.psum(jnp.sum(dec_master * dec_master, axis=0), "rows"))
    vocab_local = embed.shape[0]
    vocab_first = lat_index * vocab_local
    local_ids = token_ids - vocab_first
    inside = ((local_ids >= 0) & (local_ids < vocab_local)).astype(f32)
    picked = jnp.take(embed, jnp.clip(local_ids, 0, vocab_local - 1), axis=0).astype(f32)
    embedded = lax.psum_scatter(
        (picked * inside[:, None]).astype(bf16), "lat", scatter_dimension=0, tiled=True
    ).astype(f32)
    own_first = lat_index * tok_local
    residual = frozen_layer(
        embedded, norm_params, frozen_bias, w_joined, w_attn_out, w_mlp_in, w_mlp_out
    )
    scales = 0.5 + 0.25 * lax.dynamic_slice_in_dim(scale_index, own_first, tok_local).astype(f32)
    own_inputs = (residual * scales[:, None]).astype(bf16)
    all_inputs = lax.all_gather(own_inputs, "lat", axis=0, tiled=True)
    mask_lanes = jnp.broadcast_to(mask_float[:, None], (group_tokens, 128))
    scale_row = jnp.full((1, depth), 2.0 / count, f32)
    lasso_scale = lasso_coef / count
    active, slope, mass_rows, recon_grad, stats = forward(
        lat_size, all_inputs, enc_low, dec_cols, enc_bias[None, :], mask_lanes, dec_bias[None, :], scale_row)
    grad_enc, grad_dec, bias_rows = backward(
        rows_size, all_inputs, recon_grad, dec_cols, (lasso_scale * norms)[None, :], active, slope)
    bias_mass = jnp.stack([bias_rows.sum(0), mass_rows.sum(0)])
    grad_enc_bias, active_mass = lax.psum(bias_mass, "rows")
    leader = (lax.axis_index("rows") == 0).astype(f32)
    lasso_part = lasso_coef * jnp.sum(active_mass * norms) * leader
    loss_sum, grad_dec_bias = lax.psum((jnp.sum(stats[:8]) + lasso_part, stats[8:].sum(0)), ("rows", "lat"))
    grad_dec = grad_dec + (lasso_scale * active_mass / norms)[None, :] * dec_master
    local_squares = (
        jnp.sum(grad_enc * grad_enc) + jnp.sum(grad_dec * grad_dec)
        + jnp.sum(grad_enc_bias * grad_enc_bias) * leader
    )
    squares = lax.psum(local_squares, ("rows", "lat")) + jnp.sum(grad_dec_bias * grad_dec_bias)
    grad_norm = jnp.sqrt(squares)
    factor = clip_bound / jnp.maximum(grad_norm, clip_bound)
    enc_new = adam_update(enc_weight, enc_moment, enc_second, grad_enc * factor, weight_decay)
    dec_new = adam_update(dec_weight, dec_moment, dec_second, grad_dec.T * factor, weight_decay)
    enc_bias_new = adam_update(
        enc_bias, enc_bias_moment, enc_bias_second, grad_enc_bias * factor, 0.0
    )
    dec_bias_new = adam_update(
        dec_bias, dec_bias_moment, dec_bias_second, grad_dec_bias * factor, 0.0
    )
    return (
        enc_new[0],
        enc_new[1],
        enc_new[2],
        dec_new[0],
        dec_new[1],
        dec_new[2],
        enc_bias_new[0],
        enc_bias_new[1],
        enc_bias_new[2],
        dec_bias_new[0],
        dec_bias_new[1],
        dec_bias_new[2],
        grad_norm,
        loss_sum,
        count,
    )


def solution(mesh):
    placed = (
        P("rows"),
        P("rows"),
        P("rows"),
        P("lat", None),
        P(),
        P(),
        P(),
        P(),
        P(),
        P(),
        P("rows", "lat"),
        P("rows", "lat"),
        P("rows", "lat"),
        P("lat", "rows"),
        P("lat", "rows"),
        P("lat", "rows"),
        P("lat"),
        P("lat"),
        P("lat"),
        P(),
        P(),
        P(),
    )
    return jax.shard_map(
        body,
        mesh=mesh,
        in_specs=placed,
        out_specs=(
            P("rows", "lat"),
            P("rows", "lat"),
            P("rows", "lat"),
            P("lat", "rows"),
            P("lat", "rows"),
            P("lat", "rows"),
            P("lat"),
            P("lat"),
            P("lat"),
            P(),
            P(),
            P(),
            P(),
            P(),
            P(),
        ),
        check_vma=False,
    )
```

```python
import functools
import jax
import jax.numpy as jnp
from jax import lax
from jax.experimental import pallas as pl
from jax.experimental.pallas import tpu as pltpu
from jax.sharding import PartitionSpec as P

HEADS = 8
ROT = 16
STEP = 10
Z_CHIPS = 4
CORES = 2
SLOTS = 6
CHUNK = 1024
MESH = pl.DeviceIdType.MESH
f32 = jnp.float32
bf16 = jnp.bfloat16


lasso_coef = 5.0
clip_bound = 1.0
learn_rate = 0.03
beta_one = 0.9
beta_two = 0.999
adam_eps = 1e-08
weight_decay = 0.01


def adam_update(weight, moment, second, grad, decay):
    moment_new = beta_one * moment + (1.0 - beta_one) * grad
    second_new = beta_two * second + (1.0 - beta_two) * grad * grad
    corrected = moment_new / (1.0 - beta_one**STEP)
    scaled = jnp.sqrt(second_new / (1.0 - beta_two**STEP)) + adam_eps
    weight_new = weight - learn_rate * (corrected / scaled + decay * weight)
    return (weight_new, moment_new, second_new)


ROWS = 512
PIECE = 256
HEAD = 64
PAIR = 128


def front_kernel(
    rows_size, lat_size,
    picked_ref, norm_ref, bias_ref, joined_ref, attn_ref, mlp_in_ref, mlp_out_ref,
    turn_ref, level_ref, mask_ref, enc_ref, dec_ref,
    inputs_out, enc_out, dec_out, norms_out, count_out,
    from_core, from_y, base, queries, keys, values, context, facts, got_facts,
    out_right, in_left, out_left, in_right, out_x, in_x, out_fact, in_fact,
    out_core, in_core, out_y, in_y, out_own, in_own, out_near, in_near,
):
    tokens, depth = base.shape
    shard = enc_ref.shape[0]
    latents = enc_ref.shape[1]
    hidden = mlp_in_ref.shape[1]
    x_size = rows_size // Z_CHIPS
    y_size = lat_size // CORES
    pieces = tokens // PIECE
    row = lax.axis_index("rows")
    lat = lax.axis_index("lat")
    my_z, my_x = row // x_size, lax.rem(row, x_size)
    my_y, core = lat // CORES, lax.rem(lat, CORES)
    other = 1 - core

    def remote(src, dst, send, recv, to_row, to_lat):
        return pltpu.make_async_remote_copy(
            src_ref=src, dst_ref=dst, send_sem=send, recv_sem=recv,
            device_id=(to_row, to_lat), device_id_type=MESH)

    def peer_row(step):
        return lax.rem(row + step, rows_size)

    def x_row(step):
        return my_z * x_size + lax.rem(my_x + step, x_size)

    def y_peer(step):
        return lax.rem(my_y + step, y_size)

    barrier = pltpu.get_barrier_semaphore()
    for step in range(1, rows_size):
        pl.semaphore_signal(barrier, inc=1, device_id=(peer_row(step), lat), device_id_type=MESH)
    for step in range(1, y_size):
        pl.semaphore_signal(barrier, inc=1, device_id=(row, y_peer(step) * CORES + core), device_id_type=MESH)
    pl.semaphore_signal(barrier, inc=1, device_id=(row, my_y * CORES + other), device_id_type=MESH)

    mine = pl.ds(pl.multiple_of(row * shard, shard), shard)
    enc_out[mine, :] = enc_ref[...].astype(bf16)
    dec_out[mine, :] = dec_ref[...].astype(bf16)
    square = jnp.sum(dec_ref[...] * dec_ref[...], axis=0, keepdims=True)
    part = latents // 8
    for at in range(8):
        facts[pl.ds(at, 1), :] = square[:, at * part : (at + 1) * part]
    facts[8:16, :] = jnp.broadcast_to(jnp.sum(mask_ref[...], keepdims=True), (8, part))
    pl.semaphore_wait(barrier, rows_size + y_size - 1)

    weights = (enc_out, dec_out)

    def weight_rows(z):
        return pl.ds(pl.multiple_of((z * x_size + my_x) * shard, shard), shard)

    def right_copy(hop, which, received=False):
        area = weights[which].at[weight_rows(jnp.maximum(my_z - hop - (1 if received else 0), 0))]
        return remote(area, area, out_right.at[hop, which], in_left.at[hop, which],
                      jnp.minimum(my_z + 1, Z_CHIPS - 1) * x_size + my_x, lat)

    def left_copy(hop, which, received=False):
        area = weights[which].at[weight_rows(jnp.minimum(my_z + hop + (1 if received else 0), Z_CHIPS - 1))]
        return remote(area, area, out_left.at[hop, which], in_right.at[hop, which],
                      jnp.maximum(my_z - 1, 0) * x_size + my_x, lat)

    def x_copy(z, which, step):
        area = weights[which].at[weight_rows(z)]
        return remote(area, area, out_x.at[z, which, step - 1], in_x.at[z, which, step - 1], x_row(step), lat)

    def pass_on(hop, which):
        if hop == 0:
            @pl.when(my_z < Z_CHIPS - 1)
            def _():
                right_copy(0, which).start()

            @pl.when(my_z > 0)
            def _():
                left_copy(0, which).start()

            for step in range(1, x_size):
                x_copy(my_z, which, step).start()
            return

        @pl.when(my_z >= hop)
        def _():
            right_copy(hop - 1, which, True).wait_recv()
            if hop < Z_CHIPS - 1:
                @pl.when(my_z < Z_CHIPS - 1)
                def _():
                    right_copy(hop, which).start()
            for step in range(1, x_size):
                x_copy(my_z - hop, which, step).start()

        @pl.when(my_z + hop <= Z_CHIPS - 1)
        def _():
            left_copy(hop - 1, which, True).wait_recv()
            if hop < Z_CHIPS - 1:
                @pl.when(my_z > 0)
                def _():
                    left_copy(hop, which).start()
            for step in range(1, x_size):
                x_copy(my_z + hop, which, step).start()

    def fact_copy(step):
        return remote(facts, got_facts.at[step - 1], out_fact.at[step - 1], in_fact.at[step - 1], peer_row(step), lat)

    def block_rows(y, which_core, piece):
        return pl.ds(pl.multiple_of((y * CORES + which_core) * tokens + piece * PIECE, PIECE), PIECE)

    def core_copy(step, piece):
        return remote(
            picked_ref.at[block_rows(y_peer(step), other, piece)], from_core.at[step, pl.ds(piece * PIECE, PIECE)],
            out_core.at[step, piece], in_core.at[step, piece], row, my_y * CORES + other)

    def y_copy(step, piece):
        here = pl.ds(piece * PIECE, PIECE)
        return remote(
            from_core.at[step, here], from_y.at[step - 1, here],
            out_y.at[step - 1, piece], in_y.at[step - 1, piece], row, y_peer(step) * CORES + core)

    for piece in range(pieces):
        for step in list(range(1, y_size)) + [0]:
            core_copy(step, piece).start()
    for which in range(2):
        pass_on(0, which)
    for step in range(1, rows_size):
        fact_copy(step).start()
    for piece in range(pieces):
        here = pl.ds(piece * PIECE, PIECE)
        for step in list(range(1, y_size)) + [0]:
            core_copy(step, piece).wait_recv()
            total = picked_ref[block_rows(y_peer(step), core, piece), :].astype(f32) + from_core[step, here, :].astype(f32)
            if step == 0:
                base[here, :] = total
            else:
                from_core[step, here, :] = total.astype(bf16)
                y_copy(step, piece).start()
    pass_on(1, 0)

    def normed(value, gain, shift):
        centred = value - jnp.mean(value, axis=1, keepdims=True)
        spread = jnp.mean(centred * centred, axis=1, keepdims=True)
        return (centred * lax.rsqrt(spread + 1e-05) * gain + shift).astype(bf16)

    def dot(left, right):
        return jnp.dot(left, right, preferred_element_type=f32)

    def rotated(value, rows):
        cosine, low, high = turn_ref[0, rows, :], turn_ref[1, rows, :], turn_ref[2, rows, :]
        parts = []
        for at in range(depth // PAIR):
            tile = value[:, at * PAIR : (at + 1) * PAIR]
            parts.append(
                tile * cosine + pltpu.roll(tile, PAIR - ROT // 2, 1) * low + pltpu.roll(tile, ROT // 2, 1) * high)
        return jnp.concatenate(parts, axis=1)

    for block in range(tokens // ROWS):
        rows = pl.ds(block * ROWS, ROWS)
        for piece in range(block * ROWS // PIECE, (block + 1) * ROWS // PIECE):
            for step in range(1, y_size):
                y_copy(step, piece).wait_recv()
        embedded = base[rows, :]
        for step in range(1, y_size):
            embedded = embedded + from_y[step - 1, rows, :].astype(f32)
        attn_in = normed(embedded, norm_ref[0:1, :], norm_ref[1:2, :])
        joined = dot(attn_in, joined_ref[...]) + bias_ref[:, : 3 * depth]
        queries[rows, :] = (rotated(joined[:, :depth], rows).astype(bf16) * HEAD**-0.5).astype(bf16)
        keys[rows, :] = rotated(joined[:, depth : 2 * depth], rows).astype(bf16)
        values[rows, :] = joined[:, 2 * depth :].astype(bf16)
        mlp_in = normed(embedded, norm_ref[2:3, :], norm_ref[3:4, :])
        inner = dot(mlp_in, mlp_in_ref[...]) + bias_ref[:, 4 * depth : 4 * depth + hidden]
        inner = (0.5 * inner * (1.0 + lax.erf(inner * 0.5**0.5))).astype(bf16)
        base[rows, :] = embedded + (dot(inner, mlp_out_ref[...]) + bias_ref[:, 4 * depth + hidden :])
        if block == 0:
            pass_on(1, 1)
    pass_on(2, 0)

    def own_rows(y, which_core, piece):
        return pl.ds(pl.multiple_of((y * CORES + which_core) * tokens + piece * PIECE, PIECE), PIECE)

    def own_copy(step, piece):
        area = inputs_out.at[own_rows(my_y, core, piece)]
        return remote(area, area, out_own.at[step - 1, piece], in_own.at[step - 1, piece], row, y_peer(step) * CORES + core)

    def near_copy(step, piece):
        area = inputs_out.at[own_rows(y_peer(step), core, piece)]
        return remote(area, area, out_near.at[step, piece], in_near.at[step, piece], row, my_y * CORES + other)

    lanes = lax.broadcasted_iota(jnp.int32, (PIECE, PAIR), 1)
    for piece in range(pieces):
        here = pl.ds(piece * PIECE, PIECE)
        reach = (piece + 1) * PIECE
        visible = (
            lax.broadcasted_iota(jnp.int32, (PIECE, reach), 0) + piece * PIECE
            >= lax.broadcasted_iota(jnp.int32, (PIECE, reach), 1)
        )

        def attend(pair, carry):
            cols = pl.ds(pl.multiple_of(pair * PAIR, PAIR), PAIR)
            both = queries[here, cols]
            found = []
            for first in (True, False):
                chosen = jnp.where((lanes < HEAD) == first, both, jnp.zeros_like(both))
                scores = lax.dot_general(
                    chosen, keys[0:reach, cols], (((1,), (1,)), ((), ())), preferred_element_type=f32)
                scores = jnp.where(visible, scores, -1e30)
                powers = jnp.exp(scores - jnp.max(scores, axis=1, keepdims=True))
                probs = (powers * (1.0 / jnp.sum(powers, axis=1, keepdims=True))).astype(bf16)
                found.append(dot(probs, values[0:reach, cols]))
            context[here, cols] = jnp.where(lanes < HEAD, found[0], found[1]).astype(bf16)
            return carry

        lax.fori_loop(0, depth // PAIR, attend, 0)
        attended = dot(context[here, :], attn_ref[...]) + bias_ref[:, 3 * depth : 4 * depth]
        level = jnp.concatenate([level_ref[here, :]] * (depth // 128), axis=1)
        inputs_out[own_rows(my_y, core, piece), :] = ((base[here, :] + attended) * level).astype(bf16)
        for step in range(1, y_size):
            own_copy(step, piece).start()
        near_copy(0, piece).start()
        if piece == 1:
            pass_on(2, 1)
        if piece >= 2:
            for step in range(1, y_size):
                own_copy(step, piece - 2).wait_recv()
                near_copy(step, piece - 2).start()

    total = facts[...]
    for step in range(1, rows_size):
        fact_copy(step).wait_recv()
        total = total + got_facts[step - 1]
    count_out[...] = total[8:16, 0:128]
    norms = jnp.sqrt(total[0:8, :])
    for at in range(8):
        norms_out[:, at * part : (at + 1) * part] = norms[at : at + 1, :]
    pass_on(3, 0)
    for piece in range(pieces - 2, pieces):
        for step in range(1, y_size):
            own_copy(step, piece).wait_recv()
            near_copy(step, piece).start()
    pass_on(3, 1)

    for which in range(2):
        for hop in range(Z_CHIPS - 1):
            @pl.when((my_z < Z_CHIPS - 1) & (my_z >= hop))
            def _():
                right_copy(hop, which).wait_send()

            @pl.when((my_z > 0) & (my_z + hop <= Z_CHIPS - 1))
            def _():
                left_copy(hop, which).wait_send()

        for z in range(Z_CHIPS):
            for step in range(1, x_size):
                x_copy(z, which, step).wait_send()
                x_copy(z, which, step).wait_recv()
    for step in range(1, rows_size):
        fact_copy(step).wait_send()
    for piece in range(pieces):
        for step in range(y_size):
            core_copy(step, piece).wait_send()
            near_copy(step, piece).wait_send()
            near_copy(step, piece).wait_recv()
        for step in range(1, y_size):
            y_copy(step, piece).wait_send()
            own_copy(step, piece).wait_send()


def front(rows_size, lat_size, picked, norm_params, bias_row, w_joined, w_attn_out, w_mlp_in, w_mlp_out,
          turns, level_lanes, mask_tiles, enc_shard, dec_shard):
    group, depth = picked.shape
    tokens = group // lat_size
    shard, latents = enc_shard.shape
    x_size = rows_size // Z_CHIPS
    y_size = lat_size // CORES
    pieces = tokens // PIECE
    dma = pltpu.SemaphoreType.DMA
    vmem = pl.BlockSpec(memory_space=pltpu.VMEM)
    hops = Z_CHIPS - 1
    return pl.pallas_call(
        functools.partial(front_kernel, rows_size, lat_size),
        out_shape=[
            jax.ShapeDtypeStruct((group, depth), bf16),
            jax.ShapeDtypeStruct((depth, latents), bf16),
            jax.ShapeDtypeStruct((depth, latents), bf16),
            jax.ShapeDtypeStruct((1, latents), f32),
            jax.ShapeDtypeStruct((8, 128), f32),
        ],
        in_specs=[vmem] * 12,
        out_specs=[vmem] * 5,
        scratch_shapes=[
            pltpu.VMEM((y_size, tokens, depth), bf16),
            pltpu.VMEM((y_size - 1, tokens, depth), bf16),
            pltpu.VMEM((tokens, depth), f32),
            pltpu.VMEM((tokens, depth), bf16),
            pltpu.VMEM((tokens, depth), bf16),
            pltpu.VMEM((tokens, depth), bf16),
            pltpu.VMEM((tokens, depth), bf16),
            pltpu.VMEM((16, latents // 8), f32),
            pltpu.VMEM((rows_size - 1, 16, latents // 8), f32),
            dma((hops, 2)), dma((hops, 2)), dma((hops, 2)), dma((hops, 2)),
            dma((Z_CHIPS, 2, x_size - 1)), dma((Z_CHIPS, 2, x_size - 1)),
            dma((rows_size - 1,)), dma((rows_size - 1,)),
            dma((y_size, pieces)), dma((y_size, pieces)),
            dma((y_size - 1, pieces)), dma((y_size - 1, pieces)),
            dma((y_size - 1, pieces)), dma((y_size - 1, pieces)),
            dma((y_size, pieces)), dma((y_size, pieces)),
        ],
        compiler_params=pltpu.CompilerParams(
            collective_id=3, has_side_effects=True, vmem_limit_bytes=60 * 2**20),
        name="front",
    )(picked, norm_params, bias_row, w_joined, w_attn_out, w_mlp_in, w_mlp_out,
      turns, level_lanes, mask_tiles, enc_shard, dec_shard)


def turn_tables(length):
    half = ROT // 2
    freqs = 10000.0 ** (-2.0 * jnp.arange(half, dtype=f32) / ROT)
    angles = jnp.arange(length, dtype=f32)[:, None] * jnp.tile(freqs, PAIR // half)[None, :]
    place = jnp.arange(PAIR) % HEAD
    cosines, sines = jnp.cos(angles), jnp.sin(angles)
    return jnp.stack([
        jnp.where(place < ROT, cosines, 1.0),
        jnp.where(place < half, -sines, 0.0),
        jnp.where((place >= half) & (place < ROT), sines, 0.0),
    ])


def softplus_parts(value):
    power = jnp.exp(value)
    grown = jnp.log(1.0 + power)
    grown = jnp.where(power < 2.0**-8, power * (1.0 - 0.5 * power), grown)
    active = jnp.where(value > 30.0, value, grown)
    return active, jnp.exp(value - active)


def forward_kernel(
    lat_size,
    inputs_ref, enc_ref, dec_ref, enc_bias_ref, mask_ref, dec_bias_ref, scale_ref,
    active_hbm, slope_hbm, mass_out, back_out, stats_out,
    active_buf, slope_buf, product, partial, own, send_two, recv_one, recv_two,
    active_sem, slope_sem, out_one, in_one, out_two, in_two, out_three, in_three, out_four, in_four,
):
    tokens, depth = inputs_ref.shape
    latents = enc_ref.shape[1]
    chunk, span = product.shape[1:]
    width = active_hbm.shape[2]
    chunks, spans = tokens // chunk, latents // span
    y_size = lat_size // CORES
    share = chunk // lat_size
    strip = 16
    row = lax.axis_index("rows")
    lat = lax.axis_index("lat")
    my_y, core = lat // CORES, lax.rem(lat, CORES)
    other = 1 - core

    def y_peer(step):
        return lax.rem(my_y + step, y_size)

    def share_rows(y, which_core):
        return pl.multiple_of((y * CORES + which_core) * share, share)

    def token_rows(block, y, which_core):
        return pl.ds(pl.multiple_of(block * chunk + (y * CORES + which_core) * share, share), share)

    def remote(src, dst, send, recv, target):
        return pltpu.make_async_remote_copy(
            src_ref=src, dst_ref=dst, send_sem=send, recv_sem=recv,
            device_id=(row, target), device_id_type=MESH)

    def copy_one(block, y):
        slot = lax.rem(block, 2)
        return remote(
            partial.at[slot, pl.ds(share_rows(y, other), share)], recv_one.at[block, y],
            out_one.at[slot, y], in_one.at[block, y], my_y * CORES + other)

    def copy_two(block, step):
        slot = lax.rem(block, 2)
        return remote(
            send_two.at[slot, step - 1], recv_two.at[block, step - 1],
            out_two.at[slot, step - 1], in_two.at[block, step - 1], y_peer(step) * CORES + core)

    def copy_three(block, step):
        mine = back_out.at[token_rows(block, my_y, core)]
        return remote(
            mine, mine, out_three.at[block, step - 1], in_three.at[block, step - 1], y_peer(step) * CORES + core)

    def copy_four(block, y):
        mine = back_out.at[token_rows(block, y, core)]
        return remote(mine, mine, out_four.at[block, y], in_four.at[block, y], my_y * CORES + other)

    def stores(block, at, slot):
        rows = pl.ds(pl.multiple_of(block * chunk, chunk), chunk)
        copies = []
        for part in range(span // width):
            lanes = pl.ds(part * width, width)
            copies.append(pltpu.make_async_copy(
                active_buf.at[slot, :, lanes], active_hbm.at[at * (span // width) + part, rows], active_sem.at[slot, part]))
            copies.append(pltpu.make_async_copy(
                slope_buf.at[slot, :, lanes], slope_hbm.at[at * (span // width) + part, rows], slope_sem.at[slot, part]))
        return copies

    barrier = pltpu.get_barrier_semaphore()
    pl.semaphore_signal(barrier, inc=1, device_id=(row, my_y * CORES + other), device_id_type=MESH)
    for step in range(1, y_size):
        pl.semaphore_signal(barrier, inc=1, device_id=(row, y_peer(step) * CORES + core), device_id_type=MESH)
    mass_out[...] = jnp.zeros_like(mass_out)
    stats_out[...] = jnp.zeros_like(stats_out)
    pl.semaphore_wait(barrier, y_size)

    def compute(block):
        place = lax.rem(block, 2)
        first = pl.multiple_of(block * chunk, chunk)

        @pl.when(block >= 2)
        def _():
            for y in range(y_size):
                copy_one(block - 2, y).wait_send()

        for at in range(spans):
            slot = at % 2
            if at >= 2:
                for copy in stores(block, at - 2, slot):
                    copy.wait()
            else:
                @pl.when(block > 0)
                def _():
                    for copy in stores(block - 1, spans - 2 + at, slot):
                        copy.wait()

            product[slot] = jnp.dot(
                inputs_ref[pl.ds(first, chunk), :], enc_ref[:, at * span : (at + 1) * span], preferred_element_type=f32)
            for left in range(0, span, width):
                lanes = pl.ds(left, width)
                cols = pl.ds(at * span + left, width)
                shift = enc_bias_ref[:, cols]
                total = mass_out[:, cols]
                for top in range(0, chunk, strip):
                    rows = pl.ds(top, strip)
                    mask = mask_ref[pl.ds(first + top, strip), :]
                    mask = jnp.concatenate([mask] * (width // 128), axis=1)
                    active, slope = softplus_parts(product[slot, rows, lanes] + shift)
                    active_buf[slot, rows, lanes] = active.astype(bf16)
                    slope_buf[slot, rows, lanes] = slope * mask
                    total = total + (active * mask).reshape(strip // 8, 8, width).sum(0)
                mass_out[:, cols] = total
            for copy in stores(block, at, slot):
                copy.start()
            part = lax.dot_general(
                active_buf[slot], dec_ref[:, at * span : (at + 1) * span], (((1,), (1,)), ((), ())),
                preferred_element_type=f32)
            partial[place] = part if at == 0 else partial[place] + part

    def exchange(block):
        slot = lax.rem(block, 2)
        for y in range(y_size):
            copy_one(block, y).start()
        for y in range(y_size):
            copy_one(block, y).wait_recv()
        for step in list(range(1, y_size)) + [0]:
            y = y_peer(step)
            total = partial[slot, pl.ds(share_rows(y, core), share), :] + recv_one[block, y]
            if step == 0:
                own[slot] = total
            else:
                @pl.when(block >= 2)
                def _():
                    copy_two(block - 2, step).wait_send()

                send_two[slot, step - 1] = total
                copy_two(block, step).start()

    def settle(block):
        slot = lax.rem(block, 2)
        rows = token_rows(block, my_y, core)
        total = own[slot]
        for step in range(1, y_size):
            copy_two(block, step).wait_recv()
            total = total + recv_two[block, step - 1]
        error = total + dec_bias_ref[...] - inputs_ref[rows, :].astype(f32)
        mask = jnp.concatenate([mask_ref[rows, :]] * (depth // 128), axis=1)
        low = (scale_ref[...] * mask * error).astype(bf16)
        back_out[rows, :] = low
        stats_out[0:8, :] += (mask * error * error).reshape(share // 8, 8, depth).sum(0)
        stats_out[8:16, :] += low.astype(f32).reshape(share // 8, 8, depth).sum(0)
        for step in range(1, y_size):
            copy_three(block, step).start()

    def spread(block):
        for step in range(1, y_size):
            copy_three(block, step).wait_recv()
        for y in range(y_size):
            copy_four(block, y).start()

    def turn(block, carry):
        @pl.when(block < chunks)
        def _():
            compute(block)
            exchange(block)

        @pl.when((block >= 1) & (block <= chunks))
        def _():
            settle(block - 1)

        @pl.when(block >= 2)
        def _():
            spread(block - 2)

        return carry

    lax.fori_loop(0, chunks + 2, turn, 0)
    for slot in range(2):
        for copy in stores(chunks - 1, spans - 2 + slot, slot):
            copy.wait()
    for block in range(chunks - 2, chunks):
        for y in range(y_size):
            copy_one(block, y).wait_send()
        for step in range(1, y_size):
            copy_two(block, step).wait_send()

    def drain(block, carry):
        for step in range(1, y_size):
            copy_three(block, step).wait_send()
        for y in range(y_size):
            copy_four(block, y).wait_send()
            copy_four(block, y).wait_recv()
        return carry

    lax.fori_loop(0, chunks, drain, 0)


def forward(lat_size, inputs, enc_low, dec_cols, enc_bias_row, mask_lanes, dec_bias_row, scale_row):
    tokens, depth = inputs.shape
    latents = enc_low.shape[1]
    chunk, span, width = 512, 1024, (512 if tokens <= 4096 else 256)
    chunks = tokens // chunk
    y_size = lat_size // CORES
    share = chunk // lat_size
    dma = pltpu.SemaphoreType.DMA
    vmem = pl.BlockSpec(memory_space=pltpu.VMEM)
    hbm = pl.BlockSpec(memory_space=pl.ANY)
    return pl.pallas_call(
        functools.partial(forward_kernel, lat_size),
        out_shape=[
            jax.ShapeDtypeStruct((latents // width, tokens, width), bf16),
            jax.ShapeDtypeStruct((latents // width, tokens, width), f32),
            jax.ShapeDtypeStruct((8, latents), f32),
            jax.ShapeDtypeStruct((tokens, depth), bf16),
            jax.ShapeDtypeStruct((16, depth), f32),
        ],
        in_specs=[vmem] * 7,
        out_specs=[hbm, hbm, vmem, vmem, vmem],
        scratch_shapes=[
            pltpu.VMEM((2, chunk, span), bf16),
            pltpu.VMEM((2, chunk, span), f32),
            pltpu.VMEM((2, chunk, span), f32),
            pltpu.VMEM((2, chunk, depth), f32),
            pltpu.VMEM((2, share, depth), f32),
            pltpu.VMEM((2, y_size - 1, share, depth), f32),
            pltpu.VMEM((chunks, y_size, share, depth), f32),
            pltpu.VMEM((chunks, y_size - 1, share, depth), f32),
            dma((2, span // width)), dma((2, span // width)),
            dma((2, y_size)), dma((chunks, y_size)),
            dma((2, y_size - 1)), dma((chunks, y_size - 1)),
            dma((chunks, y_size - 1)), dma((chunks, y_size - 1)),
            dma((chunks, y_size)), dma((chunks, y_size)),
        ],
        compiler_params=pltpu.CompilerParams(
            collective_id=1, has_side_effects=True, vmem_limit_bytes=60 * 2**20),
        name="forward",
    )(inputs, enc_low, dec_cols, enc_bias_row, mask_lanes, dec_bias_row, scale_row)


def encode(value):
    top = jnp.max(jnp.abs(value), axis=0, keepdims=True)
    unit = jnp.where(top > 0.0, 32766.0 / top, 0.0)
    shifted = value * unit + 12582912.0
    return (shifted - 12582912.0).astype(jnp.int32).astype(jnp.int16), top * (1.0 / 32766.0)


def decode(code, unit):
    return code.astype(jnp.int32).astype(f32) * unit


def put_units(ref, index, unit):
    for piece in range(unit.shape[1] // 128):
        ref[index + (pl.ds(piece, 1), slice(None))] = unit[:, piece * 128 : piece * 128 + 128]


def get_units(ref, index, width):
    return jnp.concatenate(
        [ref[index + (pl.ds(piece, 1), slice(None))] for piece in range(width // 128)], axis=1)


def backward_kernel(
    rows_size,
    inputs_ref, back_ref, dec_ref, lasso_ref, active_hbm, slope_hbm,
    enc_out, dec_out, bias_out,
    grad_low, active_buf, slope_buf, sums,
    send_one, units_one, recv_one, got_one,
    send_two, units_two, recv_two, got_two,
    active_sem, slope_sem,
    out_one, in_one, outu_one, inu_one, out_two, in_two, outu_two, inu_two,
):
    blocks, tokens, width = active_hbm.shape
    chunk = slope_buf.shape[1]
    chunks = tokens // chunk
    shard = enc_out.shape[0]
    x_size = rows_size // Z_CHIPS
    row = lax.axis_index("rows")
    lat = lax.axis_index("lat")
    my_z, my_x = row // x_size, lax.rem(row, x_size)

    def x_peer(step):
        return lax.rem(my_x + step, x_size)

    def z_peer(step):
        return lax.rem(my_z + step, Z_CHIPS)

    def active_copy(block):
        slot = lax.rem(block, 2)
        return pltpu.make_async_copy(active_hbm.at[block], active_buf.at[slot], active_sem.at[slot])

    def slope_copy(index):
        slot = lax.rem(index, slope_buf.shape[0])
        return pltpu.make_async_copy(
            slope_hbm.at[index // chunks, pl.ds(pl.multiple_of(lax.rem(index, chunks) * chunk, chunk), chunk)],
            slope_buf.at[slot],
            slope_sem.at[slot],
        )

    def copies(stage, block, which, step):
        slot = lax.rem(block, 2)
        if stage == 0:
            target = (my_z * x_size + x_peer(step), lat)
            refs = (send_one, recv_one, out_one, in_one, units_one, got_one, outu_one, inu_one)
        else:
            target = (z_peer(step) * x_size + my_x, lat)
            refs = (send_two, recv_two, out_two, in_two, units_two, got_two, outu_two, inu_two)
        return [
            pltpu.make_async_remote_copy(
                src_ref=refs[at].at[slot, which, step - 1], dst_ref=refs[at + 1].at[block, which, step - 1],
                send_sem=refs[at + 2].at[slot, which, step - 1], recv_sem=refs[at + 3].at[block, which, step - 1],
                device_id=target, device_id_type=MESH)
            for at in (0, 4)
        ]

    barrier = pltpu.get_barrier_semaphore()
    for step in range(1, x_size):
        pl.semaphore_signal(barrier, inc=1, device_id=(my_z * x_size + x_peer(step), lat), device_id_type=MESH)
    for step in range(1, Z_CHIPS):
        pl.semaphore_signal(barrier, inc=1, device_id=(z_peer(step) * x_size + my_x, lat), device_id_type=MESH)
    active_copy(0).start()
    ahead = slope_buf.shape[0] - 1
    for index in range(ahead):
        slope_copy(index).start()
    pl.semaphore_wait(barrier, x_size + Z_CHIPS - 2)

    def columns(block):
        return pl.ds(pl.multiple_of(block * width, width), width)

    over_tokens = (((0,), (0,)), ((), ()))

    def compute_dec(block):
        slot = lax.rem(block, 2)

        @pl.when(block + 1 < blocks)
        def _():
            active_copy(block + 1).start()

        active_copy(block).wait()
        sums[slot, 1] = lax.dot_general(back_ref[...], active_buf[slot], over_tokens, preferred_element_type=f32)

    def compute_enc(block):
        slot = lax.rem(block, 2)
        cols = columns(block)

        def piece(index, total):
            at = block * chunks + index

            @pl.when(at + ahead < blocks * chunks)
            def _():
                slope_copy(at + ahead).start()

            slope_copy(at).wait()
            rows = pl.ds(pl.multiple_of(index * chunk, chunk), chunk)
            back = jnp.dot(back_ref[rows, :], dec_ref[:, cols], preferred_element_type=f32)
            low = ((back + lasso_ref[:, cols]) * slope_buf[lax.rem(at, ahead + 1)]).astype(bf16)
            grad_low[rows, :] = low
            return total + low.astype(f32).reshape(chunk // 8, 8, width).sum(0)

        bias_out[:, cols] = lax.fori_loop(0, chunks, piece, jnp.zeros((8, width), f32))
        sums[slot, 0] = lax.dot_general(inputs_ref[...], grad_low[...], over_tokens, preferred_element_type=f32)

    def send_x(block, which):
        slot = lax.rem(block, 2)
        for step in range(1, x_size):
            @pl.when(block >= 2)
            def _():
                for copy in copies(0, block - 2, which, step):
                    copy.wait_send()

            parts = []
            for z in range(Z_CHIPS):
                first = pl.multiple_of((z * x_size + x_peer(step)) * shard, shard)
                parts.append(sums[slot, which, pl.ds(first, shard), :])
            code, unit = encode(jnp.concatenate(parts, axis=0))
            for z in range(Z_CHIPS):
                send_one[slot, which, step - 1, z] = code[z * shard : (z + 1) * shard]
            put_units(units_one, (slot, which, step - 1), unit)
            for copy in copies(0, block, which, step):
                copy.start()

    def send_z(block, which):
        slot = lax.rem(block, 2)
        for step in range(1, x_size):
            for copy in copies(0, block, which, step):
                copy.wait_recv()
        for step in range(Z_CHIPS):
            z = z_peer(step)
            if step:
                @pl.when(block >= 2)
                def _():
                    for copy in copies(1, block - 2, which, step):
                        copy.wait_send()

            first = pl.multiple_of((z * x_size + my_x) * shard, shard)
            total = sums[slot, which, pl.ds(first, shard), :]
            for x_step in range(1, x_size):
                total = total + decode(
                    recv_one[block, which, x_step - 1, z], get_units(got_one, (block, which, x_step - 1), width))
            if step == 0:
                (enc_out, dec_out)[which][:, columns(block)] = total
            else:
                code, unit = encode(total)
                send_two[slot, which, step - 1] = code
                put_units(units_two, (slot, which, step - 1), unit)
                for copy in copies(1, block, which, step):
                    copy.start()

    def finish(block, which):
        slot = lax.rem(block, 2)
        for step in range(1, Z_CHIPS):
            for copy in copies(1, block, which, step):
                copy.wait_recv()
        out, cols = (enc_out, dec_out)[which], columns(block)
        total = out[:, cols]
        for step in range(1, Z_CHIPS):
            total = total + decode(
                recv_two[block, which, step - 1], get_units(got_two, (block, which, step - 1), width))
        out[:, cols] = total

    def turn(block, carry):
        for which, compute in ((1, compute_dec), (0, compute_enc)):
            @pl.when(block < blocks)
            def _():
                compute(block)
                send_x(block, which)

            @pl.when((block >= 1) & (block <= blocks))
            def _():
                send_z(block - 1, which)

            @pl.when(block >= 2)
            def _():
                finish(block - 2, which)

        return carry

    lax.fori_loop(0, blocks + 2, turn, 0)
    for block in range(max(blocks - 2, 0), blocks):
        for which in range(2):
            for stage, size in ((0, x_size), (1, Z_CHIPS)):
                for step in range(1, size):
                    for copy in copies(stage, block, which, step):
                        copy.wait_send()


def backward(rows_size, inputs, back, dec_cols, lasso_row, active, slope):
    blocks, tokens, width = active.shape
    depth = inputs.shape[1]
    shard = depth // rows_size
    latents = dec_cols.shape[1]
    x_size = rows_size // Z_CHIPS
    chunk = min(CHUNK, tokens)
    i16 = jnp.int16
    dma = pltpu.SemaphoreType.DMA
    vmem = pl.BlockSpec(memory_space=pltpu.VMEM)
    hbm = pl.BlockSpec(memory_space=pl.ANY)
    return pl.pallas_call(
        functools.partial(backward_kernel, rows_size),
        out_shape=[
            jax.ShapeDtypeStruct((shard, latents), f32),
            jax.ShapeDtypeStruct((shard, latents), f32),
            jax.ShapeDtypeStruct((8, latents), f32),
        ],
        in_specs=[vmem] * 4 + [hbm] * 2,
        out_specs=[vmem] * 3,
        scratch_shapes=[
            pltpu.VMEM((tokens, width), bf16),
            pltpu.VMEM((2, tokens, width), bf16),
            pltpu.VMEM((SLOTS, chunk, width), f32),
            pltpu.VMEM((2, 2, depth, width), f32),
            pltpu.VMEM((2, 2, x_size - 1, Z_CHIPS, shard, width), i16),
            pltpu.VMEM((2, 2, x_size - 1, 8, 128), f32),
            pltpu.VMEM((blocks, 2, x_size - 1, Z_CHIPS, shard, width), i16),
            pltpu.VMEM((blocks, 2, x_size - 1, 8, 128), f32),
            pltpu.VMEM((2, 2, Z_CHIPS - 1, shard, width), i16),
            pltpu.VMEM((2, 2, Z_CHIPS - 1, 8, 128), f32),
            pltpu.VMEM((blocks, 2, Z_CHIPS - 1, shard, width), i16),
            pltpu.VMEM((blocks, 2, Z_CHIPS - 1, 8, 128), f32),
            dma((2,)), dma((SLOTS,)),
            dma((2, 2, x_size - 1)), dma((blocks, 2, x_size - 1)),
            dma((2, 2, x_size - 1)), dma((blocks, 2, x_size - 1)),
            dma((2, 2, Z_CHIPS - 1)), dma((blocks, 2, Z_CHIPS - 1)),
            dma((2, 2, Z_CHIPS - 1)), dma((blocks, 2, Z_CHIPS - 1)),
        ],
        compiler_params=pltpu.CompilerParams(
            collective_id=2, has_side_effects=True, vmem_limit_bytes=60 * 2**20),
        name="backward",
    )(inputs, back, dec_cols, lasso_row, active, slope)


def body(
    token_ids,
    token_mask,
    scale_index,
    embed,
    norm_params,
    frozen_bias,
    w_joined,
    w_attn_out,
    w_mlp_in,
    w_mlp_out,
    enc_weight,
    enc_moment,
    enc_second,
    dec_weight,
    dec_moment,
    dec_second,
    enc_bias,
    enc_bias_moment,
    enc_bias_second,
    dec_bias,
    dec_bias_moment,
    dec_bias_second,
):
    lat_size = lax.axis_size("lat")
    lat_index = lax.axis_index("lat")
    group_tokens = token_ids.shape[0]
    tok_local = group_tokens // lat_size
    rows_size = lax.axis_size("rows")
    depth = enc_weight.shape[0] * rows_size
    mask_float = token_mask.astype(f32)
    dec_master = dec_weight.T
    bias_row = frozen_bias[None, :]
    vocab_local = embed.shape[0]
    vocab_first = lat_index * vocab_local
    local_ids = token_ids - vocab_first
    inside = ((local_ids >= 0) & (local_ids < vocab_local)).astype(f32)
    picked = jnp.take(embed, jnp.clip(local_ids, 0, vocab_local - 1), axis=0).astype(f32)
    picked = (picked * inside[:, None]).astype(bf16)
    own_first = lat_index * tok_local
    scales = 0.5 + 0.25 * lax.dynamic_slice_in_dim(scale_index, own_first, tok_local).astype(f32)
    level_lanes = jnp.broadcast_to(scales[:, None], (tok_local, 128))
    all_inputs, enc_low, dec_cols, norms_row, counts = front(
        rows_size, lat_size, picked, norm_params, bias_row, w_joined, w_attn_out, w_mlp_in, w_mlp_out,
        turn_tables(tok_local), level_lanes, mask_float.reshape(-1, 128), enc_weight, dec_master)
    count = counts[0, 0]
    norms = norms_row[0]
    mask_lanes = jnp.broadcast_to(mask_float[:, None], (group_tokens, 128))
    scale_row = jnp.full((1, depth), 2.0 / count, f32)
    lasso_scale = lasso_coef / count
    active, slope, mass_rows, recon_grad, stats = forward(
        lat_size, all_inputs, enc_low, dec_cols, enc_bias[None, :], mask_lanes, dec_bias[None, :], scale_row)
    grad_enc, grad_dec, bias_rows = backward(
        rows_size, all_inputs, recon_grad, dec_cols, lasso_scale * norms_row, active, slope)
    bias_mass = jnp.stack([bias_rows.sum(0), mass_rows.sum(0)])
    grad_enc_bias, active_mass = lax.psum(bias_mass, "rows")
    leader = (lax.axis_index("rows") == 0).astype(f32)
    lasso_part = lasso_coef * jnp.sum(active_mass * norms) * leader
    loss_sum, grad_dec_bias = lax.psum((jnp.sum(stats[:8]) + lasso_part, stats[8:].sum(0)), ("rows", "lat"))
    grad_dec = grad_dec + (lasso_scale * active_mass / norms)[None, :] * dec_master
    local_squares = (
        jnp.sum(grad_enc * grad_enc) + jnp.sum(grad_dec * grad_dec)
        + jnp.sum(grad_enc_bias * grad_enc_bias) * leader
    )
    squares = lax.psum(local_squares, ("rows", "lat")) + jnp.sum(grad_dec_bias * grad_dec_bias)
    grad_norm = jnp.sqrt(squares)
    factor = clip_bound / jnp.maximum(grad_norm, clip_bound)
    enc_new = adam_update(enc_weight, enc_moment, enc_second, grad_enc * factor, weight_decay)
    dec_new = adam_update(dec_weight, dec_moment, dec_second, grad_dec.T * factor, weight_decay)
    enc_bias_new = adam_update(
        enc_bias, enc_bias_moment, enc_bias_second, grad_enc_bias * factor, 0.0
    )
    dec_bias_new = adam_update(
        dec_bias, dec_bias_moment, dec_bias_second, grad_dec_bias * factor, 0.0
    )
    return (
        enc_new[0],
        enc_new[1],
        enc_new[2],
        dec_new[0],
        dec_new[1],
        dec_new[2],
        enc_bias_new[0],
        enc_bias_new[1],
        enc_bias_new[2],
        dec_bias_new[0],
        dec_bias_new[1],
        dec_bias_new[2],
        grad_norm,
        loss_sum,
        count,
    )


def solution(mesh):
    placed = (
        P("rows"),
        P("rows"),
        P("rows"),
        P("lat", None),
        P(),
        P(),
        P(),
        P(),
        P(),
        P(),
        P("rows", "lat"),
        P("rows", "lat"),
        P("rows", "lat"),
        P("lat", "rows"),
        P("lat", "rows"),
        P("lat", "rows"),
        P("lat"),
        P("lat"),
        P("lat"),
        P(),
        P(),
        P(),
    )
    return jax.shard_map(
        body,
        mesh=mesh,
        in_specs=placed,
        out_specs=(
            P("rows", "lat"),
            P("rows", "lat"),
            P("rows", "lat"),
            P("lat", "rows"),
            P("lat", "rows"),
            P("lat", "rows"),
            P("lat"),
            P("lat"),
            P("lat"),
            P(),
            P(),
            P(),
            P(),
            P(),
            P(),
        ),
        check_vma=False,
    )
```

```python
import functools
import jax
import jax.numpy as jnp
from jax import lax
from jax.experimental import pallas as pl
from jax.experimental.pallas import tpu as pltpu
from jax.sharding import PartitionSpec as P

HEADS = 8
ROT = 16
STEP = 10
Z_CHIPS = 4
CORES = 2
SLOTS = 6
CHUNK = 1024
MESH = pl.DeviceIdType.MESH
f32 = jnp.float32
bf16 = jnp.bfloat16


lasso_coef = 5.0
clip_bound = 1.0
learn_rate = 0.03
beta_one = 0.9
beta_two = 0.999
adam_eps = 1e-08
weight_decay = 0.01


def adam_update(weight, moment, second, grad, decay):
    moment_new = beta_one * moment + (1.0 - beta_one) * grad
    second_new = beta_two * second + (1.0 - beta_two) * grad * grad
    corrected = moment_new / (1.0 - beta_one**STEP)
    scaled = jnp.sqrt(second_new / (1.0 - beta_two**STEP)) + adam_eps
    weight_new = weight - learn_rate * (corrected / scaled + decay * weight)
    return (weight_new, moment_new, second_new)


ROWS = 512
PIECE = 256
HEAD = 64
PAIR = 128


def front_kernel(
    rows_size, lat_size,
    picked_ref, norm_ref, bias_ref, joined_ref, attn_ref, mlp_in_ref, mlp_out_ref,
    turn_ref, level_ref, mask_ref, enc_ref, dec_ref,
    inputs_out, enc_out, dec_out, norms_out, count_out,
    from_core, from_y, base, queries, keys, values, context, facts, got_facts,
    out_right, in_left, out_left, in_right, out_x, in_x, out_fact, in_fact,
    out_core, in_core, out_y, in_y, out_own, in_own, out_near, in_near,
):
    tokens, depth = base.shape
    shard = enc_ref.shape[0]
    latents = enc_ref.shape[1]
    hidden = mlp_in_ref.shape[1]
    x_size = rows_size // Z_CHIPS
    y_size = lat_size // CORES
    pieces = tokens // PIECE
    row = lax.axis_index("rows")
    lat = lax.axis_index("lat")
    my_z, my_x = row // x_size, lax.rem(row, x_size)
    my_y, core = lat // CORES, lax.rem(lat, CORES)
    other = 1 - core

    def remote(src, dst, send, recv, to_row, to_lat):
        return pltpu.make_async_remote_copy(
            src_ref=src, dst_ref=dst, send_sem=send, recv_sem=recv,
            device_id=(to_row, to_lat), device_id_type=MESH)

    def peer_row(step):
        return lax.rem(row + step, rows_size)

    def x_row(step):
        return my_z * x_size + lax.rem(my_x + step, x_size)

    def y_peer(step):
        return lax.rem(my_y + step, y_size)

    barrier = pltpu.get_barrier_semaphore()
    for step in range(1, rows_size):
        pl.semaphore_signal(barrier, inc=1, device_id=(peer_row(step), lat), device_id_type=MESH)
    for step in range(1, y_size):
        pl.semaphore_signal(barrier, inc=1, device_id=(row, y_peer(step) * CORES + core), device_id_type=MESH)
    pl.semaphore_signal(barrier, inc=1, device_id=(row, my_y * CORES + other), device_id_type=MESH)

    mine = pl.ds(pl.multiple_of(row * shard, shard), shard)
    enc_out[mine, :] = enc_ref[...].astype(bf16)
    dec_out[mine, :] = dec_ref[...].astype(bf16)
    square = jnp.sum(dec_ref[...] * dec_ref[...], axis=0, keepdims=True)
    part = latents // 8
    for at in range(8):
        facts[pl.ds(at, 1), :] = square[:, at * part : (at + 1) * part]
    facts[8:16, :] = jnp.broadcast_to(jnp.sum(mask_ref[...], keepdims=True), (8, part))
    pl.semaphore_wait(barrier, rows_size + y_size - 1)

    weights = (enc_out, dec_out)

    def weight_rows(z):
        return pl.ds(pl.multiple_of((z * x_size + my_x) * shard, shard), shard)

    def right_copy(hop, which, received=False):
        area = weights[which].at[weight_rows(jnp.maximum(my_z - hop - (1 if received else 0), 0))]
        return remote(area, area, out_right.at[hop, which], in_left.at[hop, which],
                      jnp.minimum(my_z + 1, Z_CHIPS - 1) * x_size + my_x, lat)

    def left_copy(hop, which, received=False):
        area = weights[which].at[weight_rows(jnp.minimum(my_z + hop + (1 if received else 0), Z_CHIPS - 1))]
        return remote(area, area, out_left.at[hop, which], in_right.at[hop, which],
                      jnp.maximum(my_z - 1, 0) * x_size + my_x, lat)

    def x_copy(z, which, step):
        area = weights[which].at[weight_rows(z)]
        return remote(area, area, out_x.at[z, which, step - 1], in_x.at[z, which, step - 1], x_row(step), lat)

    def pass_on(hop, which):
        if hop == 0:
            @pl.when(my_z < Z_CHIPS - 1)
            def _():
                right_copy(0, which).start()

            @pl.when(my_z > 0)
            def _():
                left_copy(0, which).start()

            for step in range(1, x_size):
                x_copy(my_z, which, step).start()
            return

        @pl.when(my_z >= hop)
        def _():
            right_copy(hop - 1, which, True).wait_recv()
            if hop < Z_CHIPS - 1:
                @pl.when(my_z < Z_CHIPS - 1)
                def _():
                    right_copy(hop, which).start()
            for step in range(1, x_size):
                x_copy(my_z - hop, which, step).start()

        @pl.when(my_z + hop <= Z_CHIPS - 1)
        def _():
            left_copy(hop - 1, which, True).wait_recv()
            if hop < Z_CHIPS - 1:
                @pl.when(my_z > 0)
                def _():
                    left_copy(hop, which).start()
            for step in range(1, x_size):
                x_copy(my_z + hop, which, step).start()

    def fact_copy(step):
        return remote(facts, got_facts.at[step - 1], out_fact.at[step - 1], in_fact.at[step - 1], peer_row(step), lat)

    def block_rows(y, which_core, piece):
        return pl.ds(pl.multiple_of((y * CORES + which_core) * tokens + piece * PIECE, PIECE), PIECE)

    def core_copy(step, piece):
        return remote(
            picked_ref.at[block_rows(y_peer(step), other, piece)], from_core.at[step, pl.ds(piece * PIECE, PIECE)],
            out_core.at[step, piece], in_core.at[step, piece], row, my_y * CORES + other)

    def y_copy(step, piece):
        here = pl.ds(piece * PIECE, PIECE)
        return remote(
            from_core.at[step, here], from_y.at[step - 1, here],
            out_y.at[step - 1, piece], in_y.at[step - 1, piece], row, y_peer(step) * CORES + core)

    for piece in range(pieces):
        for step in list(range(1, y_size)) + [0]:
            core_copy(step, piece).start()
    for which in range(2):
        pass_on(0, which)
    for step in range(1, rows_size):
        fact_copy(step).start()
    for piece in range(pieces):
        here = pl.ds(piece * PIECE, PIECE)
        for step in list(range(1, y_size)) + [0]:
            core_copy(step, piece).wait_recv()
            total = picked_ref[block_rows(y_peer(step), core, piece), :].astype(f32) + from_core[step, here, :].astype(f32)
            if step == 0:
                base[here, :] = total
            else:
                from_core[step, here, :] = total.astype(bf16)
                y_copy(step, piece).start()
    pass_on(1, 0)

    def normed(value, gain, shift):
        centred = value - jnp.mean(value, axis=1, keepdims=True)
        spread = jnp.mean(centred * centred, axis=1, keepdims=True)
        return (centred * lax.rsqrt(spread + 1e-05) * gain + shift).astype(bf16)

    def dot(left, right):
        return jnp.dot(left, right, preferred_element_type=f32)

    def rotated(value, rows):
        cosine, low, high = turn_ref[0, rows, :], turn_ref[1, rows, :], turn_ref[2, rows, :]
        parts = []
        for at in range(depth // PAIR):
            tile = value[:, at * PAIR : (at + 1) * PAIR]
            parts.append(
                tile * cosine + pltpu.roll(tile, PAIR - ROT // 2, 1) * low + pltpu.roll(tile, ROT // 2, 1) * high)
        return jnp.concatenate(parts, axis=1)

    for block in range(tokens // ROWS):
        rows = pl.ds(block * ROWS, ROWS)
        for piece in range(block * ROWS // PIECE, (block + 1) * ROWS // PIECE):
            for step in range(1, y_size):
                y_copy(step, piece).wait_recv()
        embedded = base[rows, :]
        for step in range(1, y_size):
            embedded = embedded + from_y[step - 1, rows, :].astype(f32)
        attn_in = normed(embedded, norm_ref[0:1, :], norm_ref[1:2, :])
        joined = dot(attn_in, joined_ref[...]) + bias_ref[:, : 3 * depth]
        queries[rows, :] = (rotated(joined[:, :depth], rows).astype(bf16) * HEAD**-0.5).astype(bf16)
        keys[rows, :] = rotated(joined[:, depth : 2 * depth], rows).astype(bf16)
        values[rows, :] = joined[:, 2 * depth :].astype(bf16)
        mlp_in = normed(embedded, norm_ref[2:3, :], norm_ref[3:4, :])
        inner = dot(mlp_in, mlp_in_ref[...]) + bias_ref[:, 4 * depth : 4 * depth + hidden]
        inner = (0.5 * inner * (1.0 + lax.erf(inner * 0.5**0.5))).astype(bf16)
        base[rows, :] = embedded + (dot(inner, mlp_out_ref[...]) + bias_ref[:, 4 * depth + hidden :])
        if block == 0:
            pass_on(1, 1)
    pass_on(2, 0)

    def own_rows(y, which_core, piece):
        return pl.ds(pl.multiple_of((y * CORES + which_core) * tokens + piece * PIECE, PIECE), PIECE)

    def own_copy(step, piece):
        area = inputs_out.at[own_rows(my_y, core, piece)]
        return remote(area, area, out_own.at[step - 1, piece], in_own.at[step - 1, piece], row, y_peer(step) * CORES + core)

    def near_copy(step, piece):
        area = inputs_out.at[own_rows(y_peer(step), core, piece)]
        return remote(area, area, out_near.at[step, piece], in_near.at[step, piece], row, my_y * CORES + other)

    lanes = lax.broadcasted_iota(jnp.int32, (PIECE, PAIR), 1)
    for piece in range(pieces):
        here = pl.ds(piece * PIECE, PIECE)
        reach = (piece + 1) * PIECE
        visible = (
            lax.broadcasted_iota(jnp.int32, (PIECE, reach), 0) + piece * PIECE
            >= lax.broadcasted_iota(jnp.int32, (PIECE, reach), 1)
        )

        def attend(pair, carry):
            cols = pl.ds(pl.multiple_of(pair * PAIR, PAIR), PAIR)
            both = queries[here, cols]
            found = []
            for first in (True, False):
                chosen = jnp.where((lanes < HEAD) == first, both, jnp.zeros_like(both))
                scores = lax.dot_general(
                    chosen, keys[0:reach, cols], (((1,), (1,)), ((), ())), preferred_element_type=f32)
                scores = jnp.where(visible, scores, -1e30)
                powers = jnp.exp(scores - jnp.max(scores, axis=1, keepdims=True))
                probs = (powers * (1.0 / jnp.sum(powers, axis=1, keepdims=True))).astype(bf16)
                found.append(dot(probs, values[0:reach, cols]))
            context[here, cols] = jnp.where(lanes < HEAD, found[0], found[1]).astype(bf16)
            return carry

        lax.fori_loop(0, depth // PAIR, attend, 0)
        attended = dot(context[here, :], attn_ref[...]) + bias_ref[:, 3 * depth : 4 * depth]
        level = jnp.concatenate([level_ref[here, :]] * (depth // 128), axis=1)
        inputs_out[own_rows(my_y, core, piece), :] = ((base[here, :] + attended) * level).astype(bf16)
        for step in range(1, y_size):
            own_copy(step, piece).start()
        near_copy(0, piece).start()
        if piece == 1:
            pass_on(2, 1)
        if piece >= 2:
            for step in range(1, y_size):
                own_copy(step, piece - 2).wait_recv()
                near_copy(step, piece - 2).start()

    total = facts[...]
    for step in range(1, rows_size):
        fact_copy(step).wait_recv()
        total = total + got_facts[step - 1]
    count_out[...] = total[8:16, 0:128]
    norms = jnp.sqrt(total[0:8, :])
    for at in range(8):
        norms_out[:, at * part : (at + 1) * part] = norms[at : at + 1, :]
    pass_on(3, 0)
    for piece in range(pieces - 2, pieces):
        for step in range(1, y_size):
            own_copy(step, piece).wait_recv()
            near_copy(step, piece).start()
    pass_on(3, 1)

    for which in range(2):
        for hop in range(Z_CHIPS - 1):
            @pl.when((my_z < Z_CHIPS - 1) & (my_z >= hop))
            def _():
                right_copy(hop, which).wait_send()

            @pl.when((my_z > 0) & (my_z + hop <= Z_CHIPS - 1))
            def _():
                left_copy(hop, which).wait_send()

        for z in range(Z_CHIPS):
            for step in range(1, x_size):
                x_copy(z, which, step).wait_send()
                x_copy(z, which, step).wait_recv()
    for step in range(1, rows_size):
        fact_copy(step).wait_send()
    for piece in range(pieces):
        for step in range(y_size):
            core_copy(step, piece).wait_send()
            near_copy(step, piece).wait_send()
            near_copy(step, piece).wait_recv()
        for step in range(1, y_size):
            y_copy(step, piece).wait_send()
            own_copy(step, piece).wait_send()


def front(rows_size, lat_size, picked, norm_params, bias_row, w_joined, w_attn_out, w_mlp_in, w_mlp_out,
          turns, level_lanes, mask_tiles, enc_shard, dec_shard):
    group, depth = picked.shape
    tokens = group // lat_size
    shard, latents = enc_shard.shape
    x_size = rows_size // Z_CHIPS
    y_size = lat_size // CORES
    pieces = tokens // PIECE
    dma = pltpu.SemaphoreType.DMA
    vmem = pl.BlockSpec(memory_space=pltpu.VMEM)
    hops = Z_CHIPS - 1
    return pl.pallas_call(
        functools.partial(front_kernel, rows_size, lat_size),
        out_shape=[
            jax.ShapeDtypeStruct((group, depth), bf16),
            jax.ShapeDtypeStruct((depth, latents), bf16),
            jax.ShapeDtypeStruct((depth, latents), bf16),
            jax.ShapeDtypeStruct((1, latents), f32),
            jax.ShapeDtypeStruct((8, 128), f32),
        ],
        in_specs=[vmem] * 12,
        out_specs=[vmem] * 5,
        scratch_shapes=[
            pltpu.VMEM((y_size, tokens, depth), bf16),
            pltpu.VMEM((y_size - 1, tokens, depth), bf16),
            pltpu.VMEM((tokens, depth), f32),
            pltpu.VMEM((tokens, depth), bf16),
            pltpu.VMEM((tokens, depth), bf16),
            pltpu.VMEM((tokens, depth), bf16),
            pltpu.VMEM((tokens, depth), bf16),
            pltpu.VMEM((16, latents // 8), f32),
            pltpu.VMEM((rows_size - 1, 16, latents // 8), f32),
            dma((hops, 2)), dma((hops, 2)), dma((hops, 2)), dma((hops, 2)),
            dma((Z_CHIPS, 2, x_size - 1)), dma((Z_CHIPS, 2, x_size - 1)),
            dma((rows_size - 1,)), dma((rows_size - 1,)),
            dma((y_size, pieces)), dma((y_size, pieces)),
            dma((y_size - 1, pieces)), dma((y_size - 1, pieces)),
            dma((y_size - 1, pieces)), dma((y_size - 1, pieces)),
            dma((y_size, pieces)), dma((y_size, pieces)),
        ],
        compiler_params=pltpu.CompilerParams(
            collective_id=3, has_side_effects=True, vmem_limit_bytes=60 * 2**20),
        name="front",
    )(picked, norm_params, bias_row, w_joined, w_attn_out, w_mlp_in, w_mlp_out,
      turns, level_lanes, mask_tiles, enc_shard, dec_shard)


def turn_tables(length):
    half = ROT // 2
    freqs = 10000.0 ** (-2.0 * jnp.arange(half, dtype=f32) / ROT)
    angles = jnp.arange(length, dtype=f32)[:, None] * jnp.tile(freqs, PAIR // half)[None, :]
    place = jnp.arange(PAIR) % HEAD
    cosines, sines = jnp.cos(angles), jnp.sin(angles)
    return jnp.stack([
        jnp.where(place < ROT, cosines, 1.0),
        jnp.where(place < half, -sines, 0.0),
        jnp.where((place >= half) & (place < ROT), sines, 0.0),
    ])


def softplus_parts(value):
    power = jnp.exp(value)
    grown = jnp.log(1.0 + power)
    grown = jnp.where(power < 2.0**-8, power * (1.0 - 0.5 * power), grown)
    active = jnp.where(value > 30.0, value, grown)
    return active, jnp.exp(value - active)


def forward_kernel(
    lat_size,
    inputs_ref, enc_ref, dec_ref, enc_bias_ref, mask_ref, dec_bias_ref, scale_ref,
    active_hbm, slope_hbm, mass_out, back_out, stats_out,
    active_buf, slope_buf, product, partial, own, send_two, recv_one, recv_two,
    active_sem, slope_sem, out_one, in_one, out_two, in_two, out_three, in_three, out_four, in_four,
):
    tokens, depth = inputs_ref.shape
    latents = enc_ref.shape[1]
    chunk, span = product.shape[1:]
    width = active_hbm.shape[2]
    chunks, spans = tokens // chunk, latents // span
    y_size = lat_size // CORES
    share = chunk // lat_size
    strip = 16
    row = lax.axis_index("rows")
    lat = lax.axis_index("lat")
    my_y, core = lat // CORES, lax.rem(lat, CORES)
    other = 1 - core

    def y_peer(step):
        return lax.rem(my_y + step, y_size)

    def share_rows(y, which_core):
        return pl.multiple_of((y * CORES + which_core) * share, share)

    def token_rows(block, y, which_core):
        return pl.ds(pl.multiple_of(block * chunk + (y * CORES + which_core) * share, share), share)

    def remote(src, dst, send, recv, target):
        return pltpu.make_async_remote_copy(
            src_ref=src, dst_ref=dst, send_sem=send, recv_sem=recv,
            device_id=(row, target), device_id_type=MESH)

    def copy_one(block, y):
        slot = lax.rem(block, 2)
        return remote(
            partial.at[slot, pl.ds(share_rows(y, other), share)], recv_one.at[block, y],
            out_one.at[slot, y], in_one.at[block, y], my_y * CORES + other)

    def copy_two(block, step):
        slot = lax.rem(block, 2)
        return remote(
            send_two.at[slot, step - 1], recv_two.at[block, step - 1],
            out_two.at[slot, step - 1], in_two.at[block, step - 1], y_peer(step) * CORES + core)

    def copy_three(block, step):
        mine = back_out.at[token_rows(block, my_y, core)]
        return remote(
            mine, mine, out_three.at[block, step - 1], in_three.at[block, step - 1], y_peer(step) * CORES + core)

    def copy_four(block, y):
        mine = back_out.at[token_rows(block, y, core)]
        return remote(mine, mine, out_four.at[block, y], in_four.at[block, y], my_y * CORES + other)

    def stores(block, at, slot):
        rows = pl.ds(pl.multiple_of(block * chunk, chunk), chunk)
        copies = []
        for part in range(span // width):
            lanes = pl.ds(part * width, width)
            copies.append(pltpu.make_async_copy(
                active_buf.at[slot, :, lanes], active_hbm.at[at * (span // width) + part, rows], active_sem.at[slot, part]))
            copies.append(pltpu.make_async_copy(
                slope_buf.at[slot, :, lanes], slope_hbm.at[at * (span // width) + part, rows], slope_sem.at[slot, part]))
        return copies

    barrier = pltpu.get_barrier_semaphore()
    pl.semaphore_signal(barrier, inc=1, device_id=(row, my_y * CORES + other), device_id_type=MESH)
    for step in range(1, y_size):
        pl.semaphore_signal(barrier, inc=1, device_id=(row, y_peer(step) * CORES + core), device_id_type=MESH)
    mass_out[...] = jnp.zeros_like(mass_out)
    stats_out[...] = jnp.zeros_like(stats_out)
    pl.semaphore_wait(barrier, y_size)

    def compute(block):
        place = lax.rem(block, 2)
        first = pl.multiple_of(block * chunk, chunk)

        @pl.when(block >= 2)
        def _():
            for y in range(y_size):
                copy_one(block - 2, y).wait_send()

        for at in range(spans):
            slot = at % 2
            if at >= 2:
                for copy in stores(block, at - 2, slot):
                    copy.wait()
            else:
                @pl.when(block > 0)
                def _():
                    for copy in stores(block - 1, spans - 2 + at, slot):
                        copy.wait()

            product[slot] = jnp.dot(
                inputs_ref[pl.ds(first, chunk), :], enc_ref[:, at * span : (at + 1) * span], preferred_element_type=f32)
            for left in range(0, span, width):
                lanes = pl.ds(left, width)
                cols = pl.ds(at * span + left, width)
                shift = enc_bias_ref[:, cols]
                total = mass_out[:, cols]
                for top in range(0, chunk, strip):
                    rows = pl.ds(top, strip)
                    mask = mask_ref[pl.ds(first + top, strip), :]
                    mask = jnp.concatenate([mask] * (width // 128), axis=1)
                    active, slope = softplus_parts(product[slot, rows, lanes] + shift)
                    active_buf[slot, rows, lanes] = active.astype(bf16)
                    slope_buf[slot, rows, lanes] = slope * mask
                    total = total + (active * mask).reshape(strip // 8, 8, width).sum(0)
                mass_out[:, cols] = total
            for copy in stores(block, at, slot):
                copy.start()
            part = lax.dot_general(
                active_buf[slot], dec_ref[:, at * span : (at + 1) * span], (((1,), (1,)), ((), ())),
                preferred_element_type=f32)
            partial[place] = part if at == 0 else partial[place] + part

    def exchange(block):
        slot = lax.rem(block, 2)
        for y in range(y_size):
            copy_one(block, y).start()
        for y in range(y_size):
            copy_one(block, y).wait_recv()
        for step in list(range(1, y_size)) + [0]:
            y = y_peer(step)
            total = partial[slot, pl.ds(share_rows(y, core), share), :] + recv_one[block, y]
            if step == 0:
                own[slot] = total
            else:
                @pl.when(block >= 2)
                def _():
                    copy_two(block - 2, step).wait_send()

                send_two[slot, step - 1] = total
                copy_two(block, step).start()

    def settle(block):
        slot = lax.rem(block, 2)
        rows = token_rows(block, my_y, core)
        total = own[slot]
        for step in range(1, y_size):
            copy_two(block, step).wait_recv()
            total = total + recv_two[block, step - 1]
        error = total + dec_bias_ref[...] - inputs_ref[rows, :].astype(f32)
        mask = jnp.concatenate([mask_ref[rows, :]] * (depth // 128), axis=1)
        low = (scale_ref[...] * mask * error).astype(bf16)
        back_out[rows, :] = low
        stats_out[0:8, :] += (mask * error * error).reshape(share // 8, 8, depth).sum(0)
        stats_out[8:16, :] += low.astype(f32).reshape(share // 8, 8, depth).sum(0)
        for step in range(1, y_size):
            copy_three(block, step).start()

    def spread(block):
        for step in range(1, y_size):
            copy_three(block, step).wait_recv()
        for y in range(y_size):
            copy_four(block, y).start()

    def turn(block, carry):
        @pl.when(block < chunks)
        def _():
            compute(block)
            exchange(block)

        @pl.when((block >= 1) & (block <= chunks))
        def _():
            settle(block - 1)

        @pl.when(block >= 2)
        def _():
            spread(block - 2)

        return carry

    lax.fori_loop(0, chunks + 2, turn, 0)
    for slot in range(2):
        for copy in stores(chunks - 1, spans - 2 + slot, slot):
            copy.wait()
    for block in range(chunks - 2, chunks):
        for y in range(y_size):
            copy_one(block, y).wait_send()
        for step in range(1, y_size):
            copy_two(block, step).wait_send()

    def drain(block, carry):
        for step in range(1, y_size):
            copy_three(block, step).wait_send()
        for y in range(y_size):
            copy_four(block, y).wait_send()
            copy_four(block, y).wait_recv()
        return carry

    lax.fori_loop(0, chunks, drain, 0)


def forward(lat_size, inputs, enc_low, dec_cols, enc_bias_row, mask_lanes, dec_bias_row, scale_row):
    tokens, depth = inputs.shape
    latents = enc_low.shape[1]
    chunk, span, width = 512, 1024, (512 if tokens <= 4096 else 256)
    chunks = tokens // chunk
    y_size = lat_size // CORES
    share = chunk // lat_size
    dma = pltpu.SemaphoreType.DMA
    vmem = pl.BlockSpec(memory_space=pltpu.VMEM)
    hbm = pl.BlockSpec(memory_space=pl.ANY)
    return pl.pallas_call(
        functools.partial(forward_kernel, lat_size),
        out_shape=[
            jax.ShapeDtypeStruct((latents // width, tokens, width), bf16),
            jax.ShapeDtypeStruct((latents // width, tokens, width), f32),
            jax.ShapeDtypeStruct((8, latents), f32),
            jax.ShapeDtypeStruct((tokens, depth), bf16),
            jax.ShapeDtypeStruct((16, depth), f32),
        ],
        in_specs=[vmem] * 7,
        out_specs=[hbm, hbm, vmem, vmem, vmem],
        scratch_shapes=[
            pltpu.VMEM((2, chunk, span), bf16),
            pltpu.VMEM((2, chunk, span), f32),
            pltpu.VMEM((2, chunk, span), f32),
            pltpu.VMEM((2, chunk, depth), f32),
            pltpu.VMEM((2, share, depth), f32),
            pltpu.VMEM((2, y_size - 1, share, depth), f32),
            pltpu.VMEM((chunks, y_size, share, depth), f32),
            pltpu.VMEM((chunks, y_size - 1, share, depth), f32),
            dma((2, span // width)), dma((2, span // width)),
            dma((2, y_size)), dma((chunks, y_size)),
            dma((2, y_size - 1)), dma((chunks, y_size - 1)),
            dma((chunks, y_size - 1)), dma((chunks, y_size - 1)),
            dma((chunks, y_size)), dma((chunks, y_size)),
        ],
        compiler_params=pltpu.CompilerParams(
            collective_id=1, has_side_effects=True, vmem_limit_bytes=60 * 2**20),
        name="forward",
    )(inputs, enc_low, dec_cols, enc_bias_row, mask_lanes, dec_bias_row, scale_row)


def encode(value):
    top = jnp.max(jnp.abs(value), axis=0, keepdims=True)
    unit = jnp.where(top > 0.0, 32766.0 / top, 0.0)
    shifted = value * unit + 12582912.0
    return (shifted - 12582912.0).astype(jnp.int32).astype(jnp.int16), top * (1.0 / 32766.0)


def decode(code, unit):
    return code.astype(jnp.int32).astype(f32) * unit


def put_units(ref, index, unit):
    for piece in range(unit.shape[1] // 128):
        ref[index + (pl.ds(piece, 1), slice(None))] = unit[:, piece * 128 : piece * 128 + 128]


def get_units(ref, index, width):
    return jnp.concatenate(
        [ref[index + (pl.ds(piece, 1), slice(None))] for piece in range(width // 128)], axis=1)


def backward_kernel(
    rows_size, lat_size,
    inputs_ref, back_ref, dec_ref, lasso_ref, norms_ref, pull_ref, mass_ref, stats_ref, master_ref,
    active_hbm, slope_hbm,
    enc_out, dec_out, bias_out, center_out, totals_out,
    grad_low, active_buf, slope_buf, sums,
    send_one, units_one, recv_one, got_one,
    send_two, units_two, recv_two, got_two,
    bias_rows, pull_cols, facts, tiles,
    active_sem, slope_sem,
    out_one, in_one, outu_one, inu_one, out_two, in_two, outu_two, inu_two, out_facts, in_facts, out_tiles, in_tiles,
):
    blocks, tokens, width = active_hbm.shape
    chunk = slope_buf.shape[1]
    chunks = tokens // chunk
    shard = enc_out.shape[0]
    x_size = rows_size // Z_CHIPS
    row = lax.axis_index("rows")
    lat = lax.axis_index("lat")
    my_z, my_x = row // x_size, lax.rem(row, x_size)

    def x_peer(step):
        return lax.rem(my_x + step, x_size)

    def z_peer(step):
        return lax.rem(my_z + step, Z_CHIPS)

    def active_copy(block):
        slot = lax.rem(block, 2)
        return pltpu.make_async_copy(active_hbm.at[block], active_buf.at[slot], active_sem.at[slot])

    def slope_copy(index):
        slot = lax.rem(index, slope_buf.shape[0])
        return pltpu.make_async_copy(
            slope_hbm.at[index // chunks, pl.ds(pl.multiple_of(lax.rem(index, chunks) * chunk, chunk), chunk)],
            slope_buf.at[slot],
            slope_sem.at[slot],
        )

    def copies(stage, block, which, step):
        slot = lax.rem(block, 2)
        if stage == 0:
            target = (my_z * x_size + x_peer(step), lat)
            refs = (send_one, recv_one, out_one, in_one, units_one, got_one, outu_one, inu_one)
        else:
            target = (z_peer(step) * x_size + my_x, lat)
            refs = (send_two, recv_two, out_two, in_two, units_two, got_two, outu_two, inu_two)
        return [
            pltpu.make_async_remote_copy(
                src_ref=refs[at].at[slot, which, step - 1], dst_ref=refs[at + 1].at[block, which, step - 1],
                send_sem=refs[at + 2].at[slot, which, step - 1], recv_sem=refs[at + 3].at[block, which, step - 1],
                device_id=target, device_id_type=MESH)
            for at in (0, 4)
        ]

    devices = rows_size * lat_size
    me = row * lat_size + lat
    latents = dec_ref.shape[1]
    depth = inputs_ref.shape[1]
    part = latents // 8

    def fact_copy(kind, step):
        area = facts.at[kind, row]
        return pltpu.make_async_remote_copy(
            src_ref=area, dst_ref=area, send_sem=out_facts.at[kind, step], recv_sem=in_facts.at[kind, row],
            device_id=(lax.rem(row + step, rows_size), lat), device_id_type=MESH)

    def fact_arrival(kind, step):
        source = lax.rem(row + step, rows_size)
        area = facts.at[kind, source]
        return pltpu.make_async_remote_copy(
            src_ref=area, dst_ref=area, send_sem=out_facts.at[kind, step], recv_sem=in_facts.at[kind, source],
            device_id=(source, lat), device_id_type=MESH)

    def tile_copy(kind, step):
        area = tiles.at[kind, me]
        target = lax.rem(me + step, devices)
        return pltpu.make_async_remote_copy(
            src_ref=area, dst_ref=area, send_sem=out_tiles.at[kind, step], recv_sem=in_tiles.at[kind, me],
            device_id=(target // lat_size, lax.rem(target, lat_size)), device_id_type=MESH)

    def tile_arrival(kind, step):
        source = lax.rem(me + step, devices)
        area = tiles.at[kind, source]
        return pltpu.make_async_remote_copy(
            src_ref=area, dst_ref=area, send_sem=out_tiles.at[kind, step], recv_sem=in_tiles.at[kind, source],
            device_id=(source // lat_size, lax.rem(source, lat_size)), device_id_type=MESH)

    def over_devices(action):
        def turn(step, carry):
            action(step)
            return carry

        lax.fori_loop(1, devices, turn, 0)

    def share_row(kind, value):
        for at in range(8):
            facts[kind, row, pl.ds(at, 1), :] = value[:, at * part : (at + 1) * part]
        for step in range(1, rows_size):
            fact_copy(kind, step).start()

    def shared_row(kind):
        for step in range(1, rows_size):
            fact_arrival(kind, step).wait_recv()
        total = facts[kind, 0]
        for source in range(1, rows_size):
            total = total + facts[kind, source]
        return jnp.concatenate([total[at : at + 1, :] for at in range(8)], axis=1)

    def share_tile(kind, value):
        tiles[kind, me] = value

        def start(step):
            tile_copy(kind, step).start()

        over_devices(start)

    def shared_tile(kind):
        def wait(step):
            tile_arrival(kind, step).wait_recv()

        over_devices(wait)
        return lax.fori_loop(1, devices, lambda source, total: total + tiles[kind, source], tiles[kind, 0])

    barrier = pltpu.get_barrier_semaphore()

    def greet(step):
        target = lax.rem(me + step, devices)
        pl.semaphore_signal(
            barrier, inc=1, device_id=(target // lat_size, lax.rem(target, lat_size)), device_id_type=MESH)

    over_devices(greet)
    active_copy(0).start()
    ahead = slope_buf.shape[0] - 1
    for index in range(ahead):
        slope_copy(index).start()
    pl.semaphore_wait(barrier, devices - 1)
    share_row(0, jnp.sum(mass_ref[...], axis=0, keepdims=True))
    center = jnp.sum(stats_ref[8:16, :], axis=0, keepdims=True)
    square = jnp.sum(stats_ref[0:8, :], keepdims=True)
    quarter = depth // 4
    share_tile(0, jnp.concatenate(
        [center[:, at * quarter : (at + 1) * quarter] for at in range(4)]
        + [jnp.broadcast_to(square, (4, quarter))], axis=0))

    def columns(block):
        return pl.ds(pl.multiple_of(block * width, width), width)

    over_tokens = (((0,), (0,)), ((), ()))

    def compute_dec(block):
        slot = lax.rem(block, 2)

        @pl.when(block + 1 < blocks)
        def _():
            active_copy(block + 1).start()

        active_copy(block).wait()
        sums[slot, 1] = lax.dot_general(back_ref[...], active_buf[slot], over_tokens, preferred_element_type=f32)

    def compute_enc(block):
        slot = lax.rem(block, 2)
        cols = columns(block)

        def piece(index, total):
            at = block * chunks + index

            @pl.when(at + ahead < blocks * chunks)
            def _():
                slope_copy(at + ahead).start()

            slope_copy(at).wait()
            rows = pl.ds(pl.multiple_of(index * chunk, chunk), chunk)
            back = jnp.dot(back_ref[rows, :], dec_ref[:, cols], preferred_element_type=f32)
            low = ((back + lasso_ref[:, cols]) * slope_buf[lax.rem(at, ahead + 1)]).astype(bf16)
            grad_low[rows, :] = low
            return total + low.astype(f32).reshape(chunk // 8, 8, width).sum(0)

        bias_rows[:, cols] = lax.fori_loop(0, chunks, piece, jnp.zeros((8, width), f32))
        sums[slot, 0] = lax.dot_general(inputs_ref[...], grad_low[...], over_tokens, preferred_element_type=f32)

    def send_x(block, which):
        slot = lax.rem(block, 2)
        for step in range(1, x_size):
            @pl.when(block >= 2)
            def _():
                for copy in copies(0, block - 2, which, step):
                    copy.wait_send()

            parts = []
            for z in range(Z_CHIPS):
                first = pl.multiple_of((z * x_size + x_peer(step)) * shard, shard)
                parts.append(sums[slot, which, pl.ds(first, shard), :])
            code, unit = encode(jnp.concatenate(parts, axis=0))
            for z in range(Z_CHIPS):
                send_one[slot, which, step - 1, z] = code[z * shard : (z + 1) * shard]
            put_units(units_one, (slot, which, step - 1), unit)
            for copy in copies(0, block, which, step):
                copy.start()

    def send_z(block, which):
        slot = lax.rem(block, 2)
        for step in range(1, x_size):
            for copy in copies(0, block, which, step):
                copy.wait_recv()
        for step in range(Z_CHIPS):
            z = z_peer(step)
            if step:
                @pl.when(block >= 2)
                def _():
                    for copy in copies(1, block - 2, which, step):
                        copy.wait_send()

            first = pl.multiple_of((z * x_size + my_x) * shard, shard)
            total = sums[slot, which, pl.ds(first, shard), :]
            for x_step in range(1, x_size):
                total = total + decode(
                    recv_one[block, which, x_step - 1, z], get_units(got_one, (block, which, x_step - 1), width))
            if step == 0:
                (enc_out, dec_out)[which][:, columns(block)] = total
            else:
                code, unit = encode(total)
                send_two[slot, which, step - 1] = code
                put_units(units_two, (slot, which, step - 1), unit)
                for copy in copies(1, block, which, step):
                    copy.start()

    def finish(block, which):
        slot = lax.rem(block, 2)
        for step in range(1, Z_CHIPS):
            for copy in copies(1, block, which, step):
                copy.wait_recv()
        out, cols = (enc_out, dec_out)[which], columns(block)
        total = out[:, cols]
        for step in range(1, Z_CHIPS):
            total = total + decode(
                recv_two[block, which, step - 1], get_units(got_two, (block, which, step - 1), width))
        out[:, cols] = total

    def turn(block, carry):
        for which, compute in ((1, compute_dec), (0, compute_enc)):
            @pl.when(block < blocks)
            def _():
                compute(block)
                send_x(block, which)

            @pl.when((block >= 1) & (block <= blocks))
            def _():
                send_z(block - 1, which)

            @pl.when(block >= 2)
            def _():
                finish(block - 2, which)

        return carry

    lax.fori_loop(0, blocks, turn, 0)
    share_row(1, jnp.sum(bias_rows[...], axis=0, keepdims=True))
    lax.fori_loop(blocks, blocks + 2, turn, 0)

    mass = shared_row(0)
    bias = shared_row(1)
    bias_out[...] = bias
    pull = mass * pull_ref[...]

    def squares(block, total):
        cols = columns(block)
        gain = dec_out[:, cols] + pull_cols[:, cols] * master_ref[:, cols]
        dec_out[:, cols] = gain
        other = enc_out[:, cols]
        return total + gain * gain + other * other

    pull_cols[...] = pull
    total = jnp.sum(lax.fori_loop(0, blocks, squares, jnp.zeros((shard, width), f32)), keepdims=True)
    leads = jnp.where(row == 0, 1.0, 0.0)
    total = total + leads * jnp.sum(bias * bias, keepdims=True)
    lasso = leads * lasso_coef * jnp.sum(mass * norms_ref[...], keepdims=True)
    share_tile(1, jnp.concatenate(
        [jnp.broadcast_to(total, (4, quarter)), jnp.broadcast_to(lasso, (4, quarter))], axis=0))
    first = shared_tile(0)
    center = jnp.concatenate([first[at : at + 1, :] for at in range(4)], axis=1)
    center_out[...] = center
    second = shared_tile(1)
    squared = second[0:4, :] + jnp.sum(center * center, keepdims=True)
    totals_out[...] = jnp.concatenate([squared, first[4:8, :] + second[4:8, :]], axis=0)
    for kind in range(2):
        for step in range(1, rows_size):
            fact_copy(kind, step).wait_send()

        def sent(step, kind=kind):
            tile_copy(kind, step).wait_send()

        over_devices(sent)
    for block in range(max(blocks - 2, 0), blocks):
        for which in range(2):
            for stage, size in ((0, x_size), (1, Z_CHIPS)):
                for step in range(1, size):
                    for copy in copies(stage, block, which, step):
                        copy.wait_send()


def backward(rows_size, lat_size, inputs, back, dec_cols, lasso_row, norms_row, pull_row, mass_rows, stats, master,
             active, slope):
    blocks, tokens, width = active.shape
    depth = inputs.shape[1]
    shard = depth // rows_size
    latents = dec_cols.shape[1]
    x_size = rows_size // Z_CHIPS
    devices = rows_size * lat_size
    chunk = min(CHUNK, tokens)
    i16 = jnp.int16
    dma = pltpu.SemaphoreType.DMA
    vmem = pl.BlockSpec(memory_space=pltpu.VMEM)
    hbm = pl.BlockSpec(memory_space=pl.ANY)
    return pl.pallas_call(
        functools.partial(backward_kernel, rows_size, lat_size),
        out_shape=[
            jax.ShapeDtypeStruct((shard, latents), f32),
            jax.ShapeDtypeStruct((shard, latents), f32),
            jax.ShapeDtypeStruct((1, latents), f32),
            jax.ShapeDtypeStruct((1, depth), f32),
            jax.ShapeDtypeStruct((8, 128), f32),
        ],
        in_specs=[vmem] * 9 + [hbm] * 2,
        out_specs=[vmem] * 5,
        scratch_shapes=[
            pltpu.VMEM((tokens, width), bf16),
            pltpu.VMEM((2, tokens, width), bf16),
            pltpu.VMEM((SLOTS, chunk, width), f32),
            pltpu.VMEM((2, 2, depth, width), f32),
            pltpu.VMEM((2, 2, x_size - 1, Z_CHIPS, shard, width), i16),
            pltpu.VMEM((2, 2, x_size - 1, 8, 128), f32),
            pltpu.VMEM((blocks, 2, x_size - 1, Z_CHIPS, shard, width), i16),
            pltpu.VMEM((blocks, 2, x_size - 1, 8, 128), f32),
            pltpu.VMEM((2, 2, Z_CHIPS - 1, shard, width), i16),
            pltpu.VMEM((2, 2, Z_CHIPS - 1, 8, 128), f32),
            pltpu.VMEM((blocks, 2, Z_CHIPS - 1, shard, width), i16),
            pltpu.VMEM((blocks, 2, Z_CHIPS - 1, 8, 128), f32),
            pltpu.VMEM((8, latents), f32),
            pltpu.VMEM((1, latents), f32),
            pltpu.VMEM((2, rows_size, 8, latents // 8), f32),
            pltpu.VMEM((2, devices, 8, 128), f32),
            dma((2,)), dma((SLOTS,)),
            dma((2, 2, x_size - 1)), dma((blocks, 2, x_size - 1)),
            dma((2, 2, x_size - 1)), dma((blocks, 2, x_size - 1)),
            dma((2, 2, Z_CHIPS - 1)), dma((blocks, 2, Z_CHIPS - 1)),
            dma((2, 2, Z_CHIPS - 1)), dma((blocks, 2, Z_CHIPS - 1)),
            dma((2, rows_size)), dma((2, rows_size)), dma((2, devices)), dma((2, devices)),
        ],
        compiler_params=pltpu.CompilerParams(
            collective_id=2, has_side_effects=True, vmem_limit_bytes=61 * 2**20),
        name="backward",
    )(inputs, back, dec_cols, lasso_row, norms_row, pull_row, mass_rows, stats, master, active, slope)


def body(
    token_ids,
    token_mask,
    scale_index,
    embed,
    norm_params,
    frozen_bias,
    w_joined,
    w_attn_out,
    w_mlp_in,
    w_mlp_out,
    enc_weight,
    enc_moment,
    enc_second,
    dec_weight,
    dec_moment,
    dec_second,
    enc_bias,
    enc_bias_moment,
    enc_bias_second,
    dec_bias,
    dec_bias_moment,
    dec_bias_second,
):
    lat_size = lax.axis_size("lat")
    lat_index = lax.axis_index("lat")
    group_tokens = token_ids.shape[0]
    tok_local = group_tokens // lat_size
    rows_size = lax.axis_size("rows")
    depth = enc_weight.shape[0] * rows_size
    mask_float = token_mask.astype(f32)
    dec_master = dec_weight.T
    bias_row = frozen_bias[None, :]
    vocab_local = embed.shape[0]
    vocab_first = lat_index * vocab_local
    local_ids = token_ids - vocab_first
    inside = ((local_ids >= 0) & (local_ids < vocab_local)).astype(f32)
    picked = jnp.take(embed, jnp.clip(local_ids, 0, vocab_local - 1), axis=0).astype(f32)
    picked = (picked * inside[:, None]).astype(bf16)
    own_first = lat_index * tok_local
    scales = 0.5 + 0.25 * lax.dynamic_slice_in_dim(scale_index, own_first, tok_local).astype(f32)
    level_lanes = jnp.broadcast_to(scales[:, None], (tok_local, 128))
    all_inputs, enc_low, dec_cols, norms_row, counts = front(
        rows_size, lat_size, picked, norm_params, bias_row, w_joined, w_attn_out, w_mlp_in, w_mlp_out,
        turn_tables(tok_local), level_lanes, mask_float.reshape(-1, 128), enc_weight, dec_master)
    count = counts[0, 0]
    mask_lanes = jnp.broadcast_to(mask_float[:, None], (group_tokens, 128))
    scale_row = jnp.full((1, depth), 2.0 / count, f32)
    lasso_scale = lasso_coef / count
    active, slope, mass_rows, recon_grad, stats = forward(
        lat_size, all_inputs, enc_low, dec_cols, enc_bias[None, :], mask_lanes, dec_bias[None, :], scale_row)
    grad_enc, grad_dec, bias_total, center, totals = backward(
        rows_size, lat_size, all_inputs, recon_grad, dec_cols, lasso_scale * norms_row, norms_row,
        lasso_scale / norms_row, mass_rows, stats, dec_master, active, slope)
    grad_enc_bias, grad_dec_bias = bias_total[0], center[0]
    grad_norm = jnp.sqrt(totals[0, 0])
    loss_sum = totals[4, 0]
    factor = clip_bound / jnp.maximum(grad_norm, clip_bound)
    enc_new = adam_update(enc_weight, enc_moment, enc_second, grad_enc * factor, weight_decay)
    dec_new = adam_update(dec_weight, dec_moment, dec_second, grad_dec.T * factor, weight_decay)
    enc_bias_new = adam_update(
        enc_bias, enc_bias_moment, enc_bias_second, grad_enc_bias * factor, 0.0
    )
    dec_bias_new = adam_update(
        dec_bias, dec_bias_moment, dec_bias_second, grad_dec_bias * factor, 0.0
    )
    return (
        enc_new[0],
        enc_new[1],
        enc_new[2],
        dec_new[0],
        dec_new[1],
        dec_new[2],
        enc_bias_new[0],
        enc_bias_new[1],
        enc_bias_new[2],
        dec_bias_new[0],
        dec_bias_new[1],
        dec_bias_new[2],
        grad_norm,
        loss_sum,
        count,
    )


def solution(mesh):
    placed = (
        P("rows"),
        P("rows"),
        P("rows"),
        P("lat", None),
        P(),
        P(),
        P(),
        P(),
        P(),
        P(),
        P("rows", "lat"),
        P("rows", "lat"),
        P("rows", "lat"),
        P("lat", "rows"),
        P("lat", "rows"),
        P("lat", "rows"),
        P("lat"),
        P("lat"),
        P("lat"),
        P(),
        P(),
        P(),
    )
    return jax.shard_map(
        body,
        mesh=mesh,
        in_specs=placed,
        out_specs=(
            P("rows", "lat"),
            P("rows", "lat"),
            P("rows", "lat"),
            P("lat", "rows"),
            P("lat", "rows"),
            P("lat", "rows"),
            P("lat"),
            P("lat"),
            P("lat"),
            P(),
            P(),
            P(),
            P(),
            P(),
            P(),
        ),
        check_vma=False,
    )
```

```python
import functools
import jax
import jax.numpy as jnp
from jax import lax
from jax.experimental import pallas as pl
from jax.experimental.pallas import tpu as pltpu
from jax.sharding import PartitionSpec as P

HEADS = 8
ROT = 16
STEP = 10
Z_CHIPS = 4
CORES = 2
SLOTS = 6
CHUNK = 1024
MESH = pl.DeviceIdType.MESH
f32 = jnp.float32
bf16 = jnp.bfloat16


lasso_coef = 5.0
clip_bound = 1.0
learn_rate = 0.03
beta_one = 0.9
beta_two = 0.999
adam_eps = 1e-08
weight_decay = 0.01


def adam_update(weight, moment, second, grad, decay):
    moment_new = beta_one * moment + (1.0 - beta_one) * grad
    second_new = beta_two * second + (1.0 - beta_two) * grad * grad
    corrected = moment_new / (1.0 - beta_one**STEP)
    scaled = jnp.sqrt(second_new / (1.0 - beta_two**STEP)) + adam_eps
    weight_new = weight - learn_rate * (corrected / scaled + decay * weight)
    return (weight_new, moment_new, second_new)


ROWS = 512
PIECE = 256
HEAD = 64
PAIR = 128


def front_kernel(
    rows_size, lat_size,
    picked_ref, norm_ref, bias_ref, joined_ref, attn_ref, mlp_in_ref, mlp_out_ref,
    turn_ref, level_ref, mask_ref, dec_ref, own_ref, left_ref, right_ref, across_ref,
    inputs_out, enc_out, dec_out, norms_out, lasso_out, pull_out, scale_out,
    from_core, from_y, base, queries, keys, values, context, ready, facts, got_facts,
    place_sem,
    out_right, in_left, out_left, in_right, out_x, in_x, out_fact, in_fact,
    out_core, in_core, out_y, in_y, out_own, in_own, out_near, in_near,
):
    tokens, depth = base.shape
    shard, latents = dec_ref.shape
    hidden = mlp_in_ref.shape[1]
    x_size = rows_size // Z_CHIPS
    y_size = lat_size // CORES
    pieces = tokens // PIECE
    row = lax.axis_index("rows")
    lat = lax.axis_index("lat")
    my_z, my_x = row // x_size, lax.rem(row, x_size)
    my_y, core = lat // CORES, lax.rem(lat, CORES)
    other = 1 - core

    def remote(src, dst, send, recv, to_row, to_lat):
        return pltpu.make_async_remote_copy(
            src_ref=src, dst_ref=dst, send_sem=send, recv_sem=recv,
            device_id=(to_row, to_lat), device_id_type=MESH)

    def peer_row(step):
        return lax.rem(row + step, rows_size)

    def x_row(step):
        return my_z * x_size + lax.rem(my_x + step, x_size)

    def y_peer(step):
        return lax.rem(my_y + step, y_size)

    barrier = pltpu.get_barrier_semaphore()
    for step in range(1, rows_size):
        pl.semaphore_signal(barrier, inc=1, device_id=(peer_row(step), lat), device_id_type=MESH)
    for step in range(1, y_size):
        pl.semaphore_signal(barrier, inc=1, device_id=(row, y_peer(step) * CORES + core), device_id_type=MESH)
    pl.semaphore_signal(barrier, inc=1, device_id=(row, my_y * CORES + other), device_id_type=MESH)

    square = jnp.sum(dec_ref[...] * dec_ref[...], axis=0, keepdims=True)
    part = latents // 8
    for at in range(8):
        facts[pl.ds(at, 1), :] = square[:, at * part : (at + 1) * part]
    facts[8:16, :] = jnp.broadcast_to(jnp.sum(mask_ref[...], keepdims=True), (8, part))
    pl.semaphore_wait(barrier, rows_size + y_size - 1)

    weights = (enc_out, dec_out)

    def weight_rows(z):
        return pl.ds(pl.multiple_of((z * x_size + my_x) * shard, shard), shard)

    def right_copy(hop, which, received=False):
        area = weights[which].at[weight_rows(jnp.maximum(my_z - hop - (1 if received else 0), 0))]
        source = left_ref.at[which] if hop == 1 and not received else area
        return remote(source, area, out_right.at[hop, which], in_left.at[hop, which],
                      jnp.minimum(my_z + 1, Z_CHIPS - 1) * x_size + my_x, lat)

    def left_copy(hop, which, received=False):
        area = weights[which].at[weight_rows(jnp.minimum(my_z + hop + (1 if received else 0), Z_CHIPS - 1))]
        source = right_ref.at[which] if hop == 1 and not received else area
        return remote(source, area, out_left.at[hop, which], in_right.at[hop, which],
                      jnp.maximum(my_z - 1, 0) * x_size + my_x, lat)

    def x_copy(z, which, step, source=None):
        area = weights[which].at[weight_rows(z)]
        return remote(area if source is None else source.at[which], area,
                      out_x.at[z, which, step - 1], in_x.at[z, which, step - 1], x_row(step), lat)

    def place(index, which):
        sources = [(own_ref, row), (left_ref, row - x_size), (right_ref, row + x_size)]
        sources += [(across_ref.at[step - 1], x_row(step)) for step in range(1, x_size)]
        source, owner = sources[index]
        owner = jnp.clip(owner, 0, rows_size - 1)
        return pltpu.make_async_copy(
            source.at[which], weights[which].at[pl.ds(pl.multiple_of(owner * shard, shard), shard)],
            place_sem.at[index, which])

    def place_all(action):
        for which in range(2):
            for index in range(x_size + 2):
                if index == 1:
                    @pl.when(my_z > 0)
                    def _():
                        action(place(1, which))
                elif index == 2:
                    @pl.when(my_z < Z_CHIPS - 1)
                    def _():
                        action(place(2, which))
                else:
                    action(place(index, which))

    def pass_on(hop, which):
        @pl.when(my_z >= hop)
        def _():
            if hop > 1:
                right_copy(hop - 1, which, True).wait_recv()
            if hop < Z_CHIPS - 1:
                @pl.when(my_z < Z_CHIPS - 1)
                def _():
                    right_copy(hop, which).start()
            for step in range(1, x_size):
                x_copy(my_z - hop, which, step, left_ref if hop == 1 else None).start()

        @pl.when(my_z + hop <= Z_CHIPS - 1)
        def _():
            if hop > 1:
                left_copy(hop - 1, which, True).wait_recv()
            if hop < Z_CHIPS - 1:
                @pl.when(my_z > 0)
                def _():
                    left_copy(hop, which).start()
            for step in range(1, x_size):
                x_copy(my_z + hop, which, step, right_ref if hop == 1 else None).start()

    def fact_copy(step):
        return remote(facts, got_facts.at[step - 1], out_fact.at[step - 1], in_fact.at[step - 1], peer_row(step), lat)

    def block_rows(y, which_core, piece):
        return pl.ds(pl.multiple_of((y * CORES + which_core) * tokens + piece * PIECE, PIECE), PIECE)

    def core_copy(step, piece):
        return remote(
            picked_ref.at[block_rows(y_peer(step), other, piece)], from_core.at[step, pl.ds(piece * PIECE, PIECE)],
            out_core.at[step, piece], in_core.at[step, piece], row, my_y * CORES + other)

    def y_copy(step, piece):
        here = pl.ds(piece * PIECE, PIECE)
        return remote(
            from_core.at[step, here], from_y.at[step - 1, here],
            out_y.at[step - 1, piece], in_y.at[step - 1, piece], row, y_peer(step) * CORES + core)

    for piece in range(pieces):
        for step in list(range(1, y_size)) + [0]:
            core_copy(step, piece).start()
    for piece in range(pieces):
        here = pl.ds(piece * PIECE, PIECE)
        for step in list(range(1, y_size)) + [0]:
            core_copy(step, piece).wait_recv()
            total = picked_ref[block_rows(y_peer(step), core, piece), :].astype(f32) + from_core[step, here, :].astype(f32)
            if step == 0:
                base[here, :] = total
            else:
                from_core[step, here, :] = total.astype(bf16)
                y_copy(step, piece).start()

    pass_on(1, 0)
    for step in range(1, rows_size):
        fact_copy(step).start()
    place_all(lambda copy: copy.start())
    pass_on(1, 1)
    pass_on(2, 0)

    def normed(value, gain, shift):
        centred = value - jnp.mean(value, axis=1, keepdims=True)
        spread = jnp.mean(centred * centred, axis=1, keepdims=True)
        return (centred * lax.rsqrt(spread + 1e-05) * gain + shift).astype(bf16)

    def dot(left, right):
        return jnp.dot(left, right, preferred_element_type=f32)

    def rotated(value, rows):
        cosine, low, high = turn_ref[0, rows, :], turn_ref[1, rows, :], turn_ref[2, rows, :]
        parts = []
        for at in range(depth // PAIR):
            tile = value[:, at * PAIR : (at + 1) * PAIR]
            parts.append(
                tile * cosine + pltpu.roll(tile, PAIR - ROT // 2, 1) * low + pltpu.roll(tile, ROT // 2, 1) * high)
        return jnp.concatenate(parts, axis=1)

    for block in range(tokens // ROWS):
        rows = pl.ds(block * ROWS, ROWS)
        for piece in range(block * ROWS // PIECE, (block + 1) * ROWS // PIECE):
            for step in range(1, y_size):
                y_copy(step, piece).wait_recv()
        embedded = base[rows, :]
        for step in range(1, y_size):
            embedded = embedded + from_y[step - 1, rows, :].astype(f32)
        attn_in = normed(embedded, norm_ref[0:1, :], norm_ref[1:2, :])
        joined = dot(attn_in, joined_ref[...]) + bias_ref[:, : 3 * depth]
        queries[rows, :] = (rotated(joined[:, :depth], rows).astype(bf16) * HEAD**-0.5).astype(bf16)
        keys[rows, :] = rotated(joined[:, depth : 2 * depth], rows).astype(bf16)
        values[rows, :] = joined[:, 2 * depth :].astype(bf16)
        mlp_in = normed(embedded, norm_ref[2:3, :], norm_ref[3:4, :])
        inner = dot(mlp_in, mlp_in_ref[...]) + bias_ref[:, 4 * depth : 4 * depth + hidden]
        inner = (0.5 * inner * (1.0 + lax.erf(inner * 0.5**0.5))).astype(bf16)
        base[rows, :] = embedded + (dot(inner, mlp_out_ref[...]) + bias_ref[:, 4 * depth + hidden :])
        if block == 0:
            pass_on(2, 1)
    pass_on(3, 0)

    def own_rows(y, which_core, piece):
        return pl.ds(pl.multiple_of((y * CORES + which_core) * tokens + piece * PIECE, PIECE), PIECE)

    def own_copy(step, piece):
        area = inputs_out.at[own_rows(my_y, core, piece)]
        return remote(ready.at[pl.ds(piece * PIECE, PIECE)], area, out_own.at[step - 1, piece], in_own.at[step - 1, piece], row, y_peer(step) * CORES + core)

    def near_copy(step, piece):
        area = inputs_out.at[own_rows(y_peer(step), core, piece)]
        source = area if step else ready.at[pl.ds(piece * PIECE, PIECE)]
        return remote(source, area, out_near.at[step, piece], in_near.at[step, piece], row, my_y * CORES + other)

    def keep_copy(piece):
        return pltpu.make_async_copy(
            ready.at[pl.ds(piece * PIECE, PIECE)], inputs_out.at[own_rows(my_y, core, piece)], place_sem.at[x_size + 2, piece])

    lanes = lax.broadcasted_iota(jnp.int32, (PIECE, PAIR), 1)
    for piece in range(pieces):
        here = pl.ds(piece * PIECE, PIECE)
        reach = (piece + 1) * PIECE
        visible = (
            lax.broadcasted_iota(jnp.int32, (PIECE, reach), 0) + piece * PIECE
            >= lax.broadcasted_iota(jnp.int32, (PIECE, reach), 1)
        )

        def attend(pair, carry):
            cols = pl.ds(pl.multiple_of(pair * PAIR, PAIR), PAIR)
            both = queries[here, cols]
            found = []
            for first in (True, False):
                chosen = jnp.where((lanes < HEAD) == first, both, jnp.zeros_like(both))
                scores = lax.dot_general(
                    chosen, keys[0:reach, cols], (((1,), (1,)), ((), ())), preferred_element_type=f32)
                scores = jnp.where(visible, scores, -1e30)
                powers = jnp.exp(scores - jnp.max(scores, axis=1, keepdims=True))
                probs = (powers * (1.0 / jnp.sum(powers, axis=1, keepdims=True))).astype(bf16)
                found.append(dot(probs, values[0:reach, cols]))
            context[here, cols] = jnp.where(lanes < HEAD, found[0], found[1]).astype(bf16)
            return carry

        lax.fori_loop(0, depth // PAIR, attend, 0)
        attended = dot(context[here, :], attn_ref[...]) + bias_ref[:, 3 * depth : 4 * depth]
        level = jnp.concatenate([level_ref[here, :]] * (depth // 128), axis=1)
        ready[here, :] = ((base[here, :] + attended) * level).astype(bf16)
        keep_copy(piece).start()
        for step in range(1, y_size):
            own_copy(step, piece).start()
        near_copy(0, piece).start()
        if piece == 1:
            pass_on(3, 1)
        if piece >= 2:
            for step in range(1, y_size):
                own_copy(step, piece - 2).wait_recv()
                near_copy(step, piece - 2).start()

    total = facts[...]
    for step in range(1, rows_size):
        fact_copy(step).wait_recv()
        total = total + got_facts[step - 1]
    count = total[8:9, 0:1]
    norms = jnp.sqrt(total[0:8, :])
    norms = jnp.concatenate([norms[at : at + 1, :] for at in range(8)], axis=1)
    lasso_scale = lasso_coef / count
    norms_out[...] = norms
    lasso_out[...] = lasso_scale * norms
    pull_out[...] = lasso_scale / norms
    scale_out[0:1, :] = jnp.broadcast_to(2.0 / count, (1, depth))
    scale_out[1:8, :] = jnp.broadcast_to(count, (7, depth))
    for piece in range(pieces - 2, pieces):
        for step in range(1, y_size):
            own_copy(step, piece).wait_recv()
            near_copy(step, piece).start()
    place_all(lambda copy: copy.wait())

    for which in range(2):
        for hop in range(1, Z_CHIPS - 1):
            @pl.when((my_z < Z_CHIPS - 1) & (my_z >= hop))
            def _():
                right_copy(hop, which).wait_send()

            @pl.when((my_z > 0) & (my_z + hop <= Z_CHIPS - 1))
            def _():
                left_copy(hop, which).wait_send()

        for z in range(Z_CHIPS):
            @pl.when(z != my_z)
            def _():
                for step in range(1, x_size):
                    x_copy(z, which, step).wait_send()
                    x_copy(z, which, step).wait_recv()
    for step in range(1, rows_size):
        fact_copy(step).wait_send()
    for piece in range(pieces):
        keep_copy(piece).wait()
        for step in range(y_size):
            core_copy(step, piece).wait_send()
            near_copy(step, piece).wait_send()
            near_copy(step, piece).wait_recv()
        for step in range(1, y_size):
            y_copy(step, piece).wait_send()
            own_copy(step, piece).wait_send()


def front(rows_size, lat_size, picked, norm_params, bias_row, w_joined, w_attn_out, w_mlp_in, w_mlp_out,
          turns, level_lanes, mask_tiles, dec_shard, own, left, right, across):
    group, depth = picked.shape
    tokens = group // lat_size
    shard, latents = dec_shard.shape
    x_size = rows_size // Z_CHIPS
    y_size = lat_size // CORES
    pieces = tokens // PIECE
    dma = pltpu.SemaphoreType.DMA
    vmem = pl.BlockSpec(memory_space=pltpu.VMEM)
    hbm = pl.BlockSpec(memory_space=pl.ANY)
    hops = Z_CHIPS - 1
    return pl.pallas_call(
        functools.partial(front_kernel, rows_size, lat_size),
        out_shape=[
            jax.ShapeDtypeStruct((group, depth), bf16),
            jax.ShapeDtypeStruct((depth, latents), bf16),
            jax.ShapeDtypeStruct((depth, latents), bf16),
            jax.ShapeDtypeStruct((1, latents), f32),
            jax.ShapeDtypeStruct((1, latents), f32),
            jax.ShapeDtypeStruct((1, latents), f32),
            jax.ShapeDtypeStruct((8, depth), f32),
        ],
        in_specs=[vmem] * 15,
        out_specs=[hbm] * 3 + [vmem] * 4,
        scratch_shapes=[
            pltpu.VMEM((y_size, tokens, depth), bf16),
            pltpu.VMEM((y_size - 1, tokens, depth), bf16),
            pltpu.VMEM((tokens, depth), f32),
            pltpu.VMEM((tokens, depth), bf16),
            pltpu.VMEM((tokens, depth), bf16),
            pltpu.VMEM((tokens, depth), bf16),
            pltpu.VMEM((tokens, depth), bf16),
            pltpu.VMEM((tokens, depth), bf16),
            pltpu.VMEM((16, latents // 8), f32),
            pltpu.VMEM((rows_size - 1, 16, latents // 8), f32),
            dma((x_size + 3, max(pieces, 2))),
            dma((hops, 2)), dma((hops, 2)), dma((hops, 2)), dma((hops, 2)),
            dma((Z_CHIPS, 2, x_size - 1)), dma((Z_CHIPS, 2, x_size - 1)),
            dma((rows_size - 1,)), dma((rows_size - 1,)),
            dma((y_size, pieces)), dma((y_size, pieces)),
            dma((y_size - 1, pieces)), dma((y_size - 1, pieces)),
            dma((y_size - 1, pieces)), dma((y_size - 1, pieces)),
            dma((y_size, pieces)), dma((y_size, pieces)),
        ],
        compiler_params=pltpu.CompilerParams(
            collective_id=3, has_side_effects=True, vmem_limit_bytes=60 * 2**20),
        name="front",
    )(picked, norm_params, bias_row, w_joined, w_attn_out, w_mlp_in, w_mlp_out,
      turns, level_lanes, mask_tiles, dec_shard, own, left, right, across)


def turn_tables(length):
    half = ROT // 2
    freqs = 10000.0 ** (-2.0 * jnp.arange(half, dtype=f32) / ROT)
    angles = jnp.arange(length, dtype=f32)[:, None] * jnp.tile(freqs, PAIR // half)[None, :]
    place = jnp.arange(PAIR) % HEAD
    cosines, sines = jnp.cos(angles), jnp.sin(angles)
    return jnp.stack([
        jnp.where(place < ROT, cosines, 1.0),
        jnp.where(place < half, -sines, 0.0),
        jnp.where((place >= half) & (place < ROT), sines, 0.0),
    ])


def softplus_parts(value):
    power = jnp.exp(value)
    grown = jnp.log(1.0 + power)
    grown = jnp.where(power < 2.0**-8, power * (1.0 - 0.5 * power), grown)
    active = jnp.where(value > 30.0, value, grown)
    return active, jnp.exp(value - active)


def forward_kernel(
    lat_size,
    inputs_ref, enc_ref, dec_ref, enc_bias_ref, mask_ref, dec_bias_ref, scale_ref,
    active_hbm, slope_hbm, mass_out, back_out, stats_out,
    active_buf, slope_buf, product, partial, own, send_two, recv_one, recv_two,
    active_sem, slope_sem, out_one, in_one, out_two, in_two, out_three, in_three, out_four, in_four,
):
    tokens, depth = inputs_ref.shape
    latents = enc_ref.shape[1]
    chunk, span = product.shape[1:]
    width = active_hbm.shape[2]
    chunks, spans = tokens // chunk, latents // span
    y_size = lat_size // CORES
    share = chunk // lat_size
    strip = 16
    row = lax.axis_index("rows")
    lat = lax.axis_index("lat")
    my_y, core = lat // CORES, lax.rem(lat, CORES)
    other = 1 - core

    def y_peer(step):
        return lax.rem(my_y + step, y_size)

    def share_rows(y, which_core):
        return pl.multiple_of((y * CORES + which_core) * share, share)

    def token_rows(block, y, which_core):
        return pl.ds(pl.multiple_of(block * chunk + (y * CORES + which_core) * share, share), share)

    def remote(src, dst, send, recv, target):
        return pltpu.make_async_remote_copy(
            src_ref=src, dst_ref=dst, send_sem=send, recv_sem=recv,
            device_id=(row, target), device_id_type=MESH)

    def copy_one(block, y):
        slot = lax.rem(block, 2)
        return remote(
            partial.at[slot, pl.ds(share_rows(y, other), share)], recv_one.at[block, y],
            out_one.at[slot, y], in_one.at[block, y], my_y * CORES + other)

    def copy_two(block, step):
        slot = lax.rem(block, 2)
        return remote(
            send_two.at[slot, step - 1], recv_two.at[block, step - 1],
            out_two.at[slot, step - 1], in_two.at[block, step - 1], y_peer(step) * CORES + core)

    def copy_three(block, step):
        mine = back_out.at[token_rows(block, my_y, core)]
        return remote(
            mine, mine, out_three.at[block, step - 1], in_three.at[block, step - 1], y_peer(step) * CORES + core)

    def copy_four(block, y):
        mine = back_out.at[token_rows(block, y, core)]
        return remote(mine, mine, out_four.at[block, y], in_four.at[block, y], my_y * CORES + other)

    def stores(block, at, slot):
        rows = pl.ds(pl.multiple_of(block * chunk, chunk), chunk)
        copies = []
        for part in range(span // width):
            lanes = pl.ds(part * width, width)
            copies.append(pltpu.make_async_copy(
                active_buf.at[slot, :, lanes], active_hbm.at[at * (span // width) + part, rows], active_sem.at[slot, part]))
            copies.append(pltpu.make_async_copy(
                slope_buf.at[slot, :, lanes], slope_hbm.at[at * (span // width) + part, rows], slope_sem.at[slot, part]))
        return copies

    barrier = pltpu.get_barrier_semaphore()
    pl.semaphore_signal(barrier, inc=1, device_id=(row, my_y * CORES + other), device_id_type=MESH)
    for step in range(1, y_size):
        pl.semaphore_signal(barrier, inc=1, device_id=(row, y_peer(step) * CORES + core), device_id_type=MESH)
    mass_out[...] = jnp.zeros_like(mass_out)
    stats_out[...] = jnp.zeros_like(stats_out)
    pl.semaphore_wait(barrier, y_size)

    def compute(block):
        place = lax.rem(block, 2)
        first = pl.multiple_of(block * chunk, chunk)

        @pl.when(block >= 2)
        def _():
            for y in range(y_size):
                copy_one(block - 2, y).wait_send()

        for at in range(spans):
            slot = at % 2
            if at >= 2:
                for copy in stores(block, at - 2, slot):
                    copy.wait()
            else:
                @pl.when(block > 0)
                def _():
                    for copy in stores(block - 1, spans - 2 + at, slot):
                        copy.wait()

            product[slot] = jnp.dot(
                inputs_ref[pl.ds(first, chunk), :], enc_ref[:, at * span : (at + 1) * span], preferred_element_type=f32)
            for left in range(0, span, width):
                lanes = pl.ds(left, width)
                cols = pl.ds(at * span + left, width)
                shift = enc_bias_ref[:, cols]
                total = mass_out[:, cols]
                for top in range(0, chunk, strip):
                    rows = pl.ds(top, strip)
                    mask = mask_ref[pl.ds(first + top, strip), :]
                    mask = jnp.concatenate([mask] * (width // 128), axis=1)
                    active, slope = softplus_parts(product[slot, rows, lanes] + shift)
                    active_buf[slot, rows, lanes] = active.astype(bf16)
                    slope_buf[slot, rows, lanes] = slope * mask
                    total = total + (active * mask).reshape(strip // 8, 8, width).sum(0)
                mass_out[:, cols] = total
            for copy in stores(block, at, slot):
                copy.start()
            part = lax.dot_general(
                active_buf[slot], dec_ref[:, at * span : (at + 1) * span], (((1,), (1,)), ((), ())),
                preferred_element_type=f32)
            partial[place] = part if at == 0 else partial[place] + part

    def exchange(block):
        slot = lax.rem(block, 2)
        for y in range(y_size):
            copy_one(block, y).start()
        for y in range(y_size):
            copy_one(block, y).wait_recv()
        for step in list(range(1, y_size)) + [0]:
            y = y_peer(step)
            total = partial[slot, pl.ds(share_rows(y, core), share), :] + recv_one[block, y]
            if step == 0:
                own[slot] = total
            else:
                @pl.when(block >= 2)
                def _():
                    copy_two(block - 2, step).wait_send()

                send_two[slot, step - 1] = total
                copy_two(block, step).start()

    def settle(block):
        slot = lax.rem(block, 2)
        rows = token_rows(block, my_y, core)
        total = own[slot]
        for step in range(1, y_size):
            copy_two(block, step).wait_recv()
            total = total + recv_two[block, step - 1]
        error = total + dec_bias_ref[...] - inputs_ref[rows, :].astype(f32)
        mask = jnp.concatenate([mask_ref[rows, :]] * (depth // 128), axis=1)
        low = (scale_ref[0:1, :] * mask * error).astype(bf16)
        back_out[rows, :] = low
        stats_out[0:8, :] += (mask * error * error).reshape(share // 8, 8, depth).sum(0)
        stats_out[8:16, :] += low.astype(f32).reshape(share // 8, 8, depth).sum(0)
        for step in range(1, y_size):
            copy_three(block, step).start()

    def spread(block):
        for step in range(1, y_size):
            copy_three(block, step).wait_recv()
        for y in range(y_size):
            copy_four(block, y).start()

    def turn(block, carry):
        @pl.when(block < chunks)
        def _():
            compute(block)
            exchange(block)

        @pl.when((block >= 1) & (block <= chunks))
        def _():
            settle(block - 1)

        @pl.when(block >= 2)
        def _():
            spread(block - 2)

        return carry

    lax.fori_loop(0, chunks + 2, turn, 0)
    for slot in range(2):
        for copy in stores(chunks - 1, spans - 2 + slot, slot):
            copy.wait()
    for block in range(chunks - 2, chunks):
        for y in range(y_size):
            copy_one(block, y).wait_send()
        for step in range(1, y_size):
            copy_two(block, step).wait_send()

    def drain(block, carry):
        for step in range(1, y_size):
            copy_three(block, step).wait_send()
        for y in range(y_size):
            copy_four(block, y).wait_send()
            copy_four(block, y).wait_recv()
        return carry

    lax.fori_loop(0, chunks, drain, 0)


def forward(lat_size, inputs, enc_low, dec_cols, enc_bias_row, mask_lanes, dec_bias_row, scale_rows):
    tokens, depth = inputs.shape
    latents = enc_low.shape[1]
    chunk, span, width = 512, 1024, (512 if tokens <= 4096 else 256)
    chunks = tokens // chunk
    y_size = lat_size // CORES
    share = chunk // lat_size
    dma = pltpu.SemaphoreType.DMA
    vmem = pl.BlockSpec(memory_space=pltpu.VMEM)
    hbm = pl.BlockSpec(memory_space=pl.ANY)
    return pl.pallas_call(
        functools.partial(forward_kernel, lat_size),
        out_shape=[
            jax.ShapeDtypeStruct((latents // width, tokens, width), bf16),
            jax.ShapeDtypeStruct((latents // width, tokens, width), f32),
            jax.ShapeDtypeStruct((8, latents), f32),
            jax.ShapeDtypeStruct((tokens, depth), bf16),
            jax.ShapeDtypeStruct((16, depth), f32),
        ],
        in_specs=[vmem] * 7,
        out_specs=[hbm, hbm, vmem, vmem, vmem],
        scratch_shapes=[
            pltpu.VMEM((2, chunk, span), bf16),
            pltpu.VMEM((2, chunk, span), f32),
            pltpu.VMEM((2, chunk, span), f32),
            pltpu.VMEM((2, chunk, depth), f32),
            pltpu.VMEM((2, share, depth), f32),
            pltpu.VMEM((2, y_size - 1, share, depth), f32),
            pltpu.VMEM((chunks, y_size, share, depth), f32),
            pltpu.VMEM((chunks, y_size - 1, share, depth), f32),
            dma((2, span // width)), dma((2, span // width)),
            dma((2, y_size)), dma((chunks, y_size)),
            dma((2, y_size - 1)), dma((chunks, y_size - 1)),
            dma((chunks, y_size - 1)), dma((chunks, y_size - 1)),
            dma((chunks, y_size)), dma((chunks, y_size)),
        ],
        compiler_params=pltpu.CompilerParams(
            collective_id=1, has_side_effects=True, vmem_limit_bytes=60 * 2**20),
        name="forward",
    )(inputs, enc_low, dec_cols, enc_bias_row, mask_lanes, dec_bias_row, scale_rows)


def encode(value):
    top = jnp.max(jnp.abs(value), axis=0, keepdims=True)
    unit = jnp.where(top > 0.0, 32766.0 / top, 0.0)
    shifted = value * unit + 12582912.0
    return (shifted - 12582912.0).astype(jnp.int32).astype(jnp.int16), top * (1.0 / 32766.0)


def decode(code, unit):
    return code.astype(jnp.int32).astype(f32) * unit


def put_units(ref, index, unit):
    for piece in range(unit.shape[1] // 128):
        ref[index + (pl.ds(piece, 1), slice(None))] = unit[:, piece * 128 : piece * 128 + 128]


def get_units(ref, index, width):
    return jnp.concatenate(
        [ref[index + (pl.ds(piece, 1), slice(None))] for piece in range(width // 128)], axis=1)


def backward_kernel(
    rows_size, lat_size,
    inputs_ref, back_ref, dec_ref, norms_ref, lasso_ref, pull_ref, mass_ref, stats_ref, master_ref,
    active_hbm, slope_hbm,
    enc_out, dec_out, bias_out, center_out, totals_out,
    grad_low, active_buf, slope_buf, sums,
    send_one, units_one, recv_one, got_one,
    send_two, units_two, recv_two, got_two,
    bias_rows, pull_cols, facts, tiles,
    active_sem, slope_sem,
    out_one, in_one, outu_one, inu_one, out_two, in_two, outu_two, inu_two, out_facts, in_facts, out_tiles, in_tiles,
):
    blocks, tokens, width = active_hbm.shape
    chunk = slope_buf.shape[1]
    chunks = tokens // chunk
    shard = enc_out.shape[0]
    x_size = rows_size // Z_CHIPS
    row = lax.axis_index("rows")
    lat = lax.axis_index("lat")
    my_z, my_x = row // x_size, lax.rem(row, x_size)

    def x_peer(step):
        return lax.rem(my_x + step, x_size)

    def z_peer(step):
        return lax.rem(my_z + step, Z_CHIPS)

    def active_copy(block):
        slot = lax.rem(block, 2)
        return pltpu.make_async_copy(active_hbm.at[block], active_buf.at[slot], active_sem.at[slot])

    def slope_copy(index):
        slot = lax.rem(index, slope_buf.shape[0])
        return pltpu.make_async_copy(
            slope_hbm.at[index // chunks, pl.ds(pl.multiple_of(lax.rem(index, chunks) * chunk, chunk), chunk)],
            slope_buf.at[slot],
            slope_sem.at[slot],
        )

    def copies(stage, block, which, step):
        slot = lax.rem(block, 2)
        if stage == 0:
            target = (my_z * x_size + x_peer(step), lat)
            refs = (send_one, recv_one, out_one, in_one, units_one, got_one, outu_one, inu_one)
        else:
            target = (z_peer(step) * x_size + my_x, lat)
            refs = (send_two, recv_two, out_two, in_two, units_two, got_two, outu_two, inu_two)
        return [
            pltpu.make_async_remote_copy(
                src_ref=refs[at].at[slot, which, step - 1], dst_ref=refs[at + 1].at[block, which, step - 1],
                send_sem=refs[at + 2].at[slot, which, step - 1], recv_sem=refs[at + 3].at[block, which, step - 1],
                device_id=target, device_id_type=MESH)
            for at in (0, 4)
        ]

    devices = rows_size * lat_size
    me = row * lat_size + lat
    latents = dec_ref.shape[1]
    depth = inputs_ref.shape[1]
    part = latents // 8

    def fact_copy(kind, step):
        area = facts.at[kind, row]
        return pltpu.make_async_remote_copy(
            src_ref=area, dst_ref=area, send_sem=out_facts.at[kind, step], recv_sem=in_facts.at[kind, row],
            device_id=(lax.rem(row + step, rows_size), lat), device_id_type=MESH)

    def fact_arrival(kind, step):
        source = lax.rem(row + step, rows_size)
        area = facts.at[kind, source]
        return pltpu.make_async_remote_copy(
            src_ref=area, dst_ref=area, send_sem=out_facts.at[kind, step], recv_sem=in_facts.at[kind, source],
            device_id=(source, lat), device_id_type=MESH)

    def tile_copy(kind, step):
        area = tiles.at[kind, me]
        target = lax.rem(me + step, devices)
        return pltpu.make_async_remote_copy(
            src_ref=area, dst_ref=area, send_sem=out_tiles.at[kind, step], recv_sem=in_tiles.at[kind, me],
            device_id=(target // lat_size, lax.rem(target, lat_size)), device_id_type=MESH)

    def tile_arrival(kind, step):
        source = lax.rem(me + step, devices)
        area = tiles.at[kind, source]
        return pltpu.make_async_remote_copy(
            src_ref=area, dst_ref=area, send_sem=out_tiles.at[kind, step], recv_sem=in_tiles.at[kind, source],
            device_id=(source // lat_size, lax.rem(source, lat_size)), device_id_type=MESH)

    def over_devices(action):
        def turn(step, carry):
            action(step)
            return carry

        lax.fori_loop(1, devices, turn, 0)

    def share_row(kind, value):
        for at in range(8):
            facts[kind, row, pl.ds(at, 1), :] = value[:, at * part : (at + 1) * part]
        for step in range(1, rows_size):
            fact_copy(kind, step).start()

    def shared_row(kind):
        for step in range(1, rows_size):
            fact_arrival(kind, step).wait_recv()
        total = facts[kind, 0]
        for source in range(1, rows_size):
            total = total + facts[kind, source]
        return jnp.concatenate([total[at : at + 1, :] for at in range(8)], axis=1)

    def share_tile(kind, value):
        tiles[kind, me] = value

        def start(step):
            tile_copy(kind, step).start()

        over_devices(start)

    def shared_tile(kind):
        def wait(step):
            tile_arrival(kind, step).wait_recv()

        over_devices(wait)
        return lax.fori_loop(1, devices, lambda source, total: total + tiles[kind, source], tiles[kind, 0])

    barrier = pltpu.get_barrier_semaphore()

    def greet(step):
        target = lax.rem(me + step, devices)
        pl.semaphore_signal(
            barrier, inc=1, device_id=(target // lat_size, lax.rem(target, lat_size)), device_id_type=MESH)

    over_devices(greet)
    active_copy(0).start()
    ahead = slope_buf.shape[0] - 1
    for index in range(ahead):
        slope_copy(index).start()
    pl.semaphore_wait(barrier, devices - 1)
    share_row(0, jnp.sum(mass_ref[...], axis=0, keepdims=True))
    center = jnp.sum(stats_ref[8:16, :], axis=0, keepdims=True)
    square = jnp.sum(stats_ref[0:8, :], keepdims=True)
    quarter = depth // 4
    share_tile(0, jnp.concatenate(
        [center[:, at * quarter : (at + 1) * quarter] for at in range(4)]
        + [jnp.broadcast_to(square, (4, quarter))], axis=0))

    def columns(block):
        return pl.ds(pl.multiple_of(block * width, width), width)

    over_tokens = (((0,), (0,)), ((), ()))

    def compute_dec(block):
        slot = lax.rem(block, 2)

        @pl.when(block + 1 < blocks)
        def _():
            active_copy(block + 1).start()

        active_copy(block).wait()
        sums[slot, 1] = lax.dot_general(back_ref[...], active_buf[slot], over_tokens, preferred_element_type=f32)

    def compute_enc(block):
        slot = lax.rem(block, 2)
        cols = columns(block)

        def piece(index, total):
            at = block * chunks + index

            @pl.when(at + ahead < blocks * chunks)
            def _():
                slope_copy(at + ahead).start()

            slope_copy(at).wait()
            rows = pl.ds(pl.multiple_of(index * chunk, chunk), chunk)
            back = jnp.dot(back_ref[rows, :], dec_ref[:, cols], preferred_element_type=f32)
            low = ((back + lasso_ref[:, cols]) * slope_buf[lax.rem(at, ahead + 1)]).astype(bf16)
            grad_low[rows, :] = low
            return total + low.astype(f32).reshape(chunk // 8, 8, width).sum(0)

        bias_rows[:, cols] = lax.fori_loop(0, chunks, piece, jnp.zeros((8, width), f32))
        sums[slot, 0] = lax.dot_general(inputs_ref[...], grad_low[...], over_tokens, preferred_element_type=f32)

    def send_x(block, which):
        slot = lax.rem(block, 2)
        for step in range(1, x_size):
            @pl.when(block >= 2)
            def _():
                for copy in copies(0, block - 2, which, step):
                    copy.wait_send()

            parts = []
            for z in range(Z_CHIPS):
                first = pl.multiple_of((z * x_size + x_peer(step)) * shard, shard)
                parts.append(sums[slot, which, pl.ds(first, shard), :])
            code, unit = encode(jnp.concatenate(parts, axis=0))
            for z in range(Z_CHIPS):
                send_one[slot, which, step - 1, z] = code[z * shard : (z + 1) * shard]
            put_units(units_one, (slot, which, step - 1), unit)
            for copy in copies(0, block, which, step):
                copy.start()

    def send_z(block, which):
        slot = lax.rem(block, 2)
        for step in range(1, x_size):
            for copy in copies(0, block, which, step):
                copy.wait_recv()
        for step in range(Z_CHIPS):
            z = z_peer(step)
            if step:
                @pl.when(block >= 2)
                def _():
                    for copy in copies(1, block - 2, which, step):
                        copy.wait_send()

            first = pl.multiple_of((z * x_size + my_x) * shard, shard)
            total = sums[slot, which, pl.ds(first, shard), :]
            for x_step in range(1, x_size):
                total = total + decode(
                    recv_one[block, which, x_step - 1, z], get_units(got_one, (block, which, x_step - 1), width))
            if step == 0:
                (enc_out, dec_out)[which][:, columns(block)] = total
            else:
                code, unit = encode(total)
                send_two[slot, which, step - 1] = code
                put_units(units_two, (slot, which, step - 1), unit)
                for copy in copies(1, block, which, step):
                    copy.start()

    def finish(block, which):
        slot = lax.rem(block, 2)
        for step in range(1, Z_CHIPS):
            for copy in copies(1, block, which, step):
                copy.wait_recv()
        out, cols = (enc_out, dec_out)[which], columns(block)
        total = out[:, cols]
        for step in range(1, Z_CHIPS):
            total = total + decode(
                recv_two[block, which, step - 1], get_units(got_two, (block, which, step - 1), width))
        out[:, cols] = total

    def turn(block, carry):
        for which, compute in ((1, compute_dec), (0, compute_enc)):
            @pl.when(block < blocks)
            def _():
                compute(block)
                send_x(block, which)

            @pl.when((block >= 1) & (block <= blocks))
            def _():
                send_z(block - 1, which)

            @pl.when(block >= 2)
            def _():
                finish(block - 2, which)

        return carry

    lax.fori_loop(0, blocks, turn, 0)
    share_row(1, jnp.sum(bias_rows[...], axis=0, keepdims=True))
    lax.fori_loop(blocks, blocks + 2, turn, 0)

    mass = shared_row(0)
    bias = shared_row(1)
    bias_out[...] = bias
    pull = mass * pull_ref[...]

    def squares(block, total):
        cols = columns(block)
        gain = dec_out[:, cols] + pull_cols[:, cols] * master_ref[:, cols]
        dec_out[:, cols] = gain
        other = enc_out[:, cols]
        return total + gain * gain + other * other

    pull_cols[...] = pull
    total = jnp.sum(lax.fori_loop(0, blocks, squares, jnp.zeros((shard, width), f32)), keepdims=True)
    leads = jnp.where(row == 0, 1.0, 0.0)
    total = total + leads * jnp.sum(bias * bias, keepdims=True)
    lasso = leads * lasso_coef * jnp.sum(mass * norms_ref[...], keepdims=True)
    share_tile(1, jnp.concatenate(
        [jnp.broadcast_to(total, (4, quarter)), jnp.broadcast_to(lasso, (4, quarter))], axis=0))
    first = shared_tile(0)
    center = jnp.concatenate([first[at : at + 1, :] for at in range(4)], axis=1)
    center_out[...] = center
    second = shared_tile(1)
    squared = second[0:4, :] + jnp.sum(center * center, keepdims=True)
    totals_out[...] = jnp.concatenate([squared, first[4:8, :] + second[4:8, :]], axis=0)
    for kind in range(2):
        for step in range(1, rows_size):
            fact_copy(kind, step).wait_send()

        def sent(step, kind=kind):
            tile_copy(kind, step).wait_send()

        over_devices(sent)
    for block in range(max(blocks - 2, 0), blocks):
        for which in range(2):
            for stage, size in ((0, x_size), (1, Z_CHIPS)):
                for step in range(1, size):
                    for copy in copies(stage, block, which, step):
                        copy.wait_send()


def backward(rows_size, lat_size, inputs, back, dec_cols, norms_row, lasso_row, pull_row, mass_rows, stats, master,
             active, slope):
    blocks, tokens, width = active.shape
    depth = inputs.shape[1]
    shard = depth // rows_size
    latents = dec_cols.shape[1]
    x_size = rows_size // Z_CHIPS
    devices = rows_size * lat_size
    chunk = min(CHUNK, tokens)
    i16 = jnp.int16
    dma = pltpu.SemaphoreType.DMA
    vmem = pl.BlockSpec(memory_space=pltpu.VMEM)
    hbm = pl.BlockSpec(memory_space=pl.ANY)
    return pl.pallas_call(
        functools.partial(backward_kernel, rows_size, lat_size),
        out_shape=[
            jax.ShapeDtypeStruct((shard, latents), f32),
            jax.ShapeDtypeStruct((shard, latents), f32),
            jax.ShapeDtypeStruct((1, latents), f32),
            jax.ShapeDtypeStruct((1, depth), f32),
            jax.ShapeDtypeStruct((8, 128), f32),
        ],
        in_specs=[vmem] * 9 + [hbm] * 2,
        out_specs=[vmem] * 5,
        scratch_shapes=[
            pltpu.VMEM((tokens, width), bf16),
            pltpu.VMEM((2, tokens, width), bf16),
            pltpu.VMEM((SLOTS, chunk, width), f32),
            pltpu.VMEM((2, 2, depth, width), f32),
            pltpu.VMEM((2, 2, x_size - 1, Z_CHIPS, shard, width), i16),
            pltpu.VMEM((2, 2, x_size - 1, 8, 128), f32),
            pltpu.VMEM((blocks, 2, x_size - 1, Z_CHIPS, shard, width), i16),
            pltpu.VMEM((blocks, 2, x_size - 1, 8, 128), f32),
            pltpu.VMEM((2, 2, Z_CHIPS - 1, shard, width), i16),
            pltpu.VMEM((2, 2, Z_CHIPS - 1, 8, 128), f32),
            pltpu.VMEM((blocks, 2, Z_CHIPS - 1, shard, width), i16),
            pltpu.VMEM((blocks, 2, Z_CHIPS - 1, 8, 128), f32),
            pltpu.VMEM((8, latents), f32),
            pltpu.VMEM((1, latents), f32),
            pltpu.VMEM((2, rows_size, 8, latents // 8), f32),
            pltpu.VMEM((2, devices, 8, 128), f32),
            dma((2,)), dma((SLOTS,)),
            dma((2, 2, x_size - 1)), dma((blocks, 2, x_size - 1)),
            dma((2, 2, x_size - 1)), dma((blocks, 2, x_size - 1)),
            dma((2, 2, Z_CHIPS - 1)), dma((blocks, 2, Z_CHIPS - 1)),
            dma((2, 2, Z_CHIPS - 1)), dma((blocks, 2, Z_CHIPS - 1)),
            dma((2, rows_size)), dma((2, rows_size)), dma((2, devices)), dma((2, devices)),
        ],
        compiler_params=pltpu.CompilerParams(
            collective_id=2, has_side_effects=True, vmem_limit_bytes=61 * 2**20),
        name="backward",
    )(inputs, back, dec_cols, norms_row, lasso_row, pull_row, mass_rows, stats, master, active, slope)


def body(
    token_ids,
    token_mask,
    scale_index,
    embed,
    norm_params,
    frozen_bias,
    w_joined,
    w_attn_out,
    w_mlp_in,
    w_mlp_out,
    enc_weight,
    enc_moment,
    enc_second,
    dec_weight,
    dec_moment,
    dec_second,
    enc_bias,
    enc_bias_moment,
    enc_bias_second,
    dec_bias,
    dec_bias_moment,
    dec_bias_second,
):
    lat_size = lax.axis_size("lat")
    lat_index = lax.axis_index("lat")
    group_tokens = token_ids.shape[0]
    tok_local = group_tokens // lat_size
    rows_size = lax.axis_size("rows")
    depth = enc_weight.shape[0] * rows_size
    mask_float = token_mask.astype(f32)
    dec_master = dec_weight.T
    bias_row = frozen_bias[None, :]
    vocab_local = embed.shape[0]
    vocab_first = lat_index * vocab_local
    local_ids = token_ids - vocab_first
    inside = (local_ids >= 0) & (local_ids < vocab_local)
    picked = jnp.take(embed, jnp.clip(local_ids, 0, vocab_local - 1), axis=0)
    picked = jnp.where(inside[:, None], picked, jnp.zeros((), bf16))
    own = jnp.stack([enc_weight.astype(bf16), dec_master.astype(bf16)])
    x_size = rows_size // Z_CHIPS
    right_pairs = [(i, i + x_size) for i in range(rows_size - x_size)]
    left_pairs = [(i + x_size, i) for i in range(rows_size - x_size)]
    from_left = lax.ppermute(own, "rows", right_pairs)
    from_right = lax.ppermute(own, "rows", left_pairs)
    across = []
    for step in range(1, x_size):
        pairs = [(i // x_size * x_size + (i + step) % x_size, i) for i in range(rows_size)]
        across.append(lax.ppermute(own, "rows", pairs))
    own_first = lat_index * tok_local
    scales = 0.5 + 0.25 * lax.dynamic_slice_in_dim(scale_index, own_first, tok_local).astype(f32)
    level_lanes = jnp.broadcast_to(scales[:, None], (tok_local, 128))
    mask_lanes = jnp.broadcast_to(mask_float[:, None], (group_tokens, 128))
    all_inputs, enc_low, dec_cols, norms_row, lasso_row, pull_row, scale_rows = front(
        rows_size, lat_size, picked, norm_params, bias_row, w_joined, w_attn_out, w_mlp_in, w_mlp_out,
        turn_tables(tok_local), level_lanes, mask_float.reshape(-1, 128), dec_master,
        own, from_left, from_right, jnp.stack(across))
    active, slope, mass_rows, recon_grad, stats = forward(
        lat_size, all_inputs, enc_low, dec_cols, enc_bias[None, :], mask_lanes, dec_bias[None, :], scale_rows)
    grad_enc, grad_dec, bias_total, center, totals = backward(
        rows_size, lat_size, all_inputs, recon_grad, dec_cols, norms_row, lasso_row, pull_row, mass_rows, stats, dec_master, active, slope)
    grad_enc_bias, grad_dec_bias = bias_total[0], center[0]
    grad_norm = jnp.sqrt(totals[0, 0])
    loss_sum = totals[4, 0]
    count = scale_rows[1, 0]
    factor = clip_bound / jnp.maximum(grad_norm, clip_bound)
    enc_new = adam_update(enc_weight, enc_moment, enc_second, grad_enc * factor, weight_decay)
    dec_new = adam_update(dec_weight, dec_moment, dec_second, grad_dec.T * factor, weight_decay)
    enc_bias_new = adam_update(
        enc_bias, enc_bias_moment, enc_bias_second, grad_enc_bias * factor, 0.0
    )
    dec_bias_new = adam_update(
        dec_bias, dec_bias_moment, dec_bias_second, grad_dec_bias * factor, 0.0
    )
    return (
        enc_new[0],
        enc_new[1],
        enc_new[2],
        dec_new[0],
        dec_new[1],
        dec_new[2],
        enc_bias_new[0],
        enc_bias_new[1],
        enc_bias_new[2],
        dec_bias_new[0],
        dec_bias_new[1],
        dec_bias_new[2],
        grad_norm,
        loss_sum,
        count,
    )


def solution(mesh):
    placed = (
        P("rows"),
        P("rows"),
        P("rows"),
        P("lat", None),
        P(),
        P(),
        P(),
        P(),
        P(),
        P(),
        P("rows", "lat"),
        P("rows", "lat"),
        P("rows", "lat"),
        P("lat", "rows"),
        P("lat", "rows"),
        P("lat", "rows"),
        P("lat"),
        P("lat"),
        P("lat"),
        P(),
        P(),
        P(),
    )
    return jax.shard_map(
        body,
        mesh=mesh,
        in_specs=placed,
        out_specs=(
            P("rows", "lat"),
            P("rows", "lat"),
            P("rows", "lat"),
            P("lat", "rows"),
            P("lat", "rows"),
            P("lat", "rows"),
            P("lat"),
            P("lat"),
            P("lat"),
            P(),
            P(),
            P(),
            P(),
            P(),
            P(),
        ),
        check_vma=False,
    )
```

```python
import functools
import jax
import jax.numpy as jnp
from jax import lax
from jax.experimental import pallas as pl
from jax.experimental.pallas import tpu as pltpu
from jax.sharding import PartitionSpec as P

HEADS = 8
ROT = 16
STEP = 10
Z_CHIPS = 4
CORES = 2
SLOTS = 6
CHUNK = 1024
MESH = pl.DeviceIdType.MESH
f32 = jnp.float32
bf16 = jnp.bfloat16


lasso_coef = 5.0
clip_bound = 1.0
learn_rate = 0.03
beta_one = 0.9
beta_two = 0.999
adam_eps = 1e-08
weight_decay = 0.01


def adam_update(weight, moment, second, grad, decay):
    moment_new = beta_one * moment + (1.0 - beta_one) * grad
    second_new = beta_two * second + (1.0 - beta_two) * grad * grad
    corrected = moment_new / (1.0 - beta_one**STEP)
    scaled = jnp.sqrt(second_new / (1.0 - beta_two**STEP)) + adam_eps
    weight_new = weight - learn_rate * (corrected / scaled + decay * weight)
    return (weight_new, moment_new, second_new)


ROWS = 512
PIECE = 256
HEAD = 64
PAIR = 128


def front_kernel(
    rows_size, lat_size,
    picked_ref, norm_ref, bias_ref, mask_ref, dec_ref,
    joined_hbm, attn_hbm, mlp_in_hbm, mlp_out_hbm, turn_hbm, level_hbm, own_ref, left_ref, right_ref, across_ref,
    inputs_out, enc_out, dec_out, norms_out, lasso_out, pull_out, scale_out,
    from_core, from_y, base, queries, keys, values, context, ready, facts, got_facts,
    joined_ref, attn_ref, mlp_in_ref, mlp_out_ref, turn_ref, level_ref,
    load_sem, place_sem,
    out_right, in_left, out_left, in_right, out_x, in_x, out_fact, in_fact,
    out_core, in_core, out_y, in_y, out_own, in_own, out_near, in_near,
):
    tokens, depth = base.shape
    shard, latents = dec_ref.shape
    hidden = mlp_in_ref.shape[1]
    loads = [
        pltpu.make_async_copy(source, target, load_sem.at[at])
        for at, (source, target) in enumerate((
            (joined_hbm, joined_ref), (turn_hbm, turn_ref), (mlp_in_hbm, mlp_in_ref),
            (mlp_out_hbm, mlp_out_ref), (attn_hbm, attn_ref), (level_hbm, level_ref)))
    ]
    for load in loads:
        load.start()
    x_size = rows_size // Z_CHIPS
    y_size = lat_size // CORES
    pieces = tokens // PIECE
    row = lax.axis_index("rows")
    lat = lax.axis_index("lat")
    my_z, my_x = row // x_size, lax.rem(row, x_size)
    my_y, core = lat // CORES, lax.rem(lat, CORES)
    other = 1 - core

    def remote(src, dst, send, recv, to_row, to_lat):
        return pltpu.make_async_remote_copy(
            src_ref=src, dst_ref=dst, send_sem=send, recv_sem=recv,
            device_id=(to_row, to_lat), device_id_type=MESH)

    def peer_row(step):
        return lax.rem(row + step, rows_size)

    def x_row(step):
        return my_z * x_size + lax.rem(my_x + step, x_size)

    def y_peer(step):
        return lax.rem(my_y + step, y_size)

    barrier = pltpu.get_barrier_semaphore()
    for step in range(1, rows_size):
        pl.semaphore_signal(barrier, inc=1, device_id=(peer_row(step), lat), device_id_type=MESH)
    for step in range(1, y_size):
        pl.semaphore_signal(barrier, inc=1, device_id=(row, y_peer(step) * CORES + core), device_id_type=MESH)
    pl.semaphore_signal(barrier, inc=1, device_id=(row, my_y * CORES + other), device_id_type=MESH)

    square = jnp.sum(dec_ref[...] * dec_ref[...], axis=0, keepdims=True)
    part = latents // 8
    for at in range(8):
        facts[pl.ds(at, 1), :] = square[:, at * part : (at + 1) * part]
    facts[8:16, :] = jnp.broadcast_to(jnp.sum(mask_ref[...], keepdims=True), (8, part))
    pl.semaphore_wait(barrier, rows_size + y_size - 1)

    weights = (enc_out, dec_out)

    def weight_rows(z):
        return pl.ds(pl.multiple_of((z * x_size + my_x) * shard, shard), shard)

    def right_copy(hop, which, received=False):
        area = weights[which].at[weight_rows(jnp.maximum(my_z - hop - (1 if received else 0), 0))]
        source = left_ref.at[which] if hop == 1 and not received else area
        return remote(source, area, out_right.at[hop, which], in_left.at[hop, which],
                      jnp.minimum(my_z + 1, Z_CHIPS - 1) * x_size + my_x, lat)

    def left_copy(hop, which, received=False):
        area = weights[which].at[weight_rows(jnp.minimum(my_z + hop + (1 if received else 0), Z_CHIPS - 1))]
        source = right_ref.at[which] if hop == 1 and not received else area
        return remote(source, area, out_left.at[hop, which], in_right.at[hop, which],
                      jnp.maximum(my_z - 1, 0) * x_size + my_x, lat)

    def x_copy(z, which, step, source=None):
        area = weights[which].at[weight_rows(z)]
        return remote(area if source is None else source.at[which], area,
                      out_x.at[z, which, step - 1], in_x.at[z, which, step - 1], x_row(step), lat)

    def place(index, which):
        sources = [(own_ref, row), (left_ref, row - x_size), (right_ref, row + x_size)]
        sources += [(across_ref.at[step - 1], x_row(step)) for step in range(1, x_size)]
        source, owner = sources[index]
        owner = jnp.clip(owner, 0, rows_size - 1)
        return pltpu.make_async_copy(
            source.at[which], weights[which].at[pl.ds(pl.multiple_of(owner * shard, shard), shard)],
            place_sem.at[index, which])

    def place_all(action):
        for which in range(2):
            for index in range(x_size + 2):
                if index == 1:
                    @pl.when(my_z > 0)
                    def _():
                        action(place(1, which))
                elif index == 2:
                    @pl.when(my_z < Z_CHIPS - 1)
                    def _():
                        action(place(2, which))
                else:
                    action(place(index, which))

    def pass_on(hop, which):
        @pl.when(my_z >= hop)
        def _():
            if hop > 1:
                right_copy(hop - 1, which, True).wait_recv()
            if hop < Z_CHIPS - 1:
                @pl.when(my_z < Z_CHIPS - 1)
                def _():
                    right_copy(hop, which).start()
            for step in range(1, x_size):
                x_copy(my_z - hop, which, step, left_ref if hop == 1 else None).start()

        @pl.when(my_z + hop <= Z_CHIPS - 1)
        def _():
            if hop > 1:
                left_copy(hop - 1, which, True).wait_recv()
            if hop < Z_CHIPS - 1:
                @pl.when(my_z > 0)
                def _():
                    left_copy(hop, which).start()
            for step in range(1, x_size):
                x_copy(my_z + hop, which, step, right_ref if hop == 1 else None).start()

    def fact_copy(step):
        return remote(facts, got_facts.at[step - 1], out_fact.at[step - 1], in_fact.at[step - 1], peer_row(step), lat)

    def block_rows(y, which_core, piece):
        return pl.ds(pl.multiple_of((y * CORES + which_core) * tokens + piece * PIECE, PIECE), PIECE)

    def core_copy(step, piece):
        return remote(
            picked_ref.at[block_rows(y_peer(step), other, piece)], from_core.at[step, pl.ds(piece * PIECE, PIECE)],
            out_core.at[step, piece], in_core.at[step, piece], row, my_y * CORES + other)

    def y_copy(step, piece):
        here = pl.ds(piece * PIECE, PIECE)
        return remote(
            from_core.at[step, here], from_y.at[step - 1, here],
            out_y.at[step - 1, piece], in_y.at[step - 1, piece], row, y_peer(step) * CORES + core)

    for piece in range(pieces):
        for step in list(range(1, y_size)) + [0]:
            core_copy(step, piece).start()
    for piece in range(pieces):
        here = pl.ds(piece * PIECE, PIECE)
        for step in list(range(1, y_size)) + [0]:
            core_copy(step, piece).wait_recv()
            total = picked_ref[block_rows(y_peer(step), core, piece), :].astype(f32) + from_core[step, here, :].astype(f32)
            if step == 0:
                base[here, :] = total
            else:
                from_core[step, here, :] = total.astype(bf16)
                y_copy(step, piece).start()

    pass_on(1, 0)
    for step in range(1, rows_size):
        fact_copy(step).start()
    place_all(lambda copy: copy.start())
    pass_on(1, 1)
    pass_on(2, 0)

    def normed(value, gain, shift):
        centred = value - jnp.mean(value, axis=1, keepdims=True)
        spread = jnp.mean(centred * centred, axis=1, keepdims=True)
        return (centred * lax.rsqrt(spread + 1e-05) * gain + shift).astype(bf16)

    def dot(left, right):
        return jnp.dot(left, right, preferred_element_type=f32)

    def rotated(value, rows):
        cosine, low, high = turn_ref[0, rows, :], turn_ref[1, rows, :], turn_ref[2, rows, :]
        parts = []
        for at in range(depth // PAIR):
            tile = value[:, at * PAIR : (at + 1) * PAIR]
            parts.append(
                tile * cosine + pltpu.roll(tile, PAIR - ROT // 2, 1) * low + pltpu.roll(tile, ROT // 2, 1) * high)
        return jnp.concatenate(parts, axis=1)

    for load in loads:
        load.wait()
    for block in range(tokens // ROWS):
        rows = pl.ds(block * ROWS, ROWS)
        for piece in range(block * ROWS // PIECE, (block + 1) * ROWS // PIECE):
            for step in range(1, y_size):
                y_copy(step, piece).wait_recv()
        embedded = base[rows, :]
        for step in range(1, y_size):
            embedded = embedded + from_y[step - 1, rows, :].astype(f32)
        attn_in = normed(embedded, norm_ref[0:1, :], norm_ref[1:2, :])
        joined = dot(attn_in, joined_ref[...]) + bias_ref[:, : 3 * depth]
        queries[rows, :] = (rotated(joined[:, :depth], rows).astype(bf16) * HEAD**-0.5).astype(bf16)
        keys[rows, :] = rotated(joined[:, depth : 2 * depth], rows).astype(bf16)
        values[rows, :] = joined[:, 2 * depth :].astype(bf16)
        mlp_in = normed(embedded, norm_ref[2:3, :], norm_ref[3:4, :])
        inner = dot(mlp_in, mlp_in_ref[...]) + bias_ref[:, 4 * depth : 4 * depth + hidden]
        inner = (0.5 * inner * (1.0 + lax.erf(inner * 0.5**0.5))).astype(bf16)
        base[rows, :] = embedded + (dot(inner, mlp_out_ref[...]) + bias_ref[:, 4 * depth + hidden :])
        if block == 0:
            pass_on(2, 1)
    pass_on(3, 0)

    def own_rows(y, which_core, piece):
        return pl.ds(pl.multiple_of((y * CORES + which_core) * tokens + piece * PIECE, PIECE), PIECE)

    def own_copy(step, piece):
        area = inputs_out.at[own_rows(my_y, core, piece)]
        return remote(ready.at[pl.ds(piece * PIECE, PIECE)], area, out_own.at[step - 1, piece], in_own.at[step - 1, piece], row, y_peer(step) * CORES + core)

    def near_copy(step, piece):
        area = inputs_out.at[own_rows(y_peer(step), core, piece)]
        source = area if step else ready.at[pl.ds(piece * PIECE, PIECE)]
        return remote(source, area, out_near.at[step, piece], in_near.at[step, piece], row, my_y * CORES + other)

    def keep_copy(piece):
        return pltpu.make_async_copy(
            ready.at[pl.ds(piece * PIECE, PIECE)], inputs_out.at[own_rows(my_y, core, piece)], place_sem.at[x_size + 2, piece])

    lanes = lax.broadcasted_iota(jnp.int32, (PIECE, PAIR), 1)
    for piece in range(pieces):
        here = pl.ds(piece * PIECE, PIECE)
        reach = (piece + 1) * PIECE
        visible = (
            lax.broadcasted_iota(jnp.int32, (PIECE, reach), 0) + piece * PIECE
            >= lax.broadcasted_iota(jnp.int32, (PIECE, reach), 1)
        )

        def attend(pair, carry):
            cols = pl.ds(pl.multiple_of(pair * PAIR, PAIR), PAIR)
            both = queries[here, cols]
            found = []
            for first in (True, False):
                chosen = jnp.where((lanes < HEAD) == first, both, jnp.zeros_like(both))
                scores = lax.dot_general(
                    chosen, keys[0:reach, cols], (((1,), (1,)), ((), ())), preferred_element_type=f32)
                scores = jnp.where(visible, scores, -1e30)
                powers = jnp.exp(scores - jnp.max(scores, axis=1, keepdims=True))
                probs = (powers * (1.0 / jnp.sum(powers, axis=1, keepdims=True))).astype(bf16)
                found.append(dot(probs, values[0:reach, cols]))
            context[here, cols] = jnp.where(lanes < HEAD, found[0], found[1]).astype(bf16)
            return carry

        lax.fori_loop(0, depth // PAIR, attend, 0)
        attended = dot(context[here, :], attn_ref[...]) + bias_ref[:, 3 * depth : 4 * depth]
        level = jnp.concatenate([level_ref[here, :]] * (depth // 128), axis=1)
        ready[here, :] = ((base[here, :] + attended) * level).astype(bf16)
        keep_copy(piece).start()
        for step in range(1, y_size):
            own_copy(step, piece).start()
        near_copy(0, piece).start()
        if piece == 1:
            pass_on(3, 1)
        if piece >= 2:
            for step in range(1, y_size):
                own_copy(step, piece - 2).wait_recv()
                near_copy(step, piece - 2).start()

    total = facts[...]
    for step in range(1, rows_size):
        fact_copy(step).wait_recv()
        total = total + got_facts[step - 1]
    count = total[8:9, 0:1]
    norms = jnp.sqrt(total[0:8, :])
    norms = jnp.concatenate([norms[at : at + 1, :] for at in range(8)], axis=1)
    lasso_scale = lasso_coef / count
    norms_out[...] = norms
    lasso_out[...] = lasso_scale * norms
    pull_out[...] = lasso_scale / norms
    scale_out[0:1, :] = jnp.broadcast_to(2.0 / count, (1, depth))
    scale_out[1:8, :] = jnp.broadcast_to(count, (7, depth))
    for piece in range(pieces - 2, pieces):
        for step in range(1, y_size):
            own_copy(step, piece).wait_recv()
            near_copy(step, piece).start()
    place_all(lambda copy: copy.wait())

    for which in range(2):
        for hop in range(1, Z_CHIPS - 1):
            @pl.when((my_z < Z_CHIPS - 1) & (my_z >= hop))
            def _():
                right_copy(hop, which).wait_send()

            @pl.when((my_z > 0) & (my_z + hop <= Z_CHIPS - 1))
            def _():
                left_copy(hop, which).wait_send()

        for z in range(Z_CHIPS):
            @pl.when(z != my_z)
            def _():
                for step in range(1, x_size):
                    x_copy(z, which, step).wait_send()
                    x_copy(z, which, step).wait_recv()
    for step in range(1, rows_size):
        fact_copy(step).wait_send()
    for piece in range(pieces):
        keep_copy(piece).wait()
        for step in range(y_size):
            core_copy(step, piece).wait_send()
            near_copy(step, piece).wait_send()
            near_copy(step, piece).wait_recv()
        for step in range(1, y_size):
            y_copy(step, piece).wait_send()
            own_copy(step, piece).wait_send()


def front(rows_size, lat_size, picked, norm_params, bias_row, w_joined, w_attn_out, w_mlp_in, w_mlp_out,
          turns, level_lanes, mask_tiles, dec_shard, own, left, right, across):
    group, depth = picked.shape
    tokens = group // lat_size
    shard, latents = dec_shard.shape
    x_size = rows_size // Z_CHIPS
    y_size = lat_size // CORES
    pieces = tokens // PIECE
    dma = pltpu.SemaphoreType.DMA
    vmem = pl.BlockSpec(memory_space=pltpu.VMEM)
    hbm = pl.BlockSpec(memory_space=pl.ANY)
    hops = Z_CHIPS - 1
    return pl.pallas_call(
        functools.partial(front_kernel, rows_size, lat_size),
        out_shape=[
            jax.ShapeDtypeStruct((group, depth), bf16),
            jax.ShapeDtypeStruct((depth, latents), bf16),
            jax.ShapeDtypeStruct((depth, latents), bf16),
            jax.ShapeDtypeStruct((1, latents), f32),
            jax.ShapeDtypeStruct((1, latents), f32),
            jax.ShapeDtypeStruct((1, latents), f32),
            jax.ShapeDtypeStruct((8, depth), f32),
        ],
        in_specs=[vmem] * 5 + [hbm] * 6 + [vmem] * 4,
        out_specs=[hbm] * 3 + [vmem] * 4,
        scratch_shapes=[
            pltpu.VMEM((y_size, tokens, depth), bf16),
            pltpu.VMEM((y_size - 1, tokens, depth), bf16),
            pltpu.VMEM((tokens, depth), f32),
            pltpu.VMEM((tokens, depth), bf16),
            pltpu.VMEM((tokens, depth), bf16),
            pltpu.VMEM((tokens, depth), bf16),
            pltpu.VMEM((tokens, depth), bf16),
            pltpu.VMEM((tokens, depth), bf16),
            pltpu.VMEM((16, latents // 8), f32),
            pltpu.VMEM((rows_size - 1, 16, latents // 8), f32),
            *[pltpu.VMEM(a.shape, a.dtype) for a in (w_joined, w_attn_out, w_mlp_in, w_mlp_out, turns, level_lanes)],
            dma((6,)), dma((x_size + 3, max(pieces, 2))),
            dma((hops, 2)), dma((hops, 2)), dma((hops, 2)), dma((hops, 2)),
            dma((Z_CHIPS, 2, x_size - 1)), dma((Z_CHIPS, 2, x_size - 1)),
            dma((rows_size - 1,)), dma((rows_size - 1,)),
            dma((y_size, pieces)), dma((y_size, pieces)),
            dma((y_size - 1, pieces)), dma((y_size - 1, pieces)),
            dma((y_size - 1, pieces)), dma((y_size - 1, pieces)),
            dma((y_size, pieces)), dma((y_size, pieces)),
        ],
        compiler_params=pltpu.CompilerParams(
            collective_id=3, has_side_effects=True, vmem_limit_bytes=60 * 2**20),
        name="front",
    )(picked, norm_params, bias_row, mask_tiles, dec_shard,
      w_joined, w_attn_out, w_mlp_in, w_mlp_out, turns, level_lanes, own, left, right, across)


def turn_tables(length):
    half = ROT // 2
    freqs = 10000.0 ** (-2.0 * jnp.arange(half, dtype=f32) / ROT)
    angles = jnp.arange(length, dtype=f32)[:, None] * jnp.tile(freqs, PAIR // half)[None, :]
    place = jnp.arange(PAIR) % HEAD
    cosines, sines = jnp.cos(angles), jnp.sin(angles)
    return jnp.stack([
        jnp.where(place < ROT, cosines, 1.0),
        jnp.where(place < half, -sines, 0.0),
        jnp.where((place >= half) & (place < ROT), sines, 0.0),
    ])


def softplus_parts(value):
    power = jnp.exp(value)
    grown = jnp.log(1.0 + power)
    grown = jnp.where(power < 2.0**-8, power * (1.0 - 0.5 * power), grown)
    active = jnp.where(value > 30.0, value, grown)
    return active, jnp.exp(value - active)


def forward_kernel(
    lat_size,
    inputs_hbm, enc_hbm, dec_hbm, mask_hbm, enc_bias_ref, dec_bias_ref, scale_ref,
    active_hbm, slope_hbm, mass_out, back_out, stats_out,
    active_buf, slope_buf, product, partial, own, send_two, units_two, recv_one, recv_two, got_two,
    inputs_ref, enc_ref, dec_ref, mask_ref, load_sem,
    active_sem, slope_sem, out_one, in_one, out_two, in_two, outu_two, inu_two, out_three, in_three, out_four, in_four,
):
    tokens, depth = inputs_ref.shape
    latents = enc_ref.shape[1]
    chunk, span = product.shape[1:]
    halves = [pl.ds(at * span, span) for at in range(latents // span)]
    loads = [pltpu.make_async_copy(inputs_hbm, inputs_ref, load_sem.at[0]), pltpu.make_async_copy(mask_hbm, mask_ref, load_sem.at[1])]
    for at, cols in enumerate(halves):
        loads.append(pltpu.make_async_copy(enc_hbm.at[:, cols], enc_ref.at[:, cols], load_sem.at[2 + 2 * at]))
        loads.append(pltpu.make_async_copy(dec_hbm.at[:, cols], dec_ref.at[:, cols], load_sem.at[3 + 2 * at]))
    for load in loads:
        load.start()

    width = active_hbm.shape[2]
    chunks, spans = tokens // chunk, latents // span
    y_size = lat_size // CORES
    share = chunk // lat_size
    strip = 16
    row = lax.axis_index("rows")
    lat = lax.axis_index("lat")
    my_y, core = lat // CORES, lax.rem(lat, CORES)
    other = 1 - core

    def y_peer(step):
        return lax.rem(my_y + step, y_size)

    def share_rows(y, which_core):
        return pl.multiple_of((y * CORES + which_core) * share, share)

    def token_rows(block, y, which_core):
        return pl.ds(pl.multiple_of(block * chunk + (y * CORES + which_core) * share, share), share)

    def remote(src, dst, send, recv, target):
        return pltpu.make_async_remote_copy(
            src_ref=src, dst_ref=dst, send_sem=send, recv_sem=recv,
            device_id=(row, target), device_id_type=MESH)

    def copy_one(block, y):
        slot = lax.rem(block, 2)
        return remote(
            partial.at[slot, pl.ds(share_rows(y, other), share)], recv_one.at[block, y],
            out_one.at[slot, y], in_one.at[block, y], my_y * CORES + other)

    def copies_two(block, step):
        slot = lax.rem(block, 2)
        target = y_peer(step) * CORES + core
        return [
            remote(send_two.at[slot, step - 1], recv_two.at[block, step - 1],
                   out_two.at[slot, step - 1], in_two.at[block, step - 1], target),
            remote(units_two.at[slot, step - 1], got_two.at[block, step - 1],
                   outu_two.at[slot, step - 1], inu_two.at[block, step - 1], target),
        ]

    def copy_three(block, step):
        mine = back_out.at[token_rows(block, my_y, core)]
        return remote(
            mine, mine, out_three.at[block, step - 1], in_three.at[block, step - 1], y_peer(step) * CORES + core)

    def copy_four(block, y):
        mine = back_out.at[token_rows(block, y, core)]
        return remote(mine, mine, out_four.at[block, y], in_four.at[block, y], my_y * CORES + other)

    def stores(block, at, slot):
        rows = pl.ds(pl.multiple_of(block * chunk, chunk), chunk)
        copies = []
        for part in range(span // width):
            lanes = pl.ds(part * width, width)
            copies.append(pltpu.make_async_copy(
                active_buf.at[slot, :, lanes], active_hbm.at[at * (span // width) + part, rows], active_sem.at[slot, part]))
            copies.append(pltpu.make_async_copy(
                slope_buf.at[slot, :, lanes], slope_hbm.at[at * (span // width) + part, rows], slope_sem.at[slot, part]))
        return copies

    barrier = pltpu.get_barrier_semaphore()
    pl.semaphore_signal(barrier, inc=1, device_id=(row, my_y * CORES + other), device_id_type=MESH)
    for step in range(1, y_size):
        pl.semaphore_signal(barrier, inc=1, device_id=(row, y_peer(step) * CORES + core), device_id_type=MESH)
    mass_out[...] = jnp.zeros_like(mass_out)
    stats_out[...] = jnp.zeros_like(stats_out)
    pl.semaphore_wait(barrier, y_size)

    def compute(block):
        place = lax.rem(block, 2)
        first = pl.multiple_of(block * chunk, chunk)

        @pl.when(block >= 2)
        def _():
            for y in range(y_size):
                copy_one(block - 2, y).wait_send()

        for at in range(spans):
            slot = at % 2
            if at >= 2:
                for copy in stores(block, at - 2, slot):
                    copy.wait()
            else:
                @pl.when(block > 0)
                def _():
                    for copy in stores(block - 1, spans - 2 + at, slot):
                        copy.wait()

            @pl.when(block == 0)
            def _():
                for load in loads[2 * at + 2 : 2 * at + 4] + (loads[:2] if at == 0 else []):
                    load.wait()

            product[slot] = jnp.dot(
                inputs_ref[pl.ds(first, chunk), :], enc_ref[:, at * span : (at + 1) * span], preferred_element_type=f32)
            for left in range(0, span, width):
                lanes = pl.ds(left, width)
                cols = pl.ds(at * span + left, width)
                shift = enc_bias_ref[:, cols]
                total = mass_out[:, cols]
                for top in range(0, chunk, strip):
                    rows = pl.ds(top, strip)
                    mask = mask_ref[pl.ds(first + top, strip), :]
                    mask = jnp.concatenate([mask] * (width // 128), axis=1)
                    active, slope = softplus_parts(product[slot, rows, lanes] + shift)
                    active_buf[slot, rows, lanes] = active.astype(bf16)
                    slope_buf[slot, rows, lanes] = slope * mask
                    total = total + (active * mask).reshape(strip // 8, 8, width).sum(0)
                mass_out[:, cols] = total
            for copy in stores(block, at, slot):
                copy.start()
            part = lax.dot_general(
                active_buf[slot], dec_ref[:, at * span : (at + 1) * span], (((1,), (1,)), ((), ())),
                preferred_element_type=f32)
            partial[place] = part if at == 0 else partial[place] + part

    def exchange(block):
        slot = lax.rem(block, 2)
        for y in range(y_size):
            copy_one(block, y).wait_recv()
        for step in list(range(1, y_size)) + [0]:
            y = y_peer(step)
            total = partial[slot, pl.ds(share_rows(y, core), share), :] + recv_one[block, y]
            if step == 0:
                own[slot] = total
            else:
                @pl.when(block >= 2)
                def _():
                    for copy in copies_two(block - 2, step):
                        copy.wait_send()

                code, unit = encode(total)
                send_two[slot, step - 1] = code
                put_units(units_two, (slot, step - 1), unit)
                for copy in copies_two(block, step):
                    copy.start()

    def settle(block):
        slot = lax.rem(block, 2)
        rows = token_rows(block, my_y, core)
        total = own[slot]
        for step in range(1, y_size):
            for copy in copies_two(block, step):
                copy.wait_recv()
            total = total + decode(recv_two[block, step - 1], get_units(got_two, (block, step - 1), depth))
        error = total + dec_bias_ref[...] - inputs_ref[rows, :].astype(f32)
        mask = jnp.concatenate([mask_ref[rows, :]] * (depth // 128), axis=1)
        low = (scale_ref[0:1, :] * mask * error).astype(bf16)
        back_out[rows, :] = low
        stats_out[0:8, :] += (mask * error * error).reshape(share // 8, 8, depth).sum(0)
        stats_out[8:16, :] += low.astype(f32).reshape(share // 8, 8, depth).sum(0)
        for step in range(1, y_size):
            copy_three(block, step).start()

    def spread(block):
        for step in range(1, y_size):
            copy_three(block, step).wait_recv()
        for y in range(y_size):
            copy_four(block, y).start()

    def turn(block, carry):
        @pl.when(block < chunks)
        def _():
            compute(block)
            for y in range(y_size):
                copy_one(block, y).start()

        @pl.when((block >= 1) & (block <= chunks))
        def _():
            exchange(block - 1)

        @pl.when((block >= 2) & (block <= chunks + 1))
        def _():
            settle(block - 2)

        @pl.when(block >= 3)
        def _():
            spread(block - 3)

        return carry

    lax.fori_loop(0, chunks + 3, turn, 0)
    for slot in range(2):
        for copy in stores(chunks - 1, spans - 2 + slot, slot):
            copy.wait()
    for block in range(chunks - 2, chunks):
        for y in range(y_size):
            copy_one(block, y).wait_send()
        for step in range(1, y_size):
            for copy in copies_two(block, step):
                copy.wait_send()

    def drain(block, carry):
        for step in range(1, y_size):
            copy_three(block, step).wait_send()
        for y in range(y_size):
            copy_four(block, y).wait_send()
            copy_four(block, y).wait_recv()
        return carry

    lax.fori_loop(0, chunks, drain, 0)


def forward(lat_size, inputs, enc_low, dec_cols, enc_bias_row, mask_lanes, dec_bias_row, scale_rows):
    tokens, depth = inputs.shape
    latents = enc_low.shape[1]
    chunk, span, width = 512, 1024, (512 if tokens <= 4096 else 256)
    chunks = tokens // chunk
    y_size = lat_size // CORES
    share = chunk // lat_size
    dma = pltpu.SemaphoreType.DMA
    vmem = pl.BlockSpec(memory_space=pltpu.VMEM)
    hbm = pl.BlockSpec(memory_space=pl.ANY)
    return pl.pallas_call(
        functools.partial(forward_kernel, lat_size),
        out_shape=[
            jax.ShapeDtypeStruct((latents // width, tokens, width), bf16),
            jax.ShapeDtypeStruct((latents // width, tokens, width), f32),
            jax.ShapeDtypeStruct((8, latents), f32),
            jax.ShapeDtypeStruct((tokens, depth), bf16),
            jax.ShapeDtypeStruct((16, depth), f32),
        ],
        in_specs=[hbm] * 4 + [vmem] * 3,
        out_specs=[hbm, hbm, vmem, vmem, vmem],
        scratch_shapes=[
            pltpu.VMEM((2, chunk, span), bf16),
            pltpu.VMEM((2, chunk, span), f32),
            pltpu.VMEM((2, chunk, span), f32),
            pltpu.VMEM((2, chunk, depth), f32),
            pltpu.VMEM((2, share, depth), f32),
            pltpu.VMEM((2, y_size - 1, share, depth), jnp.int16),
            pltpu.VMEM((2, y_size - 1, 8, 128), f32),
            pltpu.VMEM((chunks, y_size, share, depth), f32),
            pltpu.VMEM((chunks, y_size - 1, share, depth), jnp.int16),
            pltpu.VMEM((chunks, y_size - 1, 8, 128), f32),
            *[pltpu.VMEM(a.shape, a.dtype) for a in (inputs, enc_low, dec_cols, mask_lanes)],
            dma((2 + 2 * (latents // span),)),
            dma((2, span // width)), dma((2, span // width)),
            dma((2, y_size)), dma((chunks, y_size)),
            dma((2, y_size - 1)), dma((chunks, y_size - 1)),
            dma((2, y_size - 1)), dma((chunks, y_size - 1)),
            dma((chunks, y_size - 1)), dma((chunks, y_size - 1)),
            dma((chunks, y_size)), dma((chunks, y_size)),
        ],
        compiler_params=pltpu.CompilerParams(
            collective_id=1, has_side_effects=True, vmem_limit_bytes=60 * 2**20),
        name="forward",
    )(inputs, enc_low, dec_cols, mask_lanes, enc_bias_row, dec_bias_row, scale_rows)


def encode(value):
    top = jnp.max(jnp.abs(value), axis=0, keepdims=True)
    unit = jnp.where(top > 0.0, 32766.0 / top, 0.0)
    shifted = value * unit + 12582912.0
    return (shifted - 12582912.0).astype(jnp.int32).astype(jnp.int16), top * (1.0 / 32766.0)


def decode(code, unit):
    return code.astype(jnp.int32).astype(f32) * unit


def put_units(ref, index, unit):
    for piece in range(unit.shape[1] // 128):
        ref[index + (pl.ds(piece, 1), slice(None))] = unit[:, piece * 128 : piece * 128 + 128]


def get_units(ref, index, width):
    return jnp.concatenate(
        [ref[index + (pl.ds(piece, 1), slice(None))] for piece in range(width // 128)], axis=1)


def backward_kernel(
    rows_size, lat_size,
    back_ref, norms_ref, lasso_ref, pull_ref, mass_ref, stats_ref,
    inputs_hbm, dec_hbm, master_hbm, active_hbm, slope_hbm,
    enc_out, dec_out, bias_out, center_out, totals_out,
    grad_low, active_buf, slope_buf, sums,
    send_one, units_one, recv_one, got_one,
    send_two, units_two, recv_two, got_two,
    bias_rows, pull_cols, facts, tiles, inputs_ref, dec_ref, master_ref, load_sem,
    active_sem, slope_sem,
    out_one, in_one, outu_one, inu_one, out_two, in_two, outu_two, inu_two, out_facts, in_facts, out_tiles, in_tiles,
):
    blocks, tokens, width = active_hbm.shape
    chunk = slope_buf.shape[1]
    chunks = tokens // chunk
    shard = enc_out.shape[0]
    x_size = rows_size // Z_CHIPS
    row = lax.axis_index("rows")
    lat = lax.axis_index("lat")
    my_z, my_x = row // x_size, lax.rem(row, x_size)

    def x_peer(step):
        return lax.rem(my_x + step, x_size)

    def z_peer(step):
        return lax.rem(my_z + step, Z_CHIPS)

    def active_copy(block):
        slot = lax.rem(block, 2)
        return pltpu.make_async_copy(active_hbm.at[block], active_buf.at[slot], active_sem.at[slot])

    def slope_copy(index):
        slot = lax.rem(index, slope_buf.shape[0])
        return pltpu.make_async_copy(
            slope_hbm.at[index // chunks, pl.ds(pl.multiple_of(lax.rem(index, chunks) * chunk, chunk), chunk)],
            slope_buf.at[slot],
            slope_sem.at[slot],
        )

    def copies(stage, block, which, step):
        slot = lax.rem(block, 2)
        if stage == 0:
            target = (my_z * x_size + x_peer(step), lat)
            refs = (send_one, recv_one, out_one, in_one, units_one, got_one, outu_one, inu_one)
        else:
            target = (z_peer(step) * x_size + my_x, lat)
            refs = (send_two, recv_two, out_two, in_two, units_two, got_two, outu_two, inu_two)
        return [
            pltpu.make_async_remote_copy(
                src_ref=refs[at].at[slot, which, step - 1], dst_ref=refs[at + 1].at[block, which, step - 1],
                send_sem=refs[at + 2].at[slot, which, step - 1], recv_sem=refs[at + 3].at[block, which, step - 1],
                device_id=target, device_id_type=MESH)
            for at in (0, 4)
        ]

    devices = rows_size * lat_size
    me = row * lat_size + lat
    latents = dec_ref.shape[1]
    depth = inputs_ref.shape[1]
    part = latents // 8

    def fact_copy(kind, step):
        area = facts.at[kind, row]
        return pltpu.make_async_remote_copy(
            src_ref=area, dst_ref=area, send_sem=out_facts.at[kind, step], recv_sem=in_facts.at[kind, row],
            device_id=(lax.rem(row + step, rows_size), lat), device_id_type=MESH)

    def fact_arrival(kind, step):
        source = lax.rem(row + step, rows_size)
        area = facts.at[kind, source]
        return pltpu.make_async_remote_copy(
            src_ref=area, dst_ref=area, send_sem=out_facts.at[kind, step], recv_sem=in_facts.at[kind, source],
            device_id=(source, lat), device_id_type=MESH)

    def tile_copy(kind, step):
        area = tiles.at[kind, me]
        target = lax.rem(me + step, devices)
        return pltpu.make_async_remote_copy(
            src_ref=area, dst_ref=area, send_sem=out_tiles.at[kind, step], recv_sem=in_tiles.at[kind, me],
            device_id=(target // lat_size, lax.rem(target, lat_size)), device_id_type=MESH)

    def tile_arrival(kind, step):
        source = lax.rem(me + step, devices)
        area = tiles.at[kind, source]
        return pltpu.make_async_remote_copy(
            src_ref=area, dst_ref=area, send_sem=out_tiles.at[kind, step], recv_sem=in_tiles.at[kind, source],
            device_id=(source // lat_size, lax.rem(source, lat_size)), device_id_type=MESH)

    def over_devices(action):
        def turn(step, carry):
            action(step)
            return carry

        lax.fori_loop(1, devices, turn, 0)

    def share_row(kind, value):
        for at in range(8):
            facts[kind, row, pl.ds(at, 1), :] = value[:, at * part : (at + 1) * part]
        for step in range(1, rows_size):
            fact_copy(kind, step).start()

    def shared_row(kind):
        for step in range(1, rows_size):
            fact_arrival(kind, step).wait_recv()
        total = facts[kind, 0]
        for source in range(1, rows_size):
            total = total + facts[kind, source]
        return jnp.concatenate([total[at : at + 1, :] for at in range(8)], axis=1)

    def share_tile(kind, value):
        tiles[kind, me] = value

        def start(step):
            tile_copy(kind, step).start()

        over_devices(start)

    def shared_tile(kind):
        def wait(step):
            tile_arrival(kind, step).wait_recv()

        over_devices(wait)
        return lax.fori_loop(1, devices, lambda source, total: total + tiles[kind, source], tiles[kind, 0])

    barrier = pltpu.get_barrier_semaphore()

    def greet(step):
        target = lax.rem(me + step, devices)
        pl.semaphore_signal(
            barrier, inc=1, device_id=(target // lat_size, lax.rem(target, lat_size)), device_id_type=MESH)

    over_devices(greet)
    loads = [
        pltpu.make_async_copy(source, target, load_sem.at[at])
        for at, (source, target) in enumerate(((dec_hbm, dec_ref), (inputs_hbm, inputs_ref), (master_hbm, master_ref)))
    ]
    active_copy(0).start()
    for load in loads:
        load.start()
    ahead = slope_buf.shape[0] - 1
    for index in range(ahead):
        slope_copy(index).start()
    pl.semaphore_wait(barrier, devices - 1)
    share_row(0, jnp.sum(mass_ref[...], axis=0, keepdims=True))
    center = jnp.sum(stats_ref[8:16, :], axis=0, keepdims=True)
    square = jnp.sum(stats_ref[0:8, :], keepdims=True)
    quarter = depth // 4
    share_tile(0, jnp.concatenate(
        [center[:, at * quarter : (at + 1) * quarter] for at in range(4)]
        + [jnp.broadcast_to(square, (4, quarter))], axis=0))

    def columns(block):
        return pl.ds(pl.multiple_of(block * width, width), width)

    over_tokens = (((0,), (0,)), ((), ()))

    def compute_dec(block):
        slot = lax.rem(block, 2)

        @pl.when(block + 1 < blocks)
        def _():
            active_copy(block + 1).start()

        active_copy(block).wait()
        sums[slot, 1] = lax.dot_general(back_ref[...], active_buf[slot], over_tokens, preferred_element_type=f32)

    def compute_enc(block):
        slot = lax.rem(block, 2)
        cols = columns(block)

        @pl.when(block == 0)
        def _():
            for load in loads:
                load.wait()

        def piece(index, total):
            at = block * chunks + index

            @pl.when(at + ahead < blocks * chunks)
            def _():
                slope_copy(at + ahead).start()

            slope_copy(at).wait()
            rows = pl.ds(pl.multiple_of(index * chunk, chunk), chunk)
            back = jnp.dot(back_ref[rows, :], dec_ref[:, cols], preferred_element_type=f32)
            low = ((back + lasso_ref[:, cols]) * slope_buf[lax.rem(at, ahead + 1)]).astype(bf16)
            grad_low[rows, :] = low
            return total + low.astype(f32).reshape(chunk // 8, 8, width).sum(0)

        bias_rows[:, cols] = lax.fori_loop(0, chunks, piece, jnp.zeros((8, width), f32))
        sums[slot, 0] = lax.dot_general(inputs_ref[...], grad_low[...], over_tokens, preferred_element_type=f32)

    def send_x(block, which):
        slot = lax.rem(block, 2)
        for step in range(1, x_size):
            @pl.when(block >= 2)
            def _():
                for copy in copies(0, block - 2, which, step):
                    copy.wait_send()

            parts = []
            for z in range(Z_CHIPS):
                first = pl.multiple_of((z * x_size + x_peer(step)) * shard, shard)
                parts.append(sums[slot, which, pl.ds(first, shard), :])
            code, unit = encode(jnp.concatenate(parts, axis=0))
            for z in range(Z_CHIPS):
                send_one[slot, which, step - 1, z] = code[z * shard : (z + 1) * shard]
            put_units(units_one, (slot, which, step - 1), unit)
            for copy in copies(0, block, which, step):
                copy.start()

    def send_z(block, which):
        slot = lax.rem(block, 2)
        for step in range(1, x_size):
            for copy in copies(0, block, which, step):
                copy.wait_recv()
        for step in range(Z_CHIPS):
            z = z_peer(step)
            if step:
                @pl.when(block >= 2)
                def _():
                    for copy in copies(1, block - 2, which, step):
                        copy.wait_send()

            first = pl.multiple_of((z * x_size + my_x) * shard, shard)
            total = sums[slot, which, pl.ds(first, shard), :]
            for x_step in range(1, x_size):
                total = total + decode(
                    recv_one[block, which, x_step - 1, z], get_units(got_one, (block, which, x_step - 1), width))
            if step == 0:
                (enc_out, dec_out)[which][:, columns(block)] = total
            else:
                code, unit = encode(total)
                send_two[slot, which, step - 1] = code
                put_units(units_two, (slot, which, step - 1), unit)
                for copy in copies(1, block, which, step):
                    copy.start()

    def finish(block, which):
        slot = lax.rem(block, 2)
        for step in range(1, Z_CHIPS):
            for copy in copies(1, block, which, step):
                copy.wait_recv()
        out, cols = (enc_out, dec_out)[which], columns(block)
        total = out[:, cols]
        for step in range(1, Z_CHIPS):
            total = total + decode(
                recv_two[block, which, step - 1], get_units(got_two, (block, which, step - 1), width))
        out[:, cols] = total

    def turn(block, carry):
        for which, compute in ((1, compute_dec), (0, compute_enc)):
            @pl.when(block < blocks)
            def _():
                compute(block)
                send_x(block, which)

            @pl.when((block >= 1) & (block <= blocks))
            def _():
                send_z(block - 1, which)

            @pl.when(block >= 2)
            def _():
                finish(block - 2, which)

        return carry

    lax.fori_loop(0, blocks, turn, 0)
    share_row(1, jnp.sum(bias_rows[...], axis=0, keepdims=True))
    lax.fori_loop(blocks, blocks + 2, turn, 0)

    mass = shared_row(0)
    bias = shared_row(1)
    bias_out[...] = bias
    pull = mass * pull_ref[...]

    def squares(block, total):
        cols = columns(block)
        gain = dec_out[:, cols] + pull_cols[:, cols] * master_ref[:, cols]
        dec_out[:, cols] = gain
        other = enc_out[:, cols]
        return total + gain * gain + other * other

    pull_cols[...] = pull
    total = jnp.sum(lax.fori_loop(0, blocks, squares, jnp.zeros((shard, width), f32)), keepdims=True)
    leads = jnp.where(row == 0, 1.0, 0.0)
    total = total + leads * jnp.sum(bias * bias, keepdims=True)
    lasso = leads * lasso_coef * jnp.sum(mass * norms_ref[...], keepdims=True)
    share_tile(1, jnp.concatenate(
        [jnp.broadcast_to(total, (4, quarter)), jnp.broadcast_to(lasso, (4, quarter))], axis=0))
    first = shared_tile(0)
    center = jnp.concatenate([first[at : at + 1, :] for at in range(4)], axis=1)
    center_out[...] = center
    second = shared_tile(1)
    squared = second[0:4, :] + jnp.sum(center * center, keepdims=True)
    totals_out[...] = jnp.concatenate([squared, first[4:8, :] + second[4:8, :]], axis=0)
    for kind in range(2):
        for step in range(1, rows_size):
            fact_copy(kind, step).wait_send()

        def sent(step, kind=kind):
            tile_copy(kind, step).wait_send()

        over_devices(sent)
    for block in range(max(blocks - 2, 0), blocks):
        for which in range(2):
            for stage, size in ((0, x_size), (1, Z_CHIPS)):
                for step in range(1, size):
                    for copy in copies(stage, block, which, step):
                        copy.wait_send()


def backward(rows_size, lat_size, inputs, back, dec_cols, norms_row, lasso_row, pull_row, mass_rows, stats, master,
             active, slope):
    blocks, tokens, width = active.shape
    depth = inputs.shape[1]
    shard = depth // rows_size
    latents = dec_cols.shape[1]
    x_size = rows_size // Z_CHIPS
    devices = rows_size * lat_size
    chunk = min(CHUNK, tokens)
    i16 = jnp.int16
    dma = pltpu.SemaphoreType.DMA
    vmem = pl.BlockSpec(memory_space=pltpu.VMEM)
    hbm = pl.BlockSpec(memory_space=pl.ANY)
    return pl.pallas_call(
        functools.partial(backward_kernel, rows_size, lat_size),
        out_shape=[
            jax.ShapeDtypeStruct((shard, latents), f32),
            jax.ShapeDtypeStruct((shard, latents), f32),
            jax.ShapeDtypeStruct((1, latents), f32),
            jax.ShapeDtypeStruct((1, depth), f32),
            jax.ShapeDtypeStruct((8, 128), f32),
        ],
        in_specs=[vmem] * 6 + [hbm] * 5,
        out_specs=[vmem] * 5,
        scratch_shapes=[
            pltpu.VMEM((tokens, width), bf16),
            pltpu.VMEM((2, tokens, width), bf16),
            pltpu.VMEM((SLOTS, chunk, width), f32),
            pltpu.VMEM((2, 2, depth, width), f32),
            pltpu.VMEM((2, 2, x_size - 1, Z_CHIPS, shard, width), i16),
            pltpu.VMEM((2, 2, x_size - 1, 8, 128), f32),
            pltpu.VMEM((blocks, 2, x_size - 1, Z_CHIPS, shard, width), i16),
            pltpu.VMEM((blocks, 2, x_size - 1, 8, 128), f32),
            pltpu.VMEM((2, 2, Z_CHIPS - 1, shard, width), i16),
            pltpu.VMEM((2, 2, Z_CHIPS - 1, 8, 128), f32),
            pltpu.VMEM((blocks, 2, Z_CHIPS - 1, shard, width), i16),
            pltpu.VMEM((blocks, 2, Z_CHIPS - 1, 8, 128), f32),
            pltpu.VMEM((8, latents), f32),
            pltpu.VMEM((1, latents), f32),
            pltpu.VMEM((2, rows_size, 8, latents // 8), f32),
            pltpu.VMEM((2, devices, 8, 128), f32),
            *[pltpu.VMEM(a.shape, a.dtype) for a in (inputs, dec_cols, master)],
            dma((3,)),
            dma((2,)), dma((SLOTS,)),
            dma((2, 2, x_size - 1)), dma((blocks, 2, x_size - 1)),
            dma((2, 2, x_size - 1)), dma((blocks, 2, x_size - 1)),
            dma((2, 2, Z_CHIPS - 1)), dma((blocks, 2, Z_CHIPS - 1)),
            dma((2, 2, Z_CHIPS - 1)), dma((blocks, 2, Z_CHIPS - 1)),
            dma((2, rows_size)), dma((2, rows_size)), dma((2, devices)), dma((2, devices)),
        ],
        compiler_params=pltpu.CompilerParams(
            collective_id=2, has_side_effects=True, vmem_limit_bytes=61 * 2**20),
        name="backward",
    )(back, norms_row, lasso_row, pull_row, mass_rows, stats, inputs, dec_cols, master, active, slope)


def update_kernel(
    totals_ref, enc_grad, dec_grad, enc_bias_grad, dec_bias_grad,
    enc_w, enc_m, enc_s, dec_w, dec_m, dec_s, enc_b, enc_bm, enc_bs, dec_b, dec_bm, dec_bs,
    enc_w_out, enc_m_out, enc_s_out, dec_w_out, dec_m_out, dec_s_out,
    enc_b_out, enc_bm_out, enc_bs_out, dec_b_out, dec_bm_out, dec_bs_out, scalars_out,
):
    norm = jnp.sqrt(totals_ref[0:1, 0:1])
    factor = clip_bound / jnp.maximum(norm, clip_bound)
    groups = (
        (enc_grad, (enc_w, enc_m, enc_s), (enc_w_out, enc_m_out, enc_s_out), weight_decay),
        (dec_grad, (dec_w, dec_m, dec_s), (dec_w_out, dec_m_out, dec_s_out), weight_decay),
        (enc_bias_grad, (enc_b, enc_bm, enc_bs), (enc_b_out, enc_bm_out, enc_bs_out), 0.0),
        (dec_bias_grad, (dec_b, dec_bm, dec_bs), (dec_b_out, dec_bm_out, dec_bs_out), 0.0),
    )
    for grad, olds, news, decay in groups:
        found = adam_update(*[old[...] for old in olds], grad[...] * factor, decay)
        for new, value in zip(news, found):
            new[...] = value
    scalars_out[0:1, :] = jnp.broadcast_to(norm, (1, 128))
    scalars_out[1:2, :] = totals_ref[4:5, :]
    scalars_out[2:8, :] = jnp.zeros((6, 128), f32)


def update(totals, grads, states):
    shard, latents = grads[0].shape
    depth = grads[3].shape[1]
    span = latents // 4
    wide = pl.BlockSpec((shard, span), lambda i: (0, i))
    row = pl.BlockSpec((1, span), lambda i: (0, i))
    short = pl.BlockSpec((1, depth), lambda i: (0, 0))
    tile = pl.BlockSpec((8, 128), lambda i: (0, 0))
    state_specs = [wide] * 6 + [row] * 3 + [short] * 3
    return pl.pallas_call(
        update_kernel,
        grid=(latents // span,),
        out_shape=[jax.ShapeDtypeStruct(a.shape, f32) for a in states] + [jax.ShapeDtypeStruct((8, 128), f32)],
        in_specs=[tile, wide, wide, row, short] + state_specs,
        out_specs=state_specs + [tile],
        compiler_params=pltpu.CompilerParams(vmem_limit_bytes=48 * 2**20),
        name="update",
    )(totals, *grads, *states)


def body(
    token_ids,
    token_mask,
    scale_index,
    embed,
    norm_params,
    frozen_bias,
    w_joined,
    w_attn_out,
    w_mlp_in,
    w_mlp_out,
    enc_weight,
    enc_moment,
    enc_second,
    dec_weight,
    dec_moment,
    dec_second,
    enc_bias,
    enc_bias_moment,
    enc_bias_second,
    dec_bias,
    dec_bias_moment,
    dec_bias_second,
):
    lat_size = lax.axis_size("lat")
    lat_index = lax.axis_index("lat")
    group_tokens = token_ids.shape[0]
    tok_local = group_tokens // lat_size
    rows_size = lax.axis_size("rows")
    depth = enc_weight.shape[0] * rows_size
    mask_float = token_mask.astype(f32)
    dec_master = dec_weight.T
    bias_row = frozen_bias[None, :]
    vocab_local = embed.shape[0]
    vocab_first = lat_index * vocab_local
    local_ids = token_ids - vocab_first
    inside = (local_ids >= 0) & (local_ids < vocab_local)
    picked = jnp.take(embed, jnp.clip(local_ids, 0, vocab_local - 1), axis=0)
    picked = jnp.where(inside[:, None], picked, jnp.zeros((), bf16))
    own = jnp.stack([enc_weight.astype(bf16), dec_master.astype(bf16)])
    x_size = rows_size // Z_CHIPS
    right_pairs = [(i, i + x_size) for i in range(rows_size - x_size)]
    left_pairs = [(i + x_size, i) for i in range(rows_size - x_size)]
    from_left = lax.ppermute(own, "rows", right_pairs)
    from_right = lax.ppermute(own, "rows", left_pairs)
    across = []
    for step in range(1, x_size):
        pairs = [(i // x_size * x_size + (i + step) % x_size, i) for i in range(rows_size)]
        across.append(lax.ppermute(own, "rows", pairs))
    own_first = lat_index * tok_local
    scales = 0.5 + 0.25 * lax.dynamic_slice_in_dim(scale_index, own_first, tok_local).astype(f32)
    level_lanes = jnp.broadcast_to(scales[:, None], (tok_local, 128))
    mask_lanes = jnp.broadcast_to(mask_float[:, None], (group_tokens, 128))
    all_inputs, enc_low, dec_cols, norms_row, lasso_row, pull_row, scale_rows = front(
        rows_size, lat_size, picked, norm_params, bias_row, w_joined, w_attn_out, w_mlp_in, w_mlp_out,
        turn_tables(tok_local), level_lanes, mask_float.reshape(-1, 128), dec_master,
        own, from_left, from_right, jnp.stack(across))
    active, slope, mass_rows, recon_grad, stats = forward(
        lat_size, all_inputs, enc_low, dec_cols, enc_bias[None, :], mask_lanes, dec_bias[None, :], scale_rows)
    grad_enc, grad_dec, bias_total, center, totals = backward(
        rows_size, lat_size, all_inputs, recon_grad, dec_cols, norms_row, lasso_row, pull_row, mass_rows, stats, dec_master, active, slope)
    states = [
        enc_weight, enc_moment, enc_second, dec_master, dec_moment.T, dec_second.T,
        enc_bias[None, :], enc_bias_moment[None, :], enc_bias_second[None, :],
        dec_bias[None, :], dec_bias_moment[None, :], dec_bias_second[None, :],
    ]
    *fresh, scalars = update(totals, (grad_enc, grad_dec, bias_total, center), states)
    return (
        *fresh[:3],
        *[value.T for value in fresh[3:6]],
        *[value[0] for value in fresh[6:]],
        scalars[0, 0],
        scalars[1, 0],
        scale_rows[1, 0],
    )


def solution(mesh):
    placed = (
        P("rows"),
        P("rows"),
        P("rows"),
        P("lat", None),
        P(),
        P(),
        P(),
        P(),
        P(),
        P(),
        P("rows", "lat"),
        P("rows", "lat"),
        P("rows", "lat"),
        P("lat", "rows"),
        P("lat", "rows"),
        P("lat", "rows"),
        P("lat"),
        P("lat"),
        P("lat"),
        P(),
        P(),
        P(),
    )
    return jax.shard_map(
        body,
        mesh=mesh,
        in_specs=placed,
        out_specs=(
            P("rows", "lat"),
            P("rows", "lat"),
            P("rows", "lat"),
            P("lat", "rows"),
            P("lat", "rows"),
            P("lat", "rows"),
            P("lat"),
            P("lat"),
            P("lat"),
            P(),
            P(),
            P(),
            P(),
            P(),
            P(),
        ),
        check_vma=False,
    )
```

```python
import functools
import jax
import jax.numpy as jnp
import numpy as np
from jax import lax
from jax.experimental import pallas as pl
from jax.experimental.pallas import tpu as pltpu
from jax.sharding import PartitionSpec as P

HEADS = 8
ROT = 16
STEP = 10
Z_CHIPS = 4
CORES = 2
SLOTS = 6
CHUNK = 1024
MESH = pl.DeviceIdType.MESH
f32 = jnp.float32
bf16 = jnp.bfloat16


lasso_coef = 5.0
clip_bound = 1.0
learn_rate = 0.03
beta_one = 0.9
beta_two = 0.999
adam_eps = 1e-08
weight_decay = 0.01


def adam_update(weight, moment, second, grad, decay):
    moment_new = beta_one * moment + (1.0 - beta_one) * grad
    second_new = beta_two * second + (1.0 - beta_two) * grad * grad
    corrected = moment_new / (1.0 - beta_one**STEP)
    scaled = jnp.sqrt(second_new / (1.0 - beta_two**STEP)) + adam_eps
    weight_new = weight - learn_rate * (corrected / scaled + decay * weight)
    return (weight_new, moment_new, second_new)


ROWS = 512
PIECE = 256
HEAD = 64
PAIR = 128


def front_kernel(
    rows_size, lat_size,
    picked_ref, norm_ref, bias_ref, mask_ref, dec_ref,
    joined_hbm, attn_hbm, mlp_in_hbm, mlp_out_hbm, turn_hbm, level_hbm, own_ref, left_ref, right_ref, across_ref,
    inputs_out, enc_out, dec_out, norms_out, lasso_out, pull_out, scale_out,
    from_core, from_y, base, queries, keys, values, context, ready, facts, got_facts,
    joined_ref, attn_ref, mlp_in_ref, mlp_out_ref, turn_ref, level_ref,
    load_sem, place_sem,
    out_right, in_left, out_left, in_right, out_x, in_x, out_fact, in_fact,
    out_core, in_core, out_y, in_y, out_own, in_own, out_near, in_near,
):
    tokens, depth = base.shape
    shard, latents = dec_ref.shape
    hidden = mlp_in_ref.shape[1]
    loads = [
        pltpu.make_async_copy(source, target, load_sem.at[at])
        for at, (source, target) in enumerate((
            (joined_hbm, joined_ref), (turn_hbm, turn_ref), (mlp_in_hbm, mlp_in_ref),
            (mlp_out_hbm, mlp_out_ref), (attn_hbm, attn_ref), (level_hbm, level_ref)))
    ]
    for load in loads:
        load.start()
    x_size = rows_size // Z_CHIPS
    y_size = lat_size // CORES
    pieces = tokens // PIECE
    row = lax.axis_index("rows")
    lat = lax.axis_index("lat")
    my_z, my_x = row // x_size, lax.rem(row, x_size)
    my_y, core = lat // CORES, lax.rem(lat, CORES)
    other = 1 - core

    def remote(src, dst, send, recv, to_row, to_lat):
        return pltpu.make_async_remote_copy(
            src_ref=src, dst_ref=dst, send_sem=send, recv_sem=recv,
            device_id=(to_row, to_lat), device_id_type=MESH)

    def peer_row(step):
        return lax.rem(row + step, rows_size)

    def x_row(step):
        return my_z * x_size + lax.rem(my_x + step, x_size)

    def y_peer(step):
        return lax.rem(my_y + step, y_size)

    barrier = pltpu.get_barrier_semaphore()
    for step in range(1, rows_size):
        pl.semaphore_signal(barrier, inc=1, device_id=(peer_row(step), lat), device_id_type=MESH)
    for step in range(1, y_size):
        pl.semaphore_signal(barrier, inc=1, device_id=(row, y_peer(step) * CORES + core), device_id_type=MESH)
    pl.semaphore_signal(barrier, inc=1, device_id=(row, my_y * CORES + other), device_id_type=MESH)

    square = jnp.sum(dec_ref[...] * dec_ref[...], axis=0, keepdims=True)
    part = latents // 8
    for at in range(8):
        facts[pl.ds(at, 1), :] = square[:, at * part : (at + 1) * part]
    facts[8:16, :] = jnp.broadcast_to(jnp.sum(mask_ref[...], keepdims=True), (8, part))
    pl.semaphore_wait(barrier, rows_size + y_size - 1)

    weights = (enc_out, dec_out)

    def weight_rows(z):
        return pl.ds(pl.multiple_of((z * x_size + my_x) * shard, shard), shard)

    def right_copy(hop, which, received=False):
        area = weights[which].at[weight_rows(jnp.maximum(my_z - hop - (1 if received else 0), 0))]
        source = left_ref.at[which] if hop == 1 and not received else area
        return remote(source, area, out_right.at[hop, which], in_left.at[hop, which],
                      jnp.minimum(my_z + 1, Z_CHIPS - 1) * x_size + my_x, lat)

    def left_copy(hop, which, received=False):
        area = weights[which].at[weight_rows(jnp.minimum(my_z + hop + (1 if received else 0), Z_CHIPS - 1))]
        source = right_ref.at[which] if hop == 1 and not received else area
        return remote(source, area, out_left.at[hop, which], in_right.at[hop, which],
                      jnp.maximum(my_z - 1, 0) * x_size + my_x, lat)

    def x_copy(z, which, step, source=None):
        area = weights[which].at[weight_rows(z)]
        return remote(area if source is None else source.at[which], area,
                      out_x.at[z, which, step - 1], in_x.at[z, which, step - 1], x_row(step), lat)

    def place(index, which):
        sources = [(own_ref, row), (left_ref, row - x_size), (right_ref, row + x_size)]
        sources += [(across_ref.at[step - 1], x_row(step)) for step in range(1, x_size)]
        source, owner = sources[index]
        owner = jnp.clip(owner, 0, rows_size - 1)
        return pltpu.make_async_copy(
            source.at[which], weights[which].at[pl.ds(pl.multiple_of(owner * shard, shard), shard)],
            place_sem.at[index, which])

    def place_all(action):
        for which in range(2):
            for index in range(x_size + 2):
                if index == 1:
                    @pl.when(my_z > 0)
                    def _():
                        action(place(1, which))
                elif index == 2:
                    @pl.when(my_z < Z_CHIPS - 1)
                    def _():
                        action(place(2, which))
                else:
                    action(place(index, which))

    def pass_on(hop, which):
        @pl.when(my_z >= hop)
        def _():
            if hop > 1:
                right_copy(hop - 1, which, True).wait_recv()
            if hop < Z_CHIPS - 1:
                @pl.when(my_z < Z_CHIPS - 1)
                def _():
                    right_copy(hop, which).start()
            for step in range(1, x_size):
                x_copy(my_z - hop, which, step, left_ref if hop == 1 else None).start()

        @pl.when(my_z + hop <= Z_CHIPS - 1)
        def _():
            if hop > 1:
                left_copy(hop - 1, which, True).wait_recv()
            if hop < Z_CHIPS - 1:
                @pl.when(my_z > 0)
                def _():
                    left_copy(hop, which).start()
            for step in range(1, x_size):
                x_copy(my_z + hop, which, step, right_ref if hop == 1 else None).start()

    def fact_copy(step):
        return remote(facts, got_facts.at[step - 1], out_fact.at[step - 1], in_fact.at[step - 1], peer_row(step), lat)

    def block_rows(y, which_core, piece):
        return pl.ds(pl.multiple_of((y * CORES + which_core) * tokens + piece * PIECE, PIECE), PIECE)

    def core_copy(step, piece):
        return remote(
            picked_ref.at[block_rows(y_peer(step), other, piece)], from_core.at[step, pl.ds(piece * PIECE, PIECE)],
            out_core.at[step, piece], in_core.at[step, piece], row, my_y * CORES + other)

    def y_copy(step, piece):
        here = pl.ds(piece * PIECE, PIECE)
        return remote(
            from_core.at[step, here], from_y.at[step - 1, here],
            out_y.at[step - 1, piece], in_y.at[step - 1, piece], row, y_peer(step) * CORES + core)

    for piece in range(pieces):
        for step in list(range(1, y_size)) + [0]:
            core_copy(step, piece).start()
    for piece in range(pieces):
        here = pl.ds(piece * PIECE, PIECE)
        for step in list(range(1, y_size)) + [0]:
            core_copy(step, piece).wait_recv()
            total = picked_ref[block_rows(y_peer(step), core, piece), :].astype(f32) + from_core[step, here, :].astype(f32)
            if step == 0:
                base[here, :] = total
            else:
                from_core[step, here, :] = total.astype(bf16)
                y_copy(step, piece).start()

    pass_on(1, 0)
    for step in range(1, rows_size):
        fact_copy(step).start()
    place_all(lambda copy: copy.start())
    pass_on(1, 1)
    pass_on(2, 0)

    def normed(value, gain, shift):
        centred = value - jnp.mean(value, axis=1, keepdims=True)
        spread = jnp.mean(centred * centred, axis=1, keepdims=True)
        return (centred * lax.rsqrt(spread + 1e-05) * gain + shift).astype(bf16)

    def dot(left, right):
        return jnp.dot(left, right, preferred_element_type=f32)

    def rotated(value, rows):
        cosine, low, high = turn_ref[0, rows, :], turn_ref[1, rows, :], turn_ref[2, rows, :]
        parts = []
        for at in range(depth // PAIR):
            tile = value[:, at * PAIR : (at + 1) * PAIR]
            parts.append(
                tile * cosine + pltpu.roll(tile, PAIR - ROT // 2, 1) * low + pltpu.roll(tile, ROT // 2, 1) * high)
        return jnp.concatenate(parts, axis=1)

    for load in loads:
        load.wait()
    for block in range(tokens // ROWS):
        rows = pl.ds(block * ROWS, ROWS)
        for piece in range(block * ROWS // PIECE, (block + 1) * ROWS // PIECE):
            for step in range(1, y_size):
                y_copy(step, piece).wait_recv()
        embedded = base[rows, :]
        for step in range(1, y_size):
            embedded = embedded + from_y[step - 1, rows, :].astype(f32)
        attn_in = normed(embedded, norm_ref[0:1, :], norm_ref[1:2, :])
        joined = dot(attn_in, joined_ref[...]) + bias_ref[:, : 3 * depth]
        queries[rows, :] = (rotated(joined[:, :depth], rows).astype(bf16) * HEAD**-0.5).astype(bf16)
        keys[rows, :] = rotated(joined[:, depth : 2 * depth], rows).astype(bf16)
        values[rows, :] = joined[:, 2 * depth :].astype(bf16)
        mlp_in = normed(embedded, norm_ref[2:3, :], norm_ref[3:4, :])
        inner = dot(mlp_in, mlp_in_ref[...]) + bias_ref[:, 4 * depth : 4 * depth + hidden]
        inner = (0.5 * inner * (1.0 + lax.erf(inner * 0.5**0.5))).astype(bf16)
        base[rows, :] = embedded + (dot(inner, mlp_out_ref[...]) + bias_ref[:, 4 * depth + hidden :])
        if block == 0:
            pass_on(2, 1)
    pass_on(3, 0)

    def own_rows(y, which_core, piece):
        return pl.ds(pl.multiple_of((y * CORES + which_core) * tokens + piece * PIECE, PIECE), PIECE)

    def own_copy(step, piece):
        area = inputs_out.at[own_rows(my_y, core, piece)]
        return remote(ready.at[pl.ds(piece * PIECE, PIECE)], area, out_own.at[step - 1, piece], in_own.at[step - 1, piece], row, y_peer(step) * CORES + core)

    def near_copy(step, piece):
        area = inputs_out.at[own_rows(y_peer(step), core, piece)]
        source = area if step else ready.at[pl.ds(piece * PIECE, PIECE)]
        return remote(source, area, out_near.at[step, piece], in_near.at[step, piece], row, my_y * CORES + other)

    def keep_copy(piece):
        return pltpu.make_async_copy(
            ready.at[pl.ds(piece * PIECE, PIECE)], inputs_out.at[own_rows(my_y, core, piece)], place_sem.at[x_size + 2, piece])

    lanes = lax.broadcasted_iota(jnp.int32, (PIECE, PAIR), 1)
    for piece in range(pieces):
        here = pl.ds(piece * PIECE, PIECE)
        reach = (piece + 1) * PIECE
        visible = (
            lax.broadcasted_iota(jnp.int32, (PIECE, reach), 0) + piece * PIECE
            >= lax.broadcasted_iota(jnp.int32, (PIECE, reach), 1)
        )

        def attend(pair, carry):
            cols = pl.ds(pl.multiple_of(pair * PAIR, PAIR), PAIR)
            both = queries[here, cols]
            found = []
            for first in (True, False):
                chosen = jnp.where((lanes < HEAD) == first, both, jnp.zeros_like(both))
                scores = lax.dot_general(
                    chosen, keys[0:reach, cols], (((1,), (1,)), ((), ())), preferred_element_type=f32)
                scores = jnp.where(visible, scores, -1e30)
                powers = jnp.exp(scores - jnp.max(scores, axis=1, keepdims=True))
                probs = (powers * (1.0 / jnp.sum(powers, axis=1, keepdims=True))).astype(bf16)
                found.append(dot(probs, values[0:reach, cols]))
            context[here, cols] = jnp.where(lanes < HEAD, found[0], found[1]).astype(bf16)
            return carry

        lax.fori_loop(0, depth // PAIR, attend, 0)
        attended = dot(context[here, :], attn_ref[...]) + bias_ref[:, 3 * depth : 4 * depth]
        level = jnp.concatenate([level_ref[here, :]] * (depth // 128), axis=1)
        ready[here, :] = ((base[here, :] + attended) * level).astype(bf16)
        keep_copy(piece).start()
        for step in range(1, y_size):
            own_copy(step, piece).start()
        near_copy(0, piece).start()
        if piece == 1:
            pass_on(3, 1)
        if piece >= 2:
            for step in range(1, y_size):
                own_copy(step, piece - 2).wait_recv()
                near_copy(step, piece - 2).start()

    total = facts[...]
    for step in range(1, rows_size):
        fact_copy(step).wait_recv()
        total = total + got_facts[step - 1]
    count = total[8:9, 0:1]
    norms = jnp.sqrt(total[0:8, :])
    norms = jnp.concatenate([norms[at : at + 1, :] for at in range(8)], axis=1)
    lasso_scale = lasso_coef / count
    norms_out[...] = norms
    lasso_out[...] = lasso_scale * norms
    pull_out[...] = lasso_scale / norms
    scale_out[0:1, :] = jnp.broadcast_to(2.0 / count, (1, depth))
    scale_out[1:8, :] = jnp.broadcast_to(count, (7, depth))
    for piece in range(pieces - 2, pieces):
        for step in range(1, y_size):
            own_copy(step, piece).wait_recv()
            near_copy(step, piece).start()
    place_all(lambda copy: copy.wait())

    for which in range(2):
        for hop in range(1, Z_CHIPS - 1):
            @pl.when((my_z < Z_CHIPS - 1) & (my_z >= hop))
            def _():
                right_copy(hop, which).wait_send()

            @pl.when((my_z > 0) & (my_z + hop <= Z_CHIPS - 1))
            def _():
                left_copy(hop, which).wait_send()

        for z in range(Z_CHIPS):
            @pl.when(z != my_z)
            def _():
                for step in range(1, x_size):
                    x_copy(z, which, step).wait_send()
                    x_copy(z, which, step).wait_recv()
    for step in range(1, rows_size):
        fact_copy(step).wait_send()
    for piece in range(pieces):
        keep_copy(piece).wait()
        for step in range(y_size):
            core_copy(step, piece).wait_send()
            near_copy(step, piece).wait_send()
            near_copy(step, piece).wait_recv()
        for step in range(1, y_size):
            y_copy(step, piece).wait_send()
            own_copy(step, piece).wait_send()


def front(rows_size, lat_size, picked, norm_params, bias_row, w_joined, w_attn_out, w_mlp_in, w_mlp_out,
          turns, level_lanes, mask_tiles, dec_shard, own, left, right, across):
    group, depth = picked.shape
    tokens = group // lat_size
    shard, latents = dec_shard.shape
    x_size = rows_size // Z_CHIPS
    y_size = lat_size // CORES
    pieces = tokens // PIECE
    dma = pltpu.SemaphoreType.DMA
    vmem = pl.BlockSpec(memory_space=pltpu.VMEM)
    hbm = pl.BlockSpec(memory_space=pl.ANY)
    hops = Z_CHIPS - 1
    return pl.pallas_call(
        functools.partial(front_kernel, rows_size, lat_size),
        out_shape=[
            jax.ShapeDtypeStruct((group, depth), bf16),
            jax.ShapeDtypeStruct((depth, latents), bf16),
            jax.ShapeDtypeStruct((depth, latents), bf16),
            jax.ShapeDtypeStruct((1, latents), f32),
            jax.ShapeDtypeStruct((1, latents), f32),
            jax.ShapeDtypeStruct((1, latents), f32),
            jax.ShapeDtypeStruct((8, depth), f32),
        ],
        in_specs=[vmem] * 5 + [hbm] * 6 + [vmem] * 4,
        out_specs=[hbm] * 3 + [vmem] * 4,
        scratch_shapes=[
            pltpu.VMEM((y_size, tokens, depth), bf16),
            pltpu.VMEM((y_size - 1, tokens, depth), bf16),
            pltpu.VMEM((tokens, depth), f32),
            pltpu.VMEM((tokens, depth), bf16),
            pltpu.VMEM((tokens, depth), bf16),
            pltpu.VMEM((tokens, depth), bf16),
            pltpu.VMEM((tokens, depth), bf16),
            pltpu.VMEM((tokens, depth), bf16),
            pltpu.VMEM((16, latents // 8), f32),
            pltpu.VMEM((rows_size - 1, 16, latents // 8), f32),
            *[pltpu.VMEM(a.shape, a.dtype) for a in (w_joined, w_attn_out, w_mlp_in, w_mlp_out, turns, level_lanes)],
            dma((6,)), dma((x_size + 3, max(pieces, 2))),
            dma((hops, 2)), dma((hops, 2)), dma((hops, 2)), dma((hops, 2)),
            dma((Z_CHIPS, 2, x_size - 1)), dma((Z_CHIPS, 2, x_size - 1)),
            dma((rows_size - 1,)), dma((rows_size - 1,)),
            dma((y_size, pieces)), dma((y_size, pieces)),
            dma((y_size - 1, pieces)), dma((y_size - 1, pieces)),
            dma((y_size - 1, pieces)), dma((y_size - 1, pieces)),
            dma((y_size, pieces)), dma((y_size, pieces)),
        ],
        compiler_params=pltpu.CompilerParams(
            collective_id=3, has_side_effects=True, vmem_limit_bytes=60 * 2**20),
        name="front",
    )(picked, norm_params, bias_row, mask_tiles, dec_shard,
      w_joined, w_attn_out, w_mlp_in, w_mlp_out, turns, level_lanes, own, left, right, across)


def turn_tables(length):
    half = ROT // 2
    freqs = np.float32(10000.0) ** (np.float32(-2.0) * np.arange(half, dtype=np.float32) / np.float32(ROT))
    angles = np.arange(length, dtype=np.float32)[:, None] * np.tile(freqs, PAIR // half)[None, :]
    place = np.arange(PAIR) % HEAD
    cosines, sines = np.cos(angles.astype(np.float64)), np.sin(angles.astype(np.float64))
    return np.stack([
        np.where(place < ROT, cosines, 1.0),
        np.where(place < half, -sines, 0.0),
        np.where((place >= half) & (place < ROT), sines, 0.0),
    ]).astype(np.float32)


def softplus_parts(value):
    power = jnp.exp(value)
    grown = jnp.log(1.0 + power)
    grown = jnp.where(power < 2.0**-8, power * (1.0 - 0.5 * power), grown)
    active = jnp.where(value > 30.0, value, grown)
    return active, jnp.exp(value - active)


def forward_kernel(
    lat_size,
    inputs_hbm, enc_hbm, dec_hbm, mask_hbm, enc_bias_ref, dec_bias_ref, scale_ref,
    active_hbm, slope_hbm, mass_out, back_out, stats_out,
    active_buf, slope_buf, product, partial, own, send_two, units_two, recv_one, recv_two, got_two,
    inputs_ref, enc_ref, dec_ref, mask_ref, load_sem,
    active_sem, slope_sem, out_one, in_one, out_two, in_two, outu_two, inu_two, out_three, in_three, out_four, in_four,
):
    tokens, depth = inputs_ref.shape
    latents = enc_ref.shape[1]
    chunk, span = product.shape[1:]
    halves = [pl.ds(at * span, span) for at in range(latents // span)]
    loads = [pltpu.make_async_copy(inputs_hbm, inputs_ref, load_sem.at[0]), pltpu.make_async_copy(mask_hbm, mask_ref, load_sem.at[1])]
    for at, cols in enumerate(halves):
        loads.append(pltpu.make_async_copy(enc_hbm.at[:, cols], enc_ref.at[:, cols], load_sem.at[2 + 2 * at]))
        loads.append(pltpu.make_async_copy(dec_hbm.at[:, cols], dec_ref.at[:, cols], load_sem.at[3 + 2 * at]))
    for load in loads:
        load.start()

    width = active_hbm.shape[2]
    chunks, spans = tokens // chunk, latents // span
    y_size = lat_size // CORES
    share = chunk // lat_size
    strip = 16
    row = lax.axis_index("rows")
    lat = lax.axis_index("lat")
    my_y, core = lat // CORES, lax.rem(lat, CORES)
    other = 1 - core

    def y_peer(step):
        return lax.rem(my_y + step, y_size)

    def share_rows(y, which_core):
        return pl.multiple_of((y * CORES + which_core) * share, share)

    def token_rows(block, y, which_core):
        return pl.ds(pl.multiple_of(block * chunk + (y * CORES + which_core) * share, share), share)

    def remote(src, dst, send, recv, target):
        return pltpu.make_async_remote_copy(
            src_ref=src, dst_ref=dst, send_sem=send, recv_sem=recv,
            device_id=(row, target), device_id_type=MESH)

    def copy_one(block, y):
        slot = lax.rem(block, 2)
        return remote(
            partial.at[slot, pl.ds(share_rows(y, other), share)], recv_one.at[block, y],
            out_one.at[slot, y], in_one.at[block, y], my_y * CORES + other)

    def copies_two(block, step):
        slot = lax.rem(block, 2)
        target = y_peer(step) * CORES + core
        return [
            remote(send_two.at[slot, step - 1], recv_two.at[block, step - 1],
                   out_two.at[slot, step - 1], in_two.at[block, step - 1], target),
            remote(units_two.at[slot, step - 1], got_two.at[block, step - 1],
                   outu_two.at[slot, step - 1], inu_two.at[block, step - 1], target),
        ]

    def copy_three(block, step):
        mine = back_out.at[token_rows(block, my_y, core)]
        return remote(
            mine, mine, out_three.at[block, step - 1], in_three.at[block, step - 1], y_peer(step) * CORES + core)

    def copy_four(block, y):
        mine = back_out.at[token_rows(block, y, core)]
        return remote(mine, mine, out_four.at[block, y], in_four.at[block, y], my_y * CORES + other)

    def stores(block, at, slot):
        rows = pl.ds(pl.multiple_of(block * chunk, chunk), chunk)
        copies = []
        for part in range(span // width):
            lanes = pl.ds(part * width, width)
            copies.append(pltpu.make_async_copy(
                active_buf.at[slot, :, lanes], active_hbm.at[at * (span // width) + part, rows], active_sem.at[slot, part]))
            copies.append(pltpu.make_async_copy(
                slope_buf.at[slot, :, lanes], slope_hbm.at[at * (span // width) + part, rows], slope_sem.at[slot, part]))
        return copies

    barrier = pltpu.get_barrier_semaphore()
    pl.semaphore_signal(barrier, inc=1, device_id=(row, my_y * CORES + other), device_id_type=MESH)
    for step in range(1, y_size):
        pl.semaphore_signal(barrier, inc=1, device_id=(row, y_peer(step) * CORES + core), device_id_type=MESH)
    mass_out[...] = jnp.zeros_like(mass_out)
    stats_out[...] = jnp.zeros_like(stats_out)
    pl.semaphore_wait(barrier, y_size)

    def compute(block):
        place = lax.rem(block, 2)
        first = pl.multiple_of(block * chunk, chunk)

        @pl.when(block >= 2)
        def _():
            for y in range(y_size):
                copy_one(block - 2, y).wait_send()

        for at in range(spans):
            slot = at % 2
            if at >= 2:
                for copy in stores(block, at - 2, slot):
                    copy.wait()
            else:
                @pl.when(block > 0)
                def _():
                    for copy in stores(block - 1, spans - 2 + at, slot):
                        copy.wait()

            @pl.when(block == 0)
            def _():
                for load in loads[2 * at + 2 : 2 * at + 4] + (loads[:2] if at == 0 else []):
                    load.wait()

            product[slot] = jnp.dot(
                inputs_ref[pl.ds(first, chunk), :], enc_ref[:, at * span : (at + 1) * span], preferred_element_type=f32)
            for left in range(0, span, width):
                lanes = pl.ds(left, width)
                cols = pl.ds(at * span + left, width)
                shift = enc_bias_ref[:, cols]
                total = mass_out[:, cols]
                for top in range(0, chunk, strip):
                    rows = pl.ds(top, strip)
                    mask = mask_ref[pl.ds(first + top, strip), :]
                    mask = jnp.concatenate([mask] * (width // 128), axis=1)
                    active, slope = softplus_parts(product[slot, rows, lanes] + shift)
                    active_buf[slot, rows, lanes] = active.astype(bf16)
                    slope_buf[slot, rows, lanes] = slope * mask
                    total = total + (active * mask).reshape(strip // 8, 8, width).sum(0)
                mass_out[:, cols] = total
            for copy in stores(block, at, slot):
                copy.start()
            part = lax.dot_general(
                active_buf[slot], dec_ref[:, at * span : (at + 1) * span], (((1,), (1,)), ((), ())),
                preferred_element_type=f32)
            partial[place] = part if at == 0 else partial[place] + part

    def exchange(block):
        slot = lax.rem(block, 2)
        for y in range(y_size):
            copy_one(block, y).wait_recv()
        for step in list(range(1, y_size)) + [0]:
            y = y_peer(step)
            total = partial[slot, pl.ds(share_rows(y, core), share), :] + recv_one[block, y]
            if step == 0:
                own[slot] = total
            else:
                @pl.when(block >= 2)
                def _():
                    for copy in copies_two(block - 2, step):
                        copy.wait_send()

                code, unit = encode(total)
                send_two[slot, step - 1] = code
                put_units(units_two, (slot, step - 1), unit)
                for copy in copies_two(block, step):
                    copy.start()

    def settle(block):
        slot = lax.rem(block, 2)
        rows = token_rows(block, my_y, core)
        total = own[slot]
        for step in range(1, y_size):
            for copy in copies_two(block, step):
                copy.wait_recv()
            total = total + decode(recv_two[block, step - 1], get_units(got_two, (block, step - 1), depth))
        error = total + dec_bias_ref[...] - inputs_ref[rows, :].astype(f32)
        mask = jnp.concatenate([mask_ref[rows, :]] * (depth // 128), axis=1)
        low = (scale_ref[0:1, :] * mask * error).astype(bf16)
        back_out[rows, :] = low
        stats_out[0:8, :] += (mask * error * error).reshape(share // 8, 8, depth).sum(0)
        stats_out[8:16, :] += low.astype(f32).reshape(share // 8, 8, depth).sum(0)
        for step in range(1, y_size):
            copy_three(block, step).start()

    def spread(block):
        for step in range(1, y_size):
            copy_three(block, step).wait_recv()
        for y in range(y_size):
            copy_four(block, y).start()

    def turn(block, carry):
        @pl.when(block < chunks)
        def _():
            compute(block)
            for y in range(y_size):
                copy_one(block, y).start()

        @pl.when((block >= 1) & (block <= chunks))
        def _():
            exchange(block - 1)

        @pl.when((block >= 2) & (block <= chunks + 1))
        def _():
            settle(block - 2)

        @pl.when(block >= 3)
        def _():
            spread(block - 3)

        return carry

    lax.fori_loop(0, chunks + 3, turn, 0)
    for slot in range(2):
        for copy in stores(chunks - 1, spans - 2 + slot, slot):
            copy.wait()
    for block in range(chunks - 2, chunks):
        for y in range(y_size):
            copy_one(block, y).wait_send()
        for step in range(1, y_size):
            for copy in copies_two(block, step):
                copy.wait_send()

    def drain(block, carry):
        for step in range(1, y_size):
            copy_three(block, step).wait_send()
        for y in range(y_size):
            copy_four(block, y).wait_send()
            copy_four(block, y).wait_recv()
        return carry

    lax.fori_loop(0, chunks, drain, 0)


def forward(lat_size, inputs, enc_low, dec_cols, enc_bias_row, mask_lanes, dec_bias_row, scale_rows):
    tokens, depth = inputs.shape
    latents = enc_low.shape[1]
    chunk, span, width = 512, 1024, (512 if tokens <= 4096 else 256)
    chunks = tokens // chunk
    y_size = lat_size // CORES
    share = chunk // lat_size
    dma = pltpu.SemaphoreType.DMA
    vmem = pl.BlockSpec(memory_space=pltpu.VMEM)
    hbm = pl.BlockSpec(memory_space=pl.ANY)
    return pl.pallas_call(
        functools.partial(forward_kernel, lat_size),
        out_shape=[
            jax.ShapeDtypeStruct((latents // width, tokens, width), bf16),
            jax.ShapeDtypeStruct((latents // width, tokens, width), f32),
            jax.ShapeDtypeStruct((8, latents), f32),
            jax.ShapeDtypeStruct((tokens, depth), bf16),
            jax.ShapeDtypeStruct((16, depth), f32),
        ],
        in_specs=[hbm] * 4 + [vmem] * 3,
        out_specs=[hbm, hbm, vmem, vmem, vmem],
        scratch_shapes=[
            pltpu.VMEM((2, chunk, span), bf16),
            pltpu.VMEM((2, chunk, span), f32),
            pltpu.VMEM((2, chunk, span), f32),
            pltpu.VMEM((2, chunk, depth), f32),
            pltpu.VMEM((2, share, depth), f32),
            pltpu.VMEM((2, y_size - 1, share, depth), jnp.int16),
            pltpu.VMEM((2, y_size - 1, 8, 128), f32),
            pltpu.VMEM((chunks, y_size, share, depth), f32),
            pltpu.VMEM((chunks, y_size - 1, share, depth), jnp.int16),
            pltpu.VMEM((chunks, y_size - 1, 8, 128), f32),
            *[pltpu.VMEM(a.shape, a.dtype) for a in (inputs, enc_low, dec_cols, mask_lanes)],
            dma((2 + 2 * (latents // span),)),
            dma((2, span // width)), dma((2, span // width)),
            dma((2, y_size)), dma((chunks, y_size)),
            dma((2, y_size - 1)), dma((chunks, y_size - 1)),
            dma((2, y_size - 1)), dma((chunks, y_size - 1)),
            dma((chunks, y_size - 1)), dma((chunks, y_size - 1)),
            dma((chunks, y_size)), dma((chunks, y_size)),
        ],
        compiler_params=pltpu.CompilerParams(
            collective_id=1, has_side_effects=True, vmem_limit_bytes=60 * 2**20),
        name="forward",
    )(inputs, enc_low, dec_cols, mask_lanes, enc_bias_row, dec_bias_row, scale_rows)


def encode(value):
    top = jnp.max(jnp.abs(value), axis=0, keepdims=True)
    unit = jnp.where(top > 0.0, 32766.0 / top, 0.0)
    shifted = value * unit + 12582912.0
    return (shifted - 12582912.0).astype(jnp.int32).astype(jnp.int16), top * (1.0 / 32766.0)


def decode(code, unit):
    return code.astype(jnp.int32).astype(f32) * unit


def put_units(ref, index, unit):
    for piece in range(unit.shape[1] // 128):
        ref[index + (pl.ds(piece, 1), slice(None))] = unit[:, piece * 128 : piece * 128 + 128]


def get_units(ref, index, width):
    return jnp.concatenate(
        [ref[index + (pl.ds(piece, 1), slice(None))] for piece in range(width // 128)], axis=1)


def backward_kernel(
    rows_size, lat_size,
    back_ref, norms_ref, lasso_ref, pull_ref, mass_ref, stats_ref,
    inputs_hbm, dec_hbm, master_hbm, active_hbm, slope_hbm,
    enc_out, dec_out, bias_out, center_out, totals_out,
    grad_low, active_buf, slope_buf, sums,
    send_one, units_one, recv_one, got_one,
    send_two, units_two, recv_two, got_two,
    bias_rows, pull_cols, facts, tiles, inputs_ref, dec_ref, master_ref, load_sem,
    active_sem, slope_sem,
    out_one, in_one, outu_one, inu_one, out_two, in_two, outu_two, inu_two, out_facts, in_facts, out_tiles, in_tiles,
):
    blocks, tokens, width = active_hbm.shape
    chunk = slope_buf.shape[1]
    chunks = tokens // chunk
    shard = enc_out.shape[0]
    x_size = rows_size // Z_CHIPS
    row = lax.axis_index("rows")
    lat = lax.axis_index("lat")
    my_z, my_x = row // x_size, lax.rem(row, x_size)

    def x_peer(step):
        return lax.rem(my_x + step, x_size)

    def z_peer(step):
        return lax.rem(my_z + step, Z_CHIPS)

    def active_copy(block):
        slot = lax.rem(block, 2)
        return pltpu.make_async_copy(active_hbm.at[block], active_buf.at[slot], active_sem.at[slot])

    def slope_copy(index):
        slot = lax.rem(index, slope_buf.shape[0])
        return pltpu.make_async_copy(
            slope_hbm.at[index // chunks, pl.ds(pl.multiple_of(lax.rem(index, chunks) * chunk, chunk), chunk)],
            slope_buf.at[slot],
            slope_sem.at[slot],
        )

    def copies(stage, block, which, step):
        slot = lax.rem(block, 2)
        if stage == 0:
            target = (my_z * x_size + x_peer(step), lat)
            refs = (send_one, recv_one, out_one, in_one, units_one, got_one, outu_one, inu_one)
        else:
            target = (z_peer(step) * x_size + my_x, lat)
            refs = (send_two, recv_two, out_two, in_two, units_two, got_two, outu_two, inu_two)
        return [
            pltpu.make_async_remote_copy(
                src_ref=refs[at].at[slot, which, step - 1], dst_ref=refs[at + 1].at[block, which, step - 1],
                send_sem=refs[at + 2].at[slot, which, step - 1], recv_sem=refs[at + 3].at[block, which, step - 1],
                device_id=target, device_id_type=MESH)
            for at in (0, 4)
        ]

    devices = rows_size * lat_size
    me = row * lat_size + lat
    latents = dec_ref.shape[1]
    depth = inputs_ref.shape[1]
    part = latents // 8

    def fact_copy(kind, step):
        area = facts.at[kind, row]
        return pltpu.make_async_remote_copy(
            src_ref=area, dst_ref=area, send_sem=out_facts.at[kind, step], recv_sem=in_facts.at[kind, row],
            device_id=(lax.rem(row + step, rows_size), lat), device_id_type=MESH)

    def fact_arrival(kind, step):
        source = lax.rem(row + step, rows_size)
        area = facts.at[kind, source]
        return pltpu.make_async_remote_copy(
            src_ref=area, dst_ref=area, send_sem=out_facts.at[kind, step], recv_sem=in_facts.at[kind, source],
            device_id=(source, lat), device_id_type=MESH)

    def tile_copy(kind, step):
        area = tiles.at[kind, me]
        target = lax.rem(me + step, devices)
        return pltpu.make_async_remote_copy(
            src_ref=area, dst_ref=area, send_sem=out_tiles.at[kind, step], recv_sem=in_tiles.at[kind, me],
            device_id=(target // lat_size, lax.rem(target, lat_size)), device_id_type=MESH)

    def tile_arrival(kind, step):
        source = lax.rem(me + step, devices)
        area = tiles.at[kind, source]
        return pltpu.make_async_remote_copy(
            src_ref=area, dst_ref=area, send_sem=out_tiles.at[kind, step], recv_sem=in_tiles.at[kind, source],
            device_id=(source // lat_size, lax.rem(source, lat_size)), device_id_type=MESH)

    def over_devices(action):
        def turn(step, carry):
            action(step)
            return carry

        lax.fori_loop(1, devices, turn, 0)

    def share_row(kind, value):
        for at in range(8):
            facts[kind, row, pl.ds(at, 1), :] = value[:, at * part : (at + 1) * part]
        for step in range(1, rows_size):
            fact_copy(kind, step).start()

    def shared_row(kind):
        for step in range(1, rows_size):
            fact_arrival(kind, step).wait_recv()
        total = facts[kind, 0]
        for source in range(1, rows_size):
            total = total + facts[kind, source]
        return jnp.concatenate([total[at : at + 1, :] for at in range(8)], axis=1)

    def share_tile(kind, value):
        tiles[kind, me] = value

        def start(step):
            tile_copy(kind, step).start()

        over_devices(start)

    def shared_tile(kind):
        def wait(step):
            tile_arrival(kind, step).wait_recv()

        over_devices(wait)
        return lax.fori_loop(1, devices, lambda source, total: total + tiles[kind, source], tiles[kind, 0])

    barrier = pltpu.get_barrier_semaphore()

    def greet(step):
        target = lax.rem(me + step, devices)
        pl.semaphore_signal(
            barrier, inc=1, device_id=(target // lat_size, lax.rem(target, lat_size)), device_id_type=MESH)

    over_devices(greet)
    loads = [
        pltpu.make_async_copy(source, target, load_sem.at[at])
        for at, (source, target) in enumerate(((dec_hbm, dec_ref), (inputs_hbm, inputs_ref), (master_hbm, master_ref)))
    ]
    active_copy(0).start()
    for load in loads:
        load.start()
    ahead = slope_buf.shape[0] - 1
    for index in range(ahead):
        slope_copy(index).start()
    pl.semaphore_wait(barrier, devices - 1)
    share_row(0, jnp.sum(mass_ref[...], axis=0, keepdims=True))
    center = jnp.sum(stats_ref[8:16, :], axis=0, keepdims=True)
    square = jnp.sum(stats_ref[0:8, :], keepdims=True)
    quarter = depth // 4
    share_tile(0, jnp.concatenate(
        [center[:, at * quarter : (at + 1) * quarter] for at in range(4)]
        + [jnp.broadcast_to(square, (4, quarter))], axis=0))

    def columns(block):
        return pl.ds(pl.multiple_of(block * width, width), width)

    over_tokens = (((0,), (0,)), ((), ()))

    def compute_dec(block):
        slot = lax.rem(block, 2)

        @pl.when(block + 1 < blocks)
        def _():
            active_copy(block + 1).start()

        active_copy(block).wait()
        sums[slot, 1] = lax.dot_general(back_ref[...], active_buf[slot], over_tokens, preferred_element_type=f32)

    def compute_enc(block):
        slot = lax.rem(block, 2)
        cols = columns(block)

        @pl.when(block == 0)
        def _():
            for load in loads:
                load.wait()

        def piece(index, total):
            at = block * chunks + index

            @pl.when(at + ahead < blocks * chunks)
            def _():
                slope_copy(at + ahead).start()

            slope_copy(at).wait()
            rows = pl.ds(pl.multiple_of(index * chunk, chunk), chunk)
            back = jnp.dot(back_ref[rows, :], dec_ref[:, cols], preferred_element_type=f32)
            low = ((back + lasso_ref[:, cols]) * slope_buf[lax.rem(at, ahead + 1)]).astype(bf16)
            grad_low[rows, :] = low
            return total + low.astype(f32).reshape(chunk // 8, 8, width).sum(0)

        bias_rows[:, cols] = lax.fori_loop(0, chunks, piece, jnp.zeros((8, width), f32))
        sums[slot, 0] = lax.dot_general(inputs_ref[...], grad_low[...], over_tokens, preferred_element_type=f32)

    def send_x(block, which):
        slot = lax.rem(block, 2)
        for step in range(1, x_size):
            @pl.when(block >= 2)
            def _():
                for copy in copies(0, block - 2, which, step):
                    copy.wait_send()

            parts = []
            for z in range(Z_CHIPS):
                first = pl.multiple_of((z * x_size + x_peer(step)) * shard, shard)
                parts.append(sums[slot, which, pl.ds(first, shard), :])
            code, unit = encode(jnp.concatenate(parts, axis=0))
            for z in range(Z_CHIPS):
                send_one[slot, which, step - 1, z] = code[z * shard : (z + 1) * shard]
            put_units(units_one, (slot, which, step - 1), unit)
            for copy in copies(0, block, which, step):
                copy.start()

    def send_z(block, which):
        slot = lax.rem(block, 2)
        for step in range(1, x_size):
            for copy in copies(0, block, which, step):
                copy.wait_recv()
        for step in range(Z_CHIPS):
            z = z_peer(step)
            if step:
                @pl.when(block >= 2)
                def _():
                    for copy in copies(1, block - 2, which, step):
                        copy.wait_send()

            first = pl.multiple_of((z * x_size + my_x) * shard, shard)
            total = sums[slot, which, pl.ds(first, shard), :]
            for x_step in range(1, x_size):
                total = total + decode(
                    recv_one[block, which, x_step - 1, z], get_units(got_one, (block, which, x_step - 1), width))
            if step == 0:
                (enc_out, dec_out)[which][:, columns(block)] = total
            else:
                code, unit = encode(total)
                send_two[slot, which, step - 1] = code
                put_units(units_two, (slot, which, step - 1), unit)
                for copy in copies(1, block, which, step):
                    copy.start()

    def finish(block, which):
        slot = lax.rem(block, 2)
        for step in range(1, Z_CHIPS):
            for copy in copies(1, block, which, step):
                copy.wait_recv()
        out, cols = (enc_out, dec_out)[which], columns(block)
        total = out[:, cols]
        for step in range(1, Z_CHIPS):
            total = total + decode(
                recv_two[block, which, step - 1], get_units(got_two, (block, which, step - 1), width))
        out[:, cols] = total

    def turn(block, carry):
        for which, compute in ((1, compute_dec), (0, compute_enc)):
            @pl.when(block < blocks)
            def _():
                compute(block)
                send_x(block, which)

            @pl.when((block >= 1) & (block <= blocks))
            def _():
                send_z(block - 1, which)

            @pl.when(block >= 2)
            def _():
                finish(block - 2, which)

        return carry

    lax.fori_loop(0, blocks, turn, 0)
    share_row(1, jnp.sum(bias_rows[...], axis=0, keepdims=True))
    lax.fori_loop(blocks, blocks + 2, turn, 0)

    mass = shared_row(0)
    bias = shared_row(1)
    bias_out[...] = bias
    pull = mass * pull_ref[...]

    def squares(block, total):
        cols = columns(block)
        gain = dec_out[:, cols] + pull_cols[:, cols] * master_ref[:, cols]
        dec_out[:, cols] = gain
        other = enc_out[:, cols]
        return total + gain * gain + other * other

    pull_cols[...] = pull
    total = jnp.sum(lax.fori_loop(0, blocks, squares, jnp.zeros((shard, width), f32)), keepdims=True)
    leads = jnp.where(row == 0, 1.0, 0.0)
    total = total + leads * jnp.sum(bias * bias, keepdims=True)
    lasso = leads * lasso_coef * jnp.sum(mass * norms_ref[...], keepdims=True)
    share_tile(1, jnp.concatenate(
        [jnp.broadcast_to(total, (4, quarter)), jnp.broadcast_to(lasso, (4, quarter))], axis=0))
    first = shared_tile(0)
    center = jnp.concatenate([first[at : at + 1, :] for at in range(4)], axis=1)
    center_out[...] = center
    second = shared_tile(1)
    squared = second[0:4, :] + jnp.sum(center * center, keepdims=True)
    totals_out[...] = jnp.concatenate([squared, first[4:8, :] + second[4:8, :]], axis=0)
    for kind in range(2):
        for step in range(1, rows_size):
            fact_copy(kind, step).wait_send()

        def sent(step, kind=kind):
            tile_copy(kind, step).wait_send()

        over_devices(sent)
    for block in range(max(blocks - 2, 0), blocks):
        for which in range(2):
            for stage, size in ((0, x_size), (1, Z_CHIPS)):
                for step in range(1, size):
                    for copy in copies(stage, block, which, step):
                        copy.wait_send()


def backward(rows_size, lat_size, inputs, back, dec_cols, norms_row, lasso_row, pull_row, mass_rows, stats, master,
             active, slope):
    blocks, tokens, width = active.shape
    depth = inputs.shape[1]
    shard = depth // rows_size
    latents = dec_cols.shape[1]
    x_size = rows_size // Z_CHIPS
    devices = rows_size * lat_size
    chunk = min(CHUNK, tokens)
    i16 = jnp.int16
    dma = pltpu.SemaphoreType.DMA
    vmem = pl.BlockSpec(memory_space=pltpu.VMEM)
    hbm = pl.BlockSpec(memory_space=pl.ANY)
    return pl.pallas_call(
        functools.partial(backward_kernel, rows_size, lat_size),
        out_shape=[
            jax.ShapeDtypeStruct((shard, latents), f32),
            jax.ShapeDtypeStruct((shard, latents), f32),
            jax.ShapeDtypeStruct((1, latents), f32),
            jax.ShapeDtypeStruct((1, depth), f32),
            jax.ShapeDtypeStruct((8, 128), f32),
        ],
        in_specs=[vmem] * 6 + [hbm] * 5,
        out_specs=[vmem] * 5,
        scratch_shapes=[
            pltpu.VMEM((tokens, width), bf16),
            pltpu.VMEM((2, tokens, width), bf16),
            pltpu.VMEM((SLOTS, chunk, width), f32),
            pltpu.VMEM((2, 2, depth, width), f32),
            pltpu.VMEM((2, 2, x_size - 1, Z_CHIPS, shard, width), i16),
            pltpu.VMEM((2, 2, x_size - 1, 8, 128), f32),
            pltpu.VMEM((blocks, 2, x_size - 1, Z_CHIPS, shard, width), i16),
            pltpu.VMEM((blocks, 2, x_size - 1, 8, 128), f32),
            pltpu.VMEM((2, 2, Z_CHIPS - 1, shard, width), i16),
            pltpu.VMEM((2, 2, Z_CHIPS - 1, 8, 128), f32),
            pltpu.VMEM((blocks, 2, Z_CHIPS - 1, shard, width), i16),
            pltpu.VMEM((blocks, 2, Z_CHIPS - 1, 8, 128), f32),
            pltpu.VMEM((8, latents), f32),
            pltpu.VMEM((1, latents), f32),
            pltpu.VMEM((2, rows_size, 8, latents // 8), f32),
            pltpu.VMEM((2, devices, 8, 128), f32),
            *[pltpu.VMEM(a.shape, a.dtype) for a in (inputs, dec_cols, master)],
            dma((3,)),
            dma((2,)), dma((SLOTS,)),
            dma((2, 2, x_size - 1)), dma((blocks, 2, x_size - 1)),
            dma((2, 2, x_size - 1)), dma((blocks, 2, x_size - 1)),
            dma((2, 2, Z_CHIPS - 1)), dma((blocks, 2, Z_CHIPS - 1)),
            dma((2, 2, Z_CHIPS - 1)), dma((blocks, 2, Z_CHIPS - 1)),
            dma((2, rows_size)), dma((2, rows_size)), dma((2, devices)), dma((2, devices)),
        ],
        compiler_params=pltpu.CompilerParams(
            collective_id=2, has_side_effects=True, vmem_limit_bytes=61 * 2**20),
        name="backward",
    )(back, norms_row, lasso_row, pull_row, mass_rows, stats, inputs, dec_cols, master, active, slope)


def update_kernel(
    totals_ref, counts_ref, enc_grad, dec_grad, enc_bias_grad, dec_bias_grad,
    enc_w, enc_m, enc_s, dec_w, dec_m, dec_s, enc_b, enc_bm, enc_bs, dec_b, dec_bm, dec_bs,
    enc_w_out, enc_m_out, enc_s_out, dec_w_out, dec_m_out, dec_s_out,
    enc_b_out, enc_bm_out, enc_bs_out, dec_b_out, dec_bm_out, dec_bs_out, scalars_out,
):
    norm = jnp.sqrt(totals_ref[0:1, 0:1])
    factor = clip_bound / jnp.maximum(norm, clip_bound)
    groups = (
        (enc_grad, (enc_w, enc_m, enc_s), (enc_w_out, enc_m_out, enc_s_out), weight_decay),
        (dec_grad, (dec_w, dec_m, dec_s), (dec_w_out, dec_m_out, dec_s_out), weight_decay),
        (enc_bias_grad, (enc_b, enc_bm, enc_bs), (enc_b_out, enc_bm_out, enc_bs_out), 0.0),
        (dec_bias_grad, (dec_b, dec_bm, dec_bs), (dec_b_out, dec_bm_out, dec_bs_out), 0.0),
    )
    for grad, olds, news, decay in groups:
        found = adam_update(*[old[...] for old in olds], grad[...] * factor, decay)
        for new, value in zip(news, found):
            new[...] = value
    scalars_out[0:1, :] = jnp.broadcast_to(norm, (1, 128))
    scalars_out[1:2, :] = totals_ref[4:5, :]
    scalars_out[2:8, :] = counts_ref[2:8, :]


def update(totals, counts, grads, states):
    shard, latents = grads[0].shape
    depth = grads[3].shape[1]
    span = latents // 4
    wide = pl.BlockSpec((shard, span), lambda i: (0, i))
    row = pl.BlockSpec((1, span), lambda i: (0, i))
    short = pl.BlockSpec((1, depth), lambda i: (0, 0))
    tile = pl.BlockSpec((8, 128), lambda i: (0, 0))
    state_specs = [wide] * 6 + [row] * 3 + [short] * 3
    return pl.pallas_call(
        update_kernel,
        grid=(latents // span,),
        out_shape=[jax.ShapeDtypeStruct(a.shape, f32) for a in states] + [jax.ShapeDtypeStruct((8, 128), f32)],
        in_specs=[tile, tile, wide, wide, row, short] + state_specs,
        out_specs=state_specs + [tile],
        compiler_params=pltpu.CompilerParams(vmem_limit_bytes=61 * 2**20),
        name="update",
    )(totals, counts, *grads, *states)


def body(
    token_ids,
    token_mask,
    scale_index,
    embed,
    norm_params,
    frozen_bias,
    w_joined,
    w_attn_out,
    w_mlp_in,
    w_mlp_out,
    enc_weight,
    enc_moment,
    enc_second,
    dec_weight,
    dec_moment,
    dec_second,
    enc_bias,
    enc_bias_moment,
    enc_bias_second,
    dec_bias,
    dec_bias_moment,
    dec_bias_second,
):
    lat_size = lax.axis_size("lat")
    lat_index = lax.axis_index("lat")
    group_tokens = token_ids.shape[0]
    tok_local = group_tokens // lat_size
    rows_size = lax.axis_size("rows")
    depth = enc_weight.shape[0] * rows_size
    mask_float = token_mask.astype(f32)
    dec_master = dec_weight.T
    bias_row = frozen_bias[None, :]
    vocab_local = embed.shape[0]
    vocab_first = lat_index * vocab_local
    local_ids = token_ids - vocab_first
    inside = (local_ids >= 0) & (local_ids < vocab_local)
    picked = jnp.take(embed, jnp.clip(local_ids, 0, vocab_local - 1), axis=0)
    picked = jnp.where(inside[:, None], picked, jnp.zeros((), bf16))
    own = jnp.stack([enc_weight.astype(bf16), dec_master.astype(bf16)])
    x_size = rows_size // Z_CHIPS
    right_pairs = [(i, i + x_size) for i in range(rows_size - x_size)]
    left_pairs = [(i + x_size, i) for i in range(rows_size - x_size)]
    from_left = lax.ppermute(own, "rows", right_pairs)
    from_right = lax.ppermute(own, "rows", left_pairs)
    across = []
    for step in range(1, x_size):
        pairs = [(i // x_size * x_size + (i + step) % x_size, i) for i in range(rows_size)]
        across.append(lax.ppermute(own, "rows", pairs))
    own_first = lat_index * tok_local
    scales = 0.5 + 0.25 * lax.dynamic_slice_in_dim(scale_index, own_first, tok_local).astype(f32)
    level_lanes = jnp.broadcast_to(scales[:, None], (tok_local, 128))
    mask_lanes = jnp.broadcast_to(mask_float[:, None], (group_tokens, 128))
    all_inputs, enc_low, dec_cols, norms_row, lasso_row, pull_row, scale_rows = front(
        rows_size, lat_size, picked, norm_params, bias_row, w_joined, w_attn_out, w_mlp_in, w_mlp_out,
        turn_tables(tok_local), level_lanes, mask_float.reshape(-1, 128), dec_master,
        own, from_left, from_right, jnp.stack(across))
    active, slope, mass_rows, recon_grad, stats = forward(
        lat_size, all_inputs, enc_low, dec_cols, enc_bias[None, :], mask_lanes, dec_bias[None, :], scale_rows)
    grad_enc, grad_dec, bias_total, center, totals = backward(
        rows_size, lat_size, all_inputs, recon_grad, dec_cols, norms_row, lasso_row, pull_row, mass_rows, stats, dec_master, active, slope)
    states = [
        enc_weight, enc_moment, enc_second, dec_master, dec_moment.T, dec_second.T,
        enc_bias[None, :], enc_bias_moment[None, :], enc_bias_second[None, :],
        dec_bias[None, :], dec_bias_moment[None, :], dec_bias_second[None, :],
    ]
    *fresh, scalars = update(totals, scale_rows, (grad_enc, grad_dec, bias_total, center), states)
    return (
        *fresh[:3],
        *[value.T for value in fresh[3:6]],
        *[value[0] for value in fresh[6:]],
        scalars[0, 0],
        scalars[1, 0],
        scalars[2, 0],
    )


def solution(mesh):
    placed = (
        P("rows"),
        P("rows"),
        P("rows"),
        P("lat", None),
        P(),
        P(),
        P(),
        P(),
        P(),
        P(),
        P("rows", "lat"),
        P("rows", "lat"),
        P("rows", "lat"),
        P("lat", "rows"),
        P("lat", "rows"),
        P("lat", "rows"),
        P("lat"),
        P("lat"),
        P("lat"),
        P(),
        P(),
        P(),
    )
    return jax.shard_map(
        body,
        mesh=mesh,
        in_specs=placed,
        out_specs=(
            P("rows", "lat"),
            P("rows", "lat"),
            P("rows", "lat"),
            P("lat", "rows"),
            P("lat", "rows"),
            P("lat", "rows"),
            P("lat"),
            P("lat"),
            P("lat"),
            P(),
            P(),
            P(),
            P(),
            P(),
            P(),
        ),
        check_vma=False,
    )
```

```python
import functools
import jax
import jax.numpy as jnp
import numpy as np
from jax import lax
from jax.experimental import pallas as pl
from jax.experimental.pallas import tpu as pltpu
from jax.sharding import PartitionSpec as P

HEADS = 8
ROT = 16
STEP = 10
Z_CHIPS = 4
CORES = 2
SLOTS = 6
CHUNK = 1024
MESH = pl.DeviceIdType.MESH
f32 = jnp.float32
bf16 = jnp.bfloat16


lasso_coef = 5.0
clip_bound = 1.0
learn_rate = 0.03
beta_one = 0.9
beta_two = 0.999
adam_eps = 1e-08
weight_decay = 0.01


def adam_update(weight, moment, second, grad, decay):
    moment_new = beta_one * moment + (1.0 - beta_one) * grad
    second_new = beta_two * second + (1.0 - beta_two) * grad * grad
    corrected = moment_new / (1.0 - beta_one**STEP)
    scaled = jnp.sqrt(second_new / (1.0 - beta_two**STEP)) + adam_eps
    weight_new = weight - learn_rate * (corrected / scaled + decay * weight)
    return (weight_new, moment_new, second_new)


ROWS = 512
PIECE = 256
HEAD = 64
PAIR = 128


def front_kernel(
    rows_size, lat_size,
    picked_ref, norm_ref, bias_ref, mask_ref, dec_ref,
    joined_hbm, attn_hbm, mlp_in_hbm, mlp_out_hbm, turn_hbm, code_hbm, own_ref, left_ref, right_ref, across_ref,
    inputs_out, enc_out, dec_out, norms_out, lasso_out, pull_out, scale_out,
    from_core, from_y, base, queries, keys, values, context, ready, facts, got_facts,
    joined_ref, attn_ref, mlp_in_ref, mlp_out_ref, turn_ref, code_ref,
    load_sem, place_sem,
    out_right, in_left, out_left, in_right, out_x, in_x, out_fact, in_fact,
    out_core, in_core, out_y, in_y, out_own, in_own, out_near, in_near,
):
    tokens, depth = base.shape
    shard, latents = dec_ref.shape
    hidden = mlp_in_ref.shape[1]
    loads = [
        pltpu.make_async_copy(source, target, load_sem.at[at])
        for at, (source, target) in enumerate((
            (code_hbm, code_ref), (joined_hbm, joined_ref), (turn_hbm, turn_ref), (mlp_in_hbm, mlp_in_ref),
            (mlp_out_hbm, mlp_out_ref), (attn_hbm, attn_ref)))
    ]
    for load in loads:
        load.start()
    x_size = rows_size // Z_CHIPS
    y_size = lat_size // CORES
    pieces = tokens // PIECE
    row = lax.axis_index("rows")
    lat = lax.axis_index("lat")
    my_z, my_x = row // x_size, lax.rem(row, x_size)
    my_y, core = lat // CORES, lax.rem(lat, CORES)
    other = 1 - core

    def remote(src, dst, send, recv, to_row, to_lat):
        return pltpu.make_async_remote_copy(
            src_ref=src, dst_ref=dst, send_sem=send, recv_sem=recv,
            device_id=(to_row, to_lat), device_id_type=MESH)

    def peer_row(step):
        return lax.rem(row + step, rows_size)

    def x_row(step):
        return my_z * x_size + lax.rem(my_x + step, x_size)

    def y_peer(step):
        return lax.rem(my_y + step, y_size)

    barrier = pltpu.get_barrier_semaphore()
    for step in range(1, rows_size):
        pl.semaphore_signal(barrier, inc=1, device_id=(peer_row(step), lat), device_id_type=MESH)
    for step in range(1, y_size):
        pl.semaphore_signal(barrier, inc=1, device_id=(row, y_peer(step) * CORES + core), device_id_type=MESH)
    pl.semaphore_signal(barrier, inc=1, device_id=(row, my_y * CORES + other), device_id_type=MESH)

    square = jnp.sum(dec_ref[...] * dec_ref[...], axis=0, keepdims=True)
    part = latents // 8
    for at in range(8):
        facts[pl.ds(at, 1), :] = square[:, at * part : (at + 1) * part]
    facts[8:16, :] = jnp.broadcast_to(jnp.sum(mask_ref[...], keepdims=True), (8, part))
    pl.semaphore_wait(barrier, rows_size + y_size - 1)

    weights = (enc_out, dec_out)

    def weight_rows(z):
        return pl.ds(pl.multiple_of((z * x_size + my_x) * shard, shard), shard)

    def right_copy(hop, which, received=False):
        area = weights[which].at[weight_rows(jnp.maximum(my_z - hop - (1 if received else 0), 0))]
        source = left_ref.at[which] if hop == 1 and not received else area
        return remote(source, area, out_right.at[hop, which], in_left.at[hop, which],
                      jnp.minimum(my_z + 1, Z_CHIPS - 1) * x_size + my_x, lat)

    def left_copy(hop, which, received=False):
        area = weights[which].at[weight_rows(jnp.minimum(my_z + hop + (1 if received else 0), Z_CHIPS - 1))]
        source = right_ref.at[which] if hop == 1 and not received else area
        return remote(source, area, out_left.at[hop, which], in_right.at[hop, which],
                      jnp.maximum(my_z - 1, 0) * x_size + my_x, lat)

    def x_copy(z, which, step, source=None):
        area = weights[which].at[weight_rows(z)]
        return remote(area if source is None else source.at[which], area,
                      out_x.at[z, which, step - 1], in_x.at[z, which, step - 1], x_row(step), lat)

    def place(index, which):
        sources = [(own_ref, row), (left_ref, row - x_size), (right_ref, row + x_size)]
        sources += [(across_ref.at[step - 1], x_row(step)) for step in range(1, x_size)]
        source, owner = sources[index]
        owner = jnp.clip(owner, 0, rows_size - 1)
        return pltpu.make_async_copy(
            source.at[which], weights[which].at[pl.ds(pl.multiple_of(owner * shard, shard), shard)],
            place_sem.at[index, which])

    def place_all(action):
        for which in range(2):
            for index in range(x_size + 2):
                if index == 1:
                    @pl.when(my_z > 0)
                    def _():
                        action(place(1, which))
                elif index == 2:
                    @pl.when(my_z < Z_CHIPS - 1)
                    def _():
                        action(place(2, which))
                else:
                    action(place(index, which))

    def pass_on(hop, which):
        @pl.when(my_z >= hop)
        def _():
            if hop > 1:
                right_copy(hop - 1, which, True).wait_recv()
            if hop < Z_CHIPS - 1:
                @pl.when(my_z < Z_CHIPS - 1)
                def _():
                    right_copy(hop, which).start()
            for step in range(1, x_size):
                x_copy(my_z - hop, which, step, left_ref if hop == 1 else None).start()

        @pl.when(my_z + hop <= Z_CHIPS - 1)
        def _():
            if hop > 1:
                left_copy(hop - 1, which, True).wait_recv()
            if hop < Z_CHIPS - 1:
                @pl.when(my_z > 0)
                def _():
                    left_copy(hop, which).start()
            for step in range(1, x_size):
                x_copy(my_z + hop, which, step, right_ref if hop == 1 else None).start()

    def fact_copy(step):
        return remote(facts, got_facts.at[step - 1], out_fact.at[step - 1], in_fact.at[step - 1], peer_row(step), lat)

    def block_rows(y, which_core, piece):
        return pl.ds(pl.multiple_of((y * CORES + which_core) * tokens + piece * PIECE, PIECE), PIECE)

    def core_copy(step, piece):
        return remote(
            picked_ref.at[block_rows(y_peer(step), other, piece)], from_core.at[step, pl.ds(piece * PIECE, PIECE)],
            out_core.at[step, piece], in_core.at[step, piece], row, my_y * CORES + other)

    def y_copy(step, piece):
        here = pl.ds(piece * PIECE, PIECE)
        return remote(
            from_core.at[step, here], from_y.at[step - 1, here],
            out_y.at[step - 1, piece], in_y.at[step - 1, piece], row, y_peer(step) * CORES + core)

    for piece in range(pieces):
        for step in list(range(1, y_size)) + [0]:
            core_copy(step, piece).start()
    def code_rows(y, piece):
        code = code_ref[pl.ds(pl.multiple_of(y * tokens + piece * PIECE, PIECE), PIECE), :]
        return jnp.concatenate([code] * (depth // 128), axis=1)

    loads[0].wait()
    for piece in range(pieces):
        here = pl.ds(piece * PIECE, PIECE)
        for step in list(range(1, y_size)) + [0]:
            holder = lax.shift_right_logical(code_rows(y_peer(step), piece), 4)
            core_copy(step, piece).wait_recv()
            total = jnp.where(
                holder == lat, picked_ref[block_rows(y_peer(step), core, piece), :].astype(f32),
                jnp.where(holder == my_y * CORES + other, from_core[step, here, :].astype(f32), 0.0))
            if step == 0:
                base[here, :] = total
            else:
                from_core[step, here, :] = total.astype(bf16)
                y_copy(step, piece).start()

    pass_on(1, 0)
    for step in range(1, rows_size):
        fact_copy(step).start()
    place_all(lambda copy: copy.start())
    pass_on(1, 1)
    pass_on(2, 0)

    def normed(value, gain, shift):
        centred = value - jnp.mean(value, axis=1, keepdims=True)
        spread = jnp.mean(centred * centred, axis=1, keepdims=True)
        return (centred * lax.rsqrt(spread + 1e-05) * gain + shift).astype(bf16)

    def dot(left, right):
        return jnp.dot(left, right, preferred_element_type=f32)

    def rotated(value, rows):
        cosine, low, high = turn_ref[0, rows, :], turn_ref[1, rows, :], turn_ref[2, rows, :]
        parts = []
        for at in range(depth // PAIR):
            tile = value[:, at * PAIR : (at + 1) * PAIR]
            parts.append(
                tile * cosine + pltpu.roll(tile, PAIR - ROT // 2, 1) * low + pltpu.roll(tile, ROT // 2, 1) * high)
        return jnp.concatenate(parts, axis=1)

    for load in loads[1:]:
        load.wait()
    for block in range(tokens // ROWS):
        rows = pl.ds(block * ROWS, ROWS)
        for piece in range(block * ROWS // PIECE, (block + 1) * ROWS // PIECE):
            for step in range(1, y_size):
                y_copy(step, piece).wait_recv()
        embedded = base[rows, :]
        for step in range(1, y_size):
            embedded = embedded + from_y[step - 1, rows, :].astype(f32)
        attn_in = normed(embedded, norm_ref[0:1, :], norm_ref[1:2, :])
        joined = dot(attn_in, joined_ref[...]) + bias_ref[:, : 3 * depth]
        queries[rows, :] = (rotated(joined[:, :depth], rows).astype(bf16) * HEAD**-0.5).astype(bf16)
        keys[rows, :] = rotated(joined[:, depth : 2 * depth], rows).astype(bf16)
        values[rows, :] = joined[:, 2 * depth :].astype(bf16)
        mlp_in = normed(embedded, norm_ref[2:3, :], norm_ref[3:4, :])
        inner = dot(mlp_in, mlp_in_ref[...]) + bias_ref[:, 4 * depth : 4 * depth + hidden]
        inner = (0.5 * inner * (1.0 + lax.erf(inner * 0.5**0.5))).astype(bf16)
        base[rows, :] = embedded + (dot(inner, mlp_out_ref[...]) + bias_ref[:, 4 * depth + hidden :])
        if block == 0:
            pass_on(2, 1)
    pass_on(3, 0)

    def own_rows(y, which_core, piece):
        return pl.ds(pl.multiple_of((y * CORES + which_core) * tokens + piece * PIECE, PIECE), PIECE)

    def own_copy(step, piece):
        area = inputs_out.at[own_rows(my_y, core, piece)]
        return remote(ready.at[pl.ds(piece * PIECE, PIECE)], area, out_own.at[step - 1, piece], in_own.at[step - 1, piece], row, y_peer(step) * CORES + core)

    def near_copy(step, piece):
        area = inputs_out.at[own_rows(y_peer(step), core, piece)]
        source = area if step else ready.at[pl.ds(piece * PIECE, PIECE)]
        return remote(source, area, out_near.at[step, piece], in_near.at[step, piece], row, my_y * CORES + other)

    def keep_copy(piece):
        return pltpu.make_async_copy(
            ready.at[pl.ds(piece * PIECE, PIECE)], inputs_out.at[own_rows(my_y, core, piece)], place_sem.at[x_size + 2, piece])

    lanes = lax.broadcasted_iota(jnp.int32, (PIECE, PAIR), 1)
    for piece in range(pieces):
        here = pl.ds(piece * PIECE, PIECE)
        reach = (piece + 1) * PIECE
        visible = (
            lax.broadcasted_iota(jnp.int32, (PIECE, reach), 0) + piece * PIECE
            >= lax.broadcasted_iota(jnp.int32, (PIECE, reach), 1)
        )

        def attend(pair, carry):
            cols = pl.ds(pl.multiple_of(pair * PAIR, PAIR), PAIR)
            both = queries[here, cols]
            found = []
            for first in (True, False):
                chosen = jnp.where((lanes < HEAD) == first, both, jnp.zeros_like(both))
                scores = lax.dot_general(
                    chosen, keys[0:reach, cols], (((1,), (1,)), ((), ())), preferred_element_type=f32)
                scores = jnp.where(visible, scores, -1e30)
                powers = jnp.exp(scores - jnp.max(scores, axis=1, keepdims=True))
                probs = (powers * (1.0 / jnp.sum(powers, axis=1, keepdims=True))).astype(bf16)
                found.append(dot(probs, values[0:reach, cols]))
            context[here, cols] = jnp.where(lanes < HEAD, found[0], found[1]).astype(bf16)
            return carry

        lax.fori_loop(0, depth // PAIR, attend, 0)
        attended = dot(context[here, :], attn_ref[...]) + bias_ref[:, 3 * depth : 4 * depth]
        level = 0.5 + 0.25 * (code_rows(my_y, piece) & 15).astype(f32)
        ready[here, :] = ((base[here, :] + attended) * level).astype(bf16)
        keep_copy(piece).start()
        for step in range(1, y_size):
            own_copy(step, piece).start()
        near_copy(0, piece).start()
        if piece == 1:
            pass_on(3, 1)
        if piece >= 2:
            for step in range(1, y_size):
                own_copy(step, piece - 2).wait_recv()
                near_copy(step, piece - 2).start()

    total = facts[...]
    for step in range(1, rows_size):
        fact_copy(step).wait_recv()
        total = total + got_facts[step - 1]
    count = total[8:9, 0:1]
    norms = jnp.sqrt(total[0:8, :])
    norms = jnp.concatenate([norms[at : at + 1, :] for at in range(8)], axis=1)
    lasso_scale = lasso_coef / count
    norms_out[...] = norms
    lasso_out[...] = lasso_scale * norms
    pull_out[...] = lasso_scale / norms
    scale_out[0:1, :] = jnp.broadcast_to(2.0 / count, (1, depth))
    scale_out[1:8, :] = jnp.broadcast_to(count, (7, depth))
    for piece in range(pieces - 2, pieces):
        for step in range(1, y_size):
            own_copy(step, piece).wait_recv()
            near_copy(step, piece).start()
    place_all(lambda copy: copy.wait())

    for which in range(2):
        for hop in range(1, Z_CHIPS - 1):
            @pl.when((my_z < Z_CHIPS - 1) & (my_z >= hop))
            def _():
                right_copy(hop, which).wait_send()

            @pl.when((my_z > 0) & (my_z + hop <= Z_CHIPS - 1))
            def _():
                left_copy(hop, which).wait_send()

        for z in range(Z_CHIPS):
            @pl.when(z != my_z)
            def _():
                for step in range(1, x_size):
                    x_copy(z, which, step).wait_send()
                    x_copy(z, which, step).wait_recv()
    for step in range(1, rows_size):
        fact_copy(step).wait_send()
    for piece in range(pieces):
        keep_copy(piece).wait()
        for step in range(y_size):
            core_copy(step, piece).wait_send()
            near_copy(step, piece).wait_send()
            near_copy(step, piece).wait_recv()
        for step in range(1, y_size):
            y_copy(step, piece).wait_send()
            own_copy(step, piece).wait_send()


def front(rows_size, lat_size, picked, norm_params, bias_row, w_joined, w_attn_out, w_mlp_in, w_mlp_out,
          turns, code_lanes, mask_tiles, dec_shard, own, left, right, across):
    group, depth = picked.shape
    tokens = group // lat_size
    shard, latents = dec_shard.shape
    x_size = rows_size // Z_CHIPS
    y_size = lat_size // CORES
    pieces = tokens // PIECE
    dma = pltpu.SemaphoreType.DMA
    vmem = pl.BlockSpec(memory_space=pltpu.VMEM)
    hbm = pl.BlockSpec(memory_space=pl.ANY)
    hops = Z_CHIPS - 1
    return pl.pallas_call(
        functools.partial(front_kernel, rows_size, lat_size),
        out_shape=[
            jax.ShapeDtypeStruct((group, depth), bf16),
            jax.ShapeDtypeStruct((depth, latents), bf16),
            jax.ShapeDtypeStruct((depth, latents), bf16),
            jax.ShapeDtypeStruct((1, latents), f32),
            jax.ShapeDtypeStruct((1, latents), f32),
            jax.ShapeDtypeStruct((1, latents), f32),
            jax.ShapeDtypeStruct((8, depth), f32),
        ],
        in_specs=[vmem] * 5 + [hbm] * 6 + [vmem] * 4,
        out_specs=[hbm] * 3 + [vmem] * 4,
        scratch_shapes=[
            pltpu.VMEM((y_size, tokens, depth), bf16),
            pltpu.VMEM((y_size - 1, tokens, depth), bf16),
            pltpu.VMEM((tokens, depth), f32),
            pltpu.VMEM((tokens, depth), bf16),
            pltpu.VMEM((tokens, depth), bf16),
            pltpu.VMEM((tokens, depth), bf16),
            pltpu.VMEM((tokens, depth), bf16),
            pltpu.VMEM((tokens, depth), bf16),
            pltpu.VMEM((16, latents // 8), f32),
            pltpu.VMEM((rows_size - 1, 16, latents // 8), f32),
            *[pltpu.VMEM(a.shape, a.dtype) for a in (w_joined, w_attn_out, w_mlp_in, w_mlp_out, turns, code_lanes)],
            dma((6,)), dma((x_size + 3, max(pieces, 2))),
            dma((hops, 2)), dma((hops, 2)), dma((hops, 2)), dma((hops, 2)),
            dma((Z_CHIPS, 2, x_size - 1)), dma((Z_CHIPS, 2, x_size - 1)),
            dma((rows_size - 1,)), dma((rows_size - 1,)),
            dma((y_size, pieces)), dma((y_size, pieces)),
            dma((y_size - 1, pieces)), dma((y_size - 1, pieces)),
            dma((y_size - 1, pieces)), dma((y_size - 1, pieces)),
            dma((y_size, pieces)), dma((y_size, pieces)),
        ],
        compiler_params=pltpu.CompilerParams(
            collective_id=3, has_side_effects=True, vmem_limit_bytes=60 * 2**20),
        name="front",
    )(picked, norm_params, bias_row, mask_tiles, dec_shard,
      w_joined, w_attn_out, w_mlp_in, w_mlp_out, turns, code_lanes, own, left, right, across)


def turn_tables(length):
    half = ROT // 2
    freqs = np.float32(10000.0) ** (np.float32(-2.0) * np.arange(half, dtype=np.float32) / np.float32(ROT))
    angles = np.arange(length, dtype=np.float32)[:, None] * np.tile(freqs, PAIR // half)[None, :]
    place = np.arange(PAIR) % HEAD
    cosines, sines = np.cos(angles.astype(np.float64)), np.sin(angles.astype(np.float64))
    return np.stack([
        np.where(place < ROT, cosines, 1.0),
        np.where(place < half, -sines, 0.0),
        np.where((place >= half) & (place < ROT), sines, 0.0),
    ]).astype(np.float32)


def softplus_parts(value):
    power = jnp.exp(value)
    grown = jnp.log(1.0 + power)
    grown = jnp.where(power < 2.0**-8, power * (1.0 - 0.5 * power), grown)
    active = jnp.where(value > 30.0, value, grown)
    return active, jnp.exp(value - active)


def forward_kernel(
    lat_size,
    inputs_hbm, enc_hbm, dec_hbm, mask_hbm, enc_bias_ref, dec_bias_ref, scale_ref,
    active_hbm, slope_hbm, mass_out, back_out, stats_out,
    active_buf, slope_buf, product, partial, own, send_two, units_two, recv_one, recv_two, got_two,
    inputs_ref, enc_ref, dec_ref, mask_ref, load_sem,
    active_sem, slope_sem, out_one, in_one, out_two, in_two, outu_two, inu_two, out_three, in_three, out_four, in_four,
):
    tokens, depth = inputs_ref.shape
    latents = enc_ref.shape[1]
    chunk, span = product.shape[1:]
    halves = [pl.ds(at * span, span) for at in range(latents // span)]
    loads = [pltpu.make_async_copy(inputs_hbm, inputs_ref, load_sem.at[0]), pltpu.make_async_copy(mask_hbm, mask_ref, load_sem.at[1])]
    for at, cols in enumerate(halves):
        loads.append(pltpu.make_async_copy(enc_hbm.at[:, cols], enc_ref.at[:, cols], load_sem.at[2 + 2 * at]))
        loads.append(pltpu.make_async_copy(dec_hbm.at[:, cols], dec_ref.at[:, cols], load_sem.at[3 + 2 * at]))
    for load in loads:
        load.start()

    width = active_hbm.shape[2]
    chunks, spans = tokens // chunk, latents // span
    y_size = lat_size // CORES
    share = chunk // lat_size
    strip = 16
    row = lax.axis_index("rows")
    lat = lax.axis_index("lat")
    my_y, core = lat // CORES, lax.rem(lat, CORES)
    other = 1 - core

    def y_peer(step):
        return lax.rem(my_y + step, y_size)

    def share_rows(y, which_core):
        return pl.multiple_of((y * CORES + which_core) * share, share)

    def token_rows(block, y, which_core):
        return pl.ds(pl.multiple_of(block * chunk + (y * CORES + which_core) * share, share), share)

    def remote(src, dst, send, recv, target):
        return pltpu.make_async_remote_copy(
            src_ref=src, dst_ref=dst, send_sem=send, recv_sem=recv,
            device_id=(row, target), device_id_type=MESH)

    def copy_one(block, y):
        slot = lax.rem(block, 2)
        return remote(
            partial.at[slot, pl.ds(share_rows(y, other), share)], recv_one.at[block, y],
            out_one.at[slot, y], in_one.at[block, y], my_y * CORES + other)

    def copies_two(block, step):
        slot = lax.rem(block, 2)
        target = y_peer(step) * CORES + core
        return [
            remote(send_two.at[slot, step - 1], recv_two.at[block, step - 1],
                   out_two.at[slot, step - 1], in_two.at[block, step - 1], target),
            remote(units_two.at[slot, step - 1], got_two.at[block, step - 1],
                   outu_two.at[slot, step - 1], inu_two.at[block, step - 1], target),
        ]

    def copy_three(block, step):
        mine = back_out.at[token_rows(block, my_y, core)]
        return remote(
            mine, mine, out_three.at[block, step - 1], in_three.at[block, step - 1], y_peer(step) * CORES + core)

    def copy_four(block, y):
        mine = back_out.at[token_rows(block, y, core)]
        return remote(mine, mine, out_four.at[block, y], in_four.at[block, y], my_y * CORES + other)

    def stores(block, at, slot):
        rows = pl.ds(pl.multiple_of(block * chunk, chunk), chunk)
        copies = []
        for part in range(span // width):
            lanes = pl.ds(part * width, width)
            copies.append(pltpu.make_async_copy(
                active_buf.at[slot, :, lanes], active_hbm.at[at * (span // width) + part, rows], active_sem.at[slot, part]))
            copies.append(pltpu.make_async_copy(
                slope_buf.at[slot, :, lanes], slope_hbm.at[at * (span // width) + part, rows], slope_sem.at[slot, part]))
        return copies

    barrier = pltpu.get_barrier_semaphore()
    pl.semaphore_signal(barrier, inc=1, device_id=(row, my_y * CORES + other), device_id_type=MESH)
    for step in range(1, y_size):
        pl.semaphore_signal(barrier, inc=1, device_id=(row, y_peer(step) * CORES + core), device_id_type=MESH)
    mass_out[...] = jnp.zeros_like(mass_out)
    stats_out[...] = jnp.zeros_like(stats_out)
    pl.semaphore_wait(barrier, y_size)

    def compute(block):
        place = lax.rem(block, 2)
        first = pl.multiple_of(block * chunk, chunk)

        @pl.when(block >= 2)
        def _():
            for y in range(y_size):
                copy_one(block - 2, y).wait_send()

        for at in range(spans):
            slot = at % 2
            if at >= 2:
                for copy in stores(block, at - 2, slot):
                    copy.wait()
            else:
                @pl.when(block > 0)
                def _():
                    for copy in stores(block - 1, spans - 2 + at, slot):
                        copy.wait()

            @pl.when(block == 0)
            def _():
                for load in loads[2 * at + 2 : 2 * at + 4] + (loads[:2] if at == 0 else []):
                    load.wait()

            product[slot] = jnp.dot(
                inputs_ref[pl.ds(first, chunk), :], enc_ref[:, at * span : (at + 1) * span], preferred_element_type=f32)
            for left in range(0, span, width):
                lanes = pl.ds(left, width)
                cols = pl.ds(at * span + left, width)
                shift = enc_bias_ref[:, cols]
                total = mass_out[:, cols]
                for top in range(0, chunk, strip):
                    rows = pl.ds(top, strip)
                    mask = mask_ref[pl.ds(first + top, strip), :]
                    mask = jnp.concatenate([mask] * (width // 128), axis=1)
                    active, slope = softplus_parts(product[slot, rows, lanes] + shift)
                    active_buf[slot, rows, lanes] = active.astype(bf16)
                    slope_buf[slot, rows, lanes] = slope * mask
                    total = total + (active * mask).reshape(strip // 8, 8, width).sum(0)
                mass_out[:, cols] = total
            for copy in stores(block, at, slot):
                copy.start()
            part = lax.dot_general(
                active_buf[slot], dec_ref[:, at * span : (at + 1) * span], (((1,), (1,)), ((), ())),
                preferred_element_type=f32)
            partial[place] = part if at == 0 else partial[place] + part

    def exchange(block):
        slot = lax.rem(block, 2)
        for y in range(y_size):
            copy_one(block, y).wait_recv()
        for step in list(range(1, y_size)) + [0]:
            y = y_peer(step)
            total = partial[slot, pl.ds(share_rows(y, core), share), :] + recv_one[block, y]
            if step == 0:
                own[slot] = total
            else:
                @pl.when(block >= 2)
                def _():
                    for copy in copies_two(block - 2, step):
                        copy.wait_send()

                code, unit = encode(total)
                send_two[slot, step - 1] = code
                put_units(units_two, (slot, step - 1), unit)
                for copy in copies_two(block, step):
                    copy.start()

    def settle(block):
        slot = lax.rem(block, 2)
        rows = token_rows(block, my_y, core)
        total = own[slot]
        for step in range(1, y_size):
            for copy in copies_two(block, step):
                copy.wait_recv()
            total = total + decode(recv_two[block, step - 1], get_units(got_two, (block, step - 1), depth))
        error = total + dec_bias_ref[...] - inputs_ref[rows, :].astype(f32)
        mask = jnp.concatenate([mask_ref[rows, :]] * (depth // 128), axis=1)
        low = (scale_ref[0:1, :] * mask * error).astype(bf16)
        back_out[rows, :] = low
        stats_out[0:8, :] += (mask * error * error).reshape(share // 8, 8, depth).sum(0)
        stats_out[8:16, :] += low.astype(f32).reshape(share // 8, 8, depth).sum(0)
        for step in range(1, y_size):
            copy_three(block, step).start()

    def spread(block):
        for step in range(1, y_size):
            copy_three(block, step).wait_recv()
        for y in range(y_size):
            copy_four(block, y).start()

    def turn(block, carry):
        @pl.when(block < chunks)
        def _():
            compute(block)
            for y in range(y_size):
                copy_one(block, y).start()

        @pl.when((block >= 1) & (block <= chunks))
        def _():
            exchange(block - 1)

        @pl.when((block >= 2) & (block <= chunks + 1))
        def _():
            settle(block - 2)

        @pl.when(block >= 3)
        def _():
            spread(block - 3)

        return carry

    lax.fori_loop(0, chunks + 3, turn, 0)
    for slot in range(2):
        for copy in stores(chunks - 1, spans - 2 + slot, slot):
            copy.wait()
    for block in range(chunks - 2, chunks):
        for y in range(y_size):
            copy_one(block, y).wait_send()
        for step in range(1, y_size):
            for copy in copies_two(block, step):
                copy.wait_send()

    def drain(block, carry):
        for step in range(1, y_size):
            copy_three(block, step).wait_send()
        for y in range(y_size):
            copy_four(block, y).wait_send()
            copy_four(block, y).wait_recv()
        return carry

    lax.fori_loop(0, chunks, drain, 0)


def forward(lat_size, inputs, enc_low, dec_cols, enc_bias_row, mask_lanes, dec_bias_row, scale_rows):
    tokens, depth = inputs.shape
    latents = enc_low.shape[1]
    chunk, span, width = 512, 1024, (512 if tokens <= 4096 else 256)
    chunks = tokens // chunk
    y_size = lat_size // CORES
    share = chunk // lat_size
    dma = pltpu.SemaphoreType.DMA
    vmem = pl.BlockSpec(memory_space=pltpu.VMEM)
    hbm = pl.BlockSpec(memory_space=pl.ANY)
    return pl.pallas_call(
        functools.partial(forward_kernel, lat_size),
        out_shape=[
            jax.ShapeDtypeStruct((latents // width, tokens, width), bf16),
            jax.ShapeDtypeStruct((latents // width, tokens, width), f32),
            jax.ShapeDtypeStruct((8, latents), f32),
            jax.ShapeDtypeStruct((tokens, depth), bf16),
            jax.ShapeDtypeStruct((16, depth), f32),
        ],
        in_specs=[hbm] * 4 + [vmem] * 3,
        out_specs=[hbm, hbm, vmem, vmem, vmem],
        scratch_shapes=[
            pltpu.VMEM((2, chunk, span), bf16),
            pltpu.VMEM((2, chunk, span), f32),
            pltpu.VMEM((2, chunk, span), f32),
            pltpu.VMEM((2, chunk, depth), f32),
            pltpu.VMEM((2, share, depth), f32),
            pltpu.VMEM((2, y_size - 1, share, depth), jnp.int16),
            pltpu.VMEM((2, y_size - 1, 8, 128), f32),
            pltpu.VMEM((chunks, y_size, share, depth), f32),
            pltpu.VMEM((chunks, y_size - 1, share, depth), jnp.int16),
            pltpu.VMEM((chunks, y_size - 1, 8, 128), f32),
            *[pltpu.VMEM(a.shape, a.dtype) for a in (inputs, enc_low, dec_cols, mask_lanes)],
            dma((2 + 2 * (latents // span),)),
            dma((2, span // width)), dma((2, span // width)),
            dma((2, y_size)), dma((chunks, y_size)),
            dma((2, y_size - 1)), dma((chunks, y_size - 1)),
            dma((2, y_size - 1)), dma((chunks, y_size - 1)),
            dma((chunks, y_size - 1)), dma((chunks, y_size - 1)),
            dma((chunks, y_size)), dma((chunks, y_size)),
        ],
        compiler_params=pltpu.CompilerParams(
            collective_id=1, has_side_effects=True, vmem_limit_bytes=60 * 2**20),
        name="forward",
    )(inputs, enc_low, dec_cols, mask_lanes, enc_bias_row, dec_bias_row, scale_rows)


def encode(value):
    top = jnp.max(jnp.abs(value), axis=0, keepdims=True)
    unit = jnp.where(top > 0.0, 32766.0 / top, 0.0)
    shifted = value * unit + 12582912.0
    return (shifted - 12582912.0).astype(jnp.int32).astype(jnp.int16), top * (1.0 / 32766.0)


def decode(code, unit):
    return code.astype(jnp.int32).astype(f32) * unit


def put_units(ref, index, unit):
    for piece in range(unit.shape[1] // 128):
        ref[index + (pl.ds(piece, 1), slice(None))] = unit[:, piece * 128 : piece * 128 + 128]


def get_units(ref, index, width):
    return jnp.concatenate(
        [ref[index + (pl.ds(piece, 1), slice(None))] for piece in range(width // 128)], axis=1)


def backward_kernel(
    rows_size, lat_size,
    back_ref, norms_ref, lasso_ref, pull_ref, mass_ref, stats_ref,
    inputs_hbm, dec_hbm, master_hbm, active_hbm, slope_hbm,
    enc_out, dec_out, bias_out, center_out, totals_out,
    grad_low, active_buf, slope_buf, sums,
    send_one, units_one, recv_one, got_one,
    send_two, units_two, recv_two, got_two,
    bias_rows, pull_cols, facts, tiles, inputs_ref, dec_ref, master_ref, load_sem,
    active_sem, slope_sem,
    out_one, in_one, outu_one, inu_one, out_two, in_two, outu_two, inu_two, out_facts, in_facts, out_tiles, in_tiles,
):
    blocks, tokens, width = active_hbm.shape
    chunk = slope_buf.shape[1]
    chunks = tokens // chunk
    shard = enc_out.shape[0]
    x_size = rows_size // Z_CHIPS
    row = lax.axis_index("rows")
    lat = lax.axis_index("lat")
    my_z, my_x = row // x_size, lax.rem(row, x_size)

    def x_peer(step):
        return lax.rem(my_x + step, x_size)

    def z_peer(step):
        return lax.rem(my_z + step, Z_CHIPS)

    def active_copy(block):
        slot = lax.rem(block, 2)
        return pltpu.make_async_copy(active_hbm.at[block], active_buf.at[slot], active_sem.at[slot])

    def slope_copy(index):
        slot = lax.rem(index, slope_buf.shape[0])
        return pltpu.make_async_copy(
            slope_hbm.at[index // chunks, pl.ds(pl.multiple_of(lax.rem(index, chunks) * chunk, chunk), chunk)],
            slope_buf.at[slot],
            slope_sem.at[slot],
        )

    def copies(stage, block, which, step):
        slot = lax.rem(block, 2)
        if stage == 0:
            target = (my_z * x_size + x_peer(step), lat)
            refs = (send_one, recv_one, out_one, in_one, units_one, got_one, outu_one, inu_one)
        else:
            target = (z_peer(step) * x_size + my_x, lat)
            refs = (send_two, recv_two, out_two, in_two, units_two, got_two, outu_two, inu_two)
        return [
            pltpu.make_async_remote_copy(
                src_ref=refs[at].at[slot, which, step - 1], dst_ref=refs[at + 1].at[block, which, step - 1],
                send_sem=refs[at + 2].at[slot, which, step - 1], recv_sem=refs[at + 3].at[block, which, step - 1],
                device_id=target, device_id_type=MESH)
            for at in (0, 4)
        ]

    devices = rows_size * lat_size
    me = row * lat_size + lat
    latents = dec_ref.shape[1]
    depth = inputs_ref.shape[1]
    part = latents // 8

    def fact_copy(kind, step):
        area = facts.at[kind, row]
        return pltpu.make_async_remote_copy(
            src_ref=area, dst_ref=area, send_sem=out_facts.at[kind, step], recv_sem=in_facts.at[kind, row],
            device_id=(lax.rem(row + step, rows_size), lat), device_id_type=MESH)

    def fact_arrival(kind, step):
        source = lax.rem(row + step, rows_size)
        area = facts.at[kind, source]
        return pltpu.make_async_remote_copy(
            src_ref=area, dst_ref=area, send_sem=out_facts.at[kind, step], recv_sem=in_facts.at[kind, source],
            device_id=(source, lat), device_id_type=MESH)

    def tile_copy(kind, step):
        area = tiles.at[kind, me]
        target = lax.rem(me + step, devices)
        return pltpu.make_async_remote_copy(
            src_ref=area, dst_ref=area, send_sem=out_tiles.at[kind, step], recv_sem=in_tiles.at[kind, me],
            device_id=(target // lat_size, lax.rem(target, lat_size)), device_id_type=MESH)

    def tile_arrival(kind, step):
        source = lax.rem(me + step, devices)
        area = tiles.at[kind, source]
        return pltpu.make_async_remote_copy(
            src_ref=area, dst_ref=area, send_sem=out_tiles.at[kind, step], recv_sem=in_tiles.at[kind, source],
            device_id=(source // lat_size, lax.rem(source, lat_size)), device_id_type=MESH)

    def over_devices(action):
        def turn(step, carry):
            action(step)
            return carry

        lax.fori_loop(1, devices, turn, 0)

    def share_row(kind, value):
        for at in range(8):
            facts[kind, row, pl.ds(at, 1), :] = value[:, at * part : (at + 1) * part]
        for step in range(1, rows_size):
            fact_copy(kind, step).start()

    def shared_row(kind):
        for step in range(1, rows_size):
            fact_arrival(kind, step).wait_recv()
        total = facts[kind, 0]
        for source in range(1, rows_size):
            total = total + facts[kind, source]
        return jnp.concatenate([total[at : at + 1, :] for at in range(8)], axis=1)

    def share_tile(kind, value):
        tiles[kind, me] = value

        def start(step):
            tile_copy(kind, step).start()

        over_devices(start)

    def shared_tile(kind):
        def wait(step):
            tile_arrival(kind, step).wait_recv()

        over_devices(wait)
        return lax.fori_loop(1, devices, lambda source, total: total + tiles[kind, source], tiles[kind, 0])

    barrier = pltpu.get_barrier_semaphore()

    def greet(step):
        target = lax.rem(me + step, devices)
        pl.semaphore_signal(
            barrier, inc=1, device_id=(target // lat_size, lax.rem(target, lat_size)), device_id_type=MESH)

    over_devices(greet)
    loads = [
        pltpu.make_async_copy(source, target, load_sem.at[at])
        for at, (source, target) in enumerate(((dec_hbm, dec_ref), (inputs_hbm, inputs_ref), (master_hbm, master_ref)))
    ]
    active_copy(0).start()
    for load in loads:
        load.start()
    ahead = slope_buf.shape[0] - 1
    for index in range(ahead):
        slope_copy(index).start()
    pl.semaphore_wait(barrier, devices - 1)
    share_row(0, jnp.sum(mass_ref[...], axis=0, keepdims=True))
    center = jnp.sum(stats_ref[8:16, :], axis=0, keepdims=True)
    square = jnp.sum(stats_ref[0:8, :], keepdims=True)
    quarter = depth // 4
    share_tile(0, jnp.concatenate(
        [center[:, at * quarter : (at + 1) * quarter] for at in range(4)]
        + [jnp.broadcast_to(square, (4, quarter))], axis=0))

    def columns(block):
        return pl.ds(pl.multiple_of(block * width, width), width)

    over_tokens = (((0,), (0,)), ((), ()))

    def compute_dec(block):
        slot = lax.rem(block, 2)

        @pl.when(block + 1 < blocks)
        def _():
            active_copy(block + 1).start()

        active_copy(block).wait()
        sums[slot, 1] = lax.dot_general(back_ref[...], active_buf[slot], over_tokens, preferred_element_type=f32)

    def compute_enc(block):
        slot = lax.rem(block, 2)
        cols = columns(block)

        @pl.when(block == 0)
        def _():
            for load in loads:
                load.wait()

        def piece(index, total):
            at = block * chunks + index

            @pl.when(at + ahead < blocks * chunks)
            def _():
                slope_copy(at + ahead).start()

            slope_copy(at).wait()
            rows = pl.ds(pl.multiple_of(index * chunk, chunk), chunk)
            back = jnp.dot(back_ref[rows, :], dec_ref[:, cols], preferred_element_type=f32)
            low = ((back + lasso_ref[:, cols]) * slope_buf[lax.rem(at, ahead + 1)]).astype(bf16)
            grad_low[rows, :] = low
            return total + low.astype(f32).reshape(chunk // 8, 8, width).sum(0)

        bias_rows[:, cols] = lax.fori_loop(0, chunks, piece, jnp.zeros((8, width), f32))
        sums[slot, 0] = lax.dot_general(inputs_ref[...], grad_low[...], over_tokens, preferred_element_type=f32)

    def send_x(block, which):
        slot = lax.rem(block, 2)
        for step in range(1, x_size):
            @pl.when(block >= 2)
            def _():
                for copy in copies(0, block - 2, which, step):
                    copy.wait_send()

            parts = []
            for z in range(Z_CHIPS):
                first = pl.multiple_of((z * x_size + x_peer(step)) * shard, shard)
                parts.append(sums[slot, which, pl.ds(first, shard), :])
            code, unit = encode(jnp.concatenate(parts, axis=0))
            for z in range(Z_CHIPS):
                send_one[slot, which, step - 1, z] = code[z * shard : (z + 1) * shard]
            put_units(units_one, (slot, which, step - 1), unit)
            for copy in copies(0, block, which, step):
                copy.start()

    def send_z(block, which):
        slot = lax.rem(block, 2)
        for step in range(1, x_size):
            for copy in copies(0, block, which, step):
                copy.wait_recv()
        for step in range(Z_CHIPS):
            z = z_peer(step)
            if step:
                @pl.when(block >= 2)
                def _():
                    for copy in copies(1, block - 2, which, step):
                        copy.wait_send()

            first = pl.multiple_of((z * x_size + my_x) * shard, shard)
            total = sums[slot, which, pl.ds(first, shard), :]
            for x_step in range(1, x_size):
                total = total + decode(
                    recv_one[block, which, x_step - 1, z], get_units(got_one, (block, which, x_step - 1), width))
            if step == 0:
                (enc_out, dec_out)[which][:, columns(block)] = total
            else:
                code, unit = encode(total)
                send_two[slot, which, step - 1] = code
                put_units(units_two, (slot, which, step - 1), unit)
                for copy in copies(1, block, which, step):
                    copy.start()

    def finish(block, which):
        slot = lax.rem(block, 2)
        for step in range(1, Z_CHIPS):
            for copy in copies(1, block, which, step):
                copy.wait_recv()
        out, cols = (enc_out, dec_out)[which], columns(block)
        total = out[:, cols]
        for step in range(1, Z_CHIPS):
            total = total + decode(
                recv_two[block, which, step - 1], get_units(got_two, (block, which, step - 1), width))
        out[:, cols] = total

    def turn(block, carry):
        for which, compute in ((1, compute_dec), (0, compute_enc)):
            @pl.when(block < blocks)
            def _():
                compute(block)
                send_x(block, which)

            @pl.when((block >= 1) & (block <= blocks))
            def _():
                send_z(block - 1, which)

            @pl.when(block >= 2)
            def _():
                finish(block - 2, which)

        return carry

    lax.fori_loop(0, blocks, turn, 0)
    share_row(1, jnp.sum(bias_rows[...], axis=0, keepdims=True))
    lax.fori_loop(blocks, blocks + 2, turn, 0)

    mass = shared_row(0)
    bias = shared_row(1)
    bias_out[...] = bias
    pull = mass * pull_ref[...]

    def squares(block, total):
        cols = columns(block)
        gain = dec_out[:, cols] + pull_cols[:, cols] * master_ref[:, cols]
        dec_out[:, cols] = gain
        other = enc_out[:, cols]
        return total + gain * gain + other * other

    pull_cols[...] = pull
    total = jnp.sum(lax.fori_loop(0, blocks, squares, jnp.zeros((shard, width), f32)), keepdims=True)
    leads = jnp.where(row == 0, 1.0, 0.0)
    total = total + leads * jnp.sum(bias * bias, keepdims=True)
    lasso = leads * lasso_coef * jnp.sum(mass * norms_ref[...], keepdims=True)
    share_tile(1, jnp.concatenate(
        [jnp.broadcast_to(total, (4, quarter)), jnp.broadcast_to(lasso, (4, quarter))], axis=0))
    first = shared_tile(0)
    center = jnp.concatenate([first[at : at + 1, :] for at in range(4)], axis=1)
    center_out[...] = center
    second = shared_tile(1)
    squared = second[0:4, :] + jnp.sum(center * center, keepdims=True)
    totals_out[...] = jnp.concatenate([squared, first[4:8, :] + second[4:8, :]], axis=0)
    for kind in range(2):
        for step in range(1, rows_size):
            fact_copy(kind, step).wait_send()

        def sent(step, kind=kind):
            tile_copy(kind, step).wait_send()

        over_devices(sent)
    for block in range(max(blocks - 2, 0), blocks):
        for which in range(2):
            for stage, size in ((0, x_size), (1, Z_CHIPS)):
                for step in range(1, size):
                    for copy in copies(stage, block, which, step):
                        copy.wait_send()


def backward(rows_size, lat_size, inputs, back, dec_cols, norms_row, lasso_row, pull_row, mass_rows, stats, master,
             active, slope):
    blocks, tokens, width = active.shape
    depth = inputs.shape[1]
    shard = depth // rows_size
    latents = dec_cols.shape[1]
    x_size = rows_size // Z_CHIPS
    devices = rows_size * lat_size
    chunk = min(CHUNK, tokens)
    i16 = jnp.int16
    dma = pltpu.SemaphoreType.DMA
    vmem = pl.BlockSpec(memory_space=pltpu.VMEM)
    hbm = pl.BlockSpec(memory_space=pl.ANY)
    return pl.pallas_call(
        functools.partial(backward_kernel, rows_size, lat_size),
        out_shape=[
            jax.ShapeDtypeStruct((shard, latents), f32),
            jax.ShapeDtypeStruct((shard, latents), f32),
            jax.ShapeDtypeStruct((1, latents), f32),
            jax.ShapeDtypeStruct((1, depth), f32),
            jax.ShapeDtypeStruct((8, 128), f32),
        ],
        in_specs=[vmem] * 6 + [hbm] * 5,
        out_specs=[vmem] * 5,
        scratch_shapes=[
            pltpu.VMEM((tokens, width), bf16),
            pltpu.VMEM((2, tokens, width), bf16),
            pltpu.VMEM((SLOTS, chunk, width), f32),
            pltpu.VMEM((2, 2, depth, width), f32),
            pltpu.VMEM((2, 2, x_size - 1, Z_CHIPS, shard, width), i16),
            pltpu.VMEM((2, 2, x_size - 1, 8, 128), f32),
            pltpu.VMEM((blocks, 2, x_size - 1, Z_CHIPS, shard, width), i16),
            pltpu.VMEM((blocks, 2, x_size - 1, 8, 128), f32),
            pltpu.VMEM((2, 2, Z_CHIPS - 1, shard, width), i16),
            pltpu.VMEM((2, 2, Z_CHIPS - 1, 8, 128), f32),
            pltpu.VMEM((blocks, 2, Z_CHIPS - 1, shard, width), i16),
            pltpu.VMEM((blocks, 2, Z_CHIPS - 1, 8, 128), f32),
            pltpu.VMEM((8, latents), f32),
            pltpu.VMEM((1, latents), f32),
            pltpu.VMEM((2, rows_size, 8, latents // 8), f32),
            pltpu.VMEM((2, devices, 8, 128), f32),
            *[pltpu.VMEM(a.shape, a.dtype) for a in (inputs, dec_cols, master)],
            dma((3,)),
            dma((2,)), dma((SLOTS,)),
            dma((2, 2, x_size - 1)), dma((blocks, 2, x_size - 1)),
            dma((2, 2, x_size - 1)), dma((blocks, 2, x_size - 1)),
            dma((2, 2, Z_CHIPS - 1)), dma((blocks, 2, Z_CHIPS - 1)),
            dma((2, 2, Z_CHIPS - 1)), dma((blocks, 2, Z_CHIPS - 1)),
            dma((2, rows_size)), dma((2, rows_size)), dma((2, devices)), dma((2, devices)),
        ],
        compiler_params=pltpu.CompilerParams(
            collective_id=2, has_side_effects=True, vmem_limit_bytes=61 * 2**20),
        name="backward",
    )(back, norms_row, lasso_row, pull_row, mass_rows, stats, inputs, dec_cols, master, active, slope)


def update_kernel(
    totals_ref, counts_ref, enc_grad, dec_grad, enc_bias_grad, dec_bias_grad,
    enc_w, enc_m, enc_s, dec_w, dec_m, dec_s, enc_b, enc_bm, enc_bs, dec_b, dec_bm, dec_bs,
    enc_w_out, enc_m_out, enc_s_out, dec_w_out, dec_m_out, dec_s_out,
    enc_b_out, enc_bm_out, enc_bs_out, dec_b_out, dec_bm_out, dec_bs_out, scalars_out,
):
    norm = jnp.sqrt(totals_ref[0:1, 0:1])
    factor = clip_bound / jnp.maximum(norm, clip_bound)
    groups = (
        (enc_grad, (enc_w, enc_m, enc_s), (enc_w_out, enc_m_out, enc_s_out), weight_decay),
        (dec_grad, (dec_w, dec_m, dec_s), (dec_w_out, dec_m_out, dec_s_out), weight_decay),
        (enc_bias_grad, (enc_b, enc_bm, enc_bs), (enc_b_out, enc_bm_out, enc_bs_out), 0.0),
        (dec_bias_grad, (dec_b, dec_bm, dec_bs), (dec_b_out, dec_bm_out, dec_bs_out), 0.0),
    )
    for grad, olds, news, decay in groups:
        found = adam_update(*[old[...] for old in olds], grad[...] * factor, decay)
        for new, value in zip(news, found):
            new[...] = value
    scalars_out[0:1, :] = jnp.broadcast_to(norm, (1, 128))
    scalars_out[1:2, :] = totals_ref[4:5, :]
    scalars_out[2:8, :] = counts_ref[2:8, :]


def update(totals, counts, grads, states):
    shard, latents = grads[0].shape
    depth = grads[3].shape[1]
    span = latents // 4
    wide = pl.BlockSpec((shard, span), lambda i: (0, i))
    row = pl.BlockSpec((1, span), lambda i: (0, i))
    short = pl.BlockSpec((1, depth), lambda i: (0, 0))
    tile = pl.BlockSpec((8, 128), lambda i: (0, 0))
    state_specs = [wide] * 6 + [row] * 3 + [short] * 3
    return pl.pallas_call(
        update_kernel,
        grid=(latents // span,),
        out_shape=[jax.ShapeDtypeStruct(a.shape, f32) for a in states] + [jax.ShapeDtypeStruct((8, 128), f32)],
        in_specs=[tile, tile, wide, wide, row, short] + state_specs,
        out_specs=state_specs + [tile],
        compiler_params=pltpu.CompilerParams(vmem_limit_bytes=61 * 2**20),
        name="update",
    )(totals, counts, *grads, *states)


def body(
    token_ids,
    token_mask,
    scale_index,
    embed,
    norm_params,
    frozen_bias,
    w_joined,
    w_attn_out,
    w_mlp_in,
    w_mlp_out,
    enc_weight,
    enc_moment,
    enc_second,
    dec_weight,
    dec_moment,
    dec_second,
    enc_bias,
    enc_bias_moment,
    enc_bias_second,
    dec_bias,
    dec_bias_moment,
    dec_bias_second,
):
    lat_size = lax.axis_size("lat")
    lat_index = lax.axis_index("lat")
    group_tokens = token_ids.shape[0]
    tok_local = group_tokens // lat_size
    rows_size = lax.axis_size("rows")
    depth = enc_weight.shape[0] * rows_size
    mask_float = token_mask.astype(f32)
    dec_master = dec_weight.T
    bias_row = frozen_bias[None, :]
    vocab_local = embed.shape[0]
    vocab_first = lat_index * vocab_local
    local_ids = token_ids - vocab_first
    picked = jnp.take(embed, local_ids, axis=0, mode="clip")
    codes = (token_ids // vocab_local * 16 + scale_index).reshape(lat_size // CORES, CORES, tok_local)
    codes = lax.dynamic_index_in_dim(codes, lat_index % CORES, 1, keepdims=False).reshape(-1)
    code_lanes = jnp.broadcast_to(codes[:, None], (codes.shape[0], 128))
    own = jnp.stack([enc_weight.astype(bf16), dec_master.astype(bf16)])
    x_size = rows_size // Z_CHIPS
    right_pairs = [(i, i + x_size) for i in range(rows_size - x_size)]
    left_pairs = [(i + x_size, i) for i in range(rows_size - x_size)]
    from_left = lax.ppermute(own, "rows", right_pairs)
    from_right = lax.ppermute(own, "rows", left_pairs)
    across = []
    for step in range(1, x_size):
        pairs = [(i // x_size * x_size + (i + step) % x_size, i) for i in range(rows_size)]
        across.append(lax.ppermute(own, "rows", pairs))
    mask_lanes = jnp.broadcast_to(mask_float[:, None], (group_tokens, 128))
    all_inputs, enc_low, dec_cols, norms_row, lasso_row, pull_row, scale_rows = front(
        rows_size, lat_size, picked, norm_params, bias_row, w_joined, w_attn_out, w_mlp_in, w_mlp_out,
        turn_tables(tok_local), code_lanes, mask_float.reshape(-1, 128), dec_master,
        own, from_left, from_right, jnp.stack(across))
    active, slope, mass_rows, recon_grad, stats = forward(
        lat_size, all_inputs, enc_low, dec_cols, enc_bias[None, :], mask_lanes, dec_bias[None, :], scale_rows)
    grad_enc, grad_dec, bias_total, center, totals = backward(
        rows_size, lat_size, all_inputs, recon_grad, dec_cols, norms_row, lasso_row, pull_row, mass_rows, stats, dec_master, active, slope)
    states = [
        enc_weight, enc_moment, enc_second, dec_master, dec_moment.T, dec_second.T,
        enc_bias[None, :], enc_bias_moment[None, :], enc_bias_second[None, :],
        dec_bias[None, :], dec_bias_moment[None, :], dec_bias_second[None, :],
    ]
    *fresh, scalars = update(totals, scale_rows, (grad_enc, grad_dec, bias_total, center), states)
    return (
        *fresh[:3],
        *[value.T for value in fresh[3:6]],
        *[value[0] for value in fresh[6:]],
        scalars[0, 0],
        scalars[1, 0],
        scalars[2, 0],
    )


def solution(mesh):
    placed = (
        P("rows"),
        P("rows"),
        P("rows"),
        P("lat", None),
        P(),
        P(),
        P(),
        P(),
        P(),
        P(),
        P("rows", "lat"),
        P("rows", "lat"),
        P("rows", "lat"),
        P("lat", "rows"),
        P("lat", "rows"),
        P("lat", "rows"),
        P("lat"),
        P("lat"),
        P("lat"),
        P(),
        P(),
        P(),
    )
    return jax.shard_map(
        body,
        mesh=mesh,
        in_specs=placed,
        out_specs=(
            P("rows", "lat"),
            P("rows", "lat"),
            P("rows", "lat"),
            P("lat", "rows"),
            P("lat", "rows"),
            P("lat", "rows"),
            P("lat"),
            P("lat"),
            P("lat"),
            P(),
            P(),
            P(),
            P(),
            P(),
            P(),
        ),
        check_vma=False,
    )
```

```python
import functools
import jax
import jax.numpy as jnp
import numpy as np
from jax import lax
from jax.experimental import pallas as pl
from jax.experimental.pallas import tpu as pltpu
from jax.sharding import PartitionSpec as P

HEADS = 8
ROT = 16
STEP = 10
Z_CHIPS = 4
CORES = 2
SLOTS = 6
CHUNK = 1024
MESH = pl.DeviceIdType.MESH
f32 = jnp.float32
bf16 = jnp.bfloat16


lasso_coef = 5.0
clip_bound = 1.0
learn_rate = 0.03
beta_one = 0.9
beta_two = 0.999
adam_eps = 1e-08
weight_decay = 0.01


def adam_update(weight, moment, second, grad, decay):
    moment_new = beta_one * moment + (1.0 - beta_one) * grad
    second_new = beta_two * second + (1.0 - beta_two) * grad * grad
    corrected = moment_new / (1.0 - beta_one**STEP)
    scaled = jnp.sqrt(second_new / (1.0 - beta_two**STEP)) + adam_eps
    weight_new = weight - learn_rate * (corrected / scaled + decay * weight)
    return (weight_new, moment_new, second_new)


ROWS = 512
PIECE = 256
HEAD = 64
PAIR = 128


def front_kernel(
    rows_size, lat_size,
    picked_ref, norm_ref, bias_ref, mask_ref, dec_ref,
    joined_hbm, attn_hbm, mlp_in_hbm, mlp_out_hbm, turn_hbm, code_hbm, own_ref, left_ref, right_ref, across_ref,
    inputs_out, enc_out, dec_out, norms_out, lasso_out, pull_out, scale_out,
    from_core, from_y, base, queries, keys, values, context, ready, facts, got_facts,
    joined_ref, attn_ref, mlp_in_ref, mlp_out_ref, turn_ref, code_ref,
    load_sem, place_sem,
    out_right, in_left, out_left, in_right, out_x, in_x, out_fact, in_fact,
    out_core, in_core, out_y, in_y, out_own, in_own, out_near, in_near,
):
    tokens, depth = base.shape
    shard, latents = dec_ref.shape
    hidden = mlp_in_ref.shape[1]
    loads = [
        pltpu.make_async_copy(source, target, load_sem.at[at])
        for at, (source, target) in enumerate((
            (code_hbm, code_ref), (joined_hbm, joined_ref), (turn_hbm, turn_ref), (mlp_in_hbm, mlp_in_ref),
            (mlp_out_hbm, mlp_out_ref), (attn_hbm, attn_ref)))
    ]
    for load in loads:
        load.start()
    x_size = rows_size // Z_CHIPS
    y_size = lat_size // CORES
    pieces = tokens // PIECE
    row = lax.axis_index("rows")
    lat = lax.axis_index("lat")
    my_z, my_x = row // x_size, lax.rem(row, x_size)
    my_y, core = lat // CORES, lax.rem(lat, CORES)
    other = 1 - core

    def remote(src, dst, send, recv, to_row, to_lat):
        return pltpu.make_async_remote_copy(
            src_ref=src, dst_ref=dst, send_sem=send, recv_sem=recv,
            device_id=(to_row, to_lat), device_id_type=MESH)

    def peer_row(step):
        return lax.rem(row + step, rows_size)

    def x_row(step):
        return my_z * x_size + lax.rem(my_x + step, x_size)

    def y_peer(step):
        return lax.rem(my_y + step, y_size)

    barrier = pltpu.get_barrier_semaphore()
    for step in range(1, rows_size):
        pl.semaphore_signal(barrier, inc=1, device_id=(peer_row(step), lat), device_id_type=MESH)
    for step in range(1, y_size):
        pl.semaphore_signal(barrier, inc=1, device_id=(row, y_peer(step) * CORES + core), device_id_type=MESH)
    pl.semaphore_signal(barrier, inc=1, device_id=(row, my_y * CORES + other), device_id_type=MESH)

    square = jnp.sum(dec_ref[...] * dec_ref[...], axis=0, keepdims=True)
    part = latents // 8
    for at in range(8):
        facts[pl.ds(at, 1), :] = square[:, at * part : (at + 1) * part]
    facts[8:16, :] = jnp.broadcast_to(jnp.sum(mask_ref[...], keepdims=True), (8, part))
    pl.semaphore_wait(barrier, rows_size + y_size - 1)

    weights = (enc_out, dec_out)

    def weight_rows(z):
        return pl.ds(pl.multiple_of((z * x_size + my_x) * shard, shard), shard)

    def right_copy(hop, which, received=False):
        area = weights[which].at[weight_rows(jnp.maximum(my_z - hop - (1 if received else 0), 0))]
        source = left_ref.at[which] if hop == 1 and not received else area
        return remote(source, area, out_right.at[hop, which], in_left.at[hop, which],
                      jnp.minimum(my_z + 1, Z_CHIPS - 1) * x_size + my_x, lat)

    def left_copy(hop, which, received=False):
        area = weights[which].at[weight_rows(jnp.minimum(my_z + hop + (1 if received else 0), Z_CHIPS - 1))]
        source = right_ref.at[which] if hop == 1 and not received else area
        return remote(source, area, out_left.at[hop, which], in_right.at[hop, which],
                      jnp.maximum(my_z - 1, 0) * x_size + my_x, lat)

    def x_copy(z, which, step, source=None):
        area = weights[which].at[weight_rows(z)]
        return remote(area if source is None else source.at[which], area,
                      out_x.at[z, which, step - 1], in_x.at[z, which, step - 1], x_row(step), lat)

    def place(index, which):
        sources = [(own_ref, row), (left_ref, row - x_size), (right_ref, row + x_size)]
        sources += [(across_ref.at[step - 1], x_row(step)) for step in range(1, x_size)]
        source, owner = sources[index]
        owner = jnp.clip(owner, 0, rows_size - 1)
        return pltpu.make_async_copy(
            source.at[which], weights[which].at[pl.ds(pl.multiple_of(owner * shard, shard), shard)],
            place_sem.at[index, which])

    def place_all(action):
        for which in range(2):
            for index in range(x_size + 2):
                if index == 1:
                    @pl.when(my_z > 0)
                    def _():
                        action(place(1, which))
                elif index == 2:
                    @pl.when(my_z < Z_CHIPS - 1)
                    def _():
                        action(place(2, which))
                else:
                    action(place(index, which))

    def pass_on(hop, which):
        @pl.when(my_z >= hop)
        def _():
            if hop > 1:
                right_copy(hop - 1, which, True).wait_recv()
            if hop < Z_CHIPS - 1:
                @pl.when(my_z < Z_CHIPS - 1)
                def _():
                    right_copy(hop, which).start()
            for step in range(1, x_size):
                x_copy(my_z - hop, which, step, left_ref if hop == 1 else None).start()

        @pl.when(my_z + hop <= Z_CHIPS - 1)
        def _():
            if hop > 1:
                left_copy(hop - 1, which, True).wait_recv()
            if hop < Z_CHIPS - 1:
                @pl.when(my_z > 0)
                def _():
                    left_copy(hop, which).start()
            for step in range(1, x_size):
                x_copy(my_z + hop, which, step, right_ref if hop == 1 else None).start()

    def fact_copy(step):
        return remote(facts, got_facts.at[step - 1], out_fact.at[step - 1], in_fact.at[step - 1], peer_row(step), lat)

    def block_rows(y, which_core, piece):
        return pl.ds(pl.multiple_of((y * CORES + which_core) * tokens + piece * PIECE, PIECE), PIECE)

    def core_copy(step, piece):
        return remote(
            picked_ref.at[block_rows(y_peer(step), other, piece)], from_core.at[step, pl.ds(piece * PIECE, PIECE)],
            out_core.at[step, piece], in_core.at[step, piece], row, my_y * CORES + other)

    def y_copy(step, piece):
        here = pl.ds(piece * PIECE, PIECE)
        return remote(
            from_core.at[step, here], from_y.at[step - 1, here],
            out_y.at[step - 1, piece], in_y.at[step - 1, piece], row, y_peer(step) * CORES + core)

    for piece in range(pieces):
        for step in list(range(1, y_size)) + [0]:
            core_copy(step, piece).start()
    def code_rows(y, piece):
        code = code_ref[pl.ds(pl.multiple_of(y * tokens + piece * PIECE, PIECE), PIECE), :]
        return jnp.concatenate([code] * (depth // 128), axis=1)

    loads[0].wait()
    for piece in range(pieces):
        here = pl.ds(piece * PIECE, PIECE)
        for step in list(range(1, y_size)) + [0]:
            holder = lax.shift_right_logical(code_rows(y_peer(step), piece), 4)
            core_copy(step, piece).wait_recv()
            total = jnp.where(
                holder == lat, picked_ref[block_rows(y_peer(step), core, piece), :].astype(f32),
                jnp.where(holder == my_y * CORES + other, from_core[step, here, :].astype(f32), 0.0))
            if step == 0:
                base[here, :] = total
            else:
                from_core[step, here, :] = total.astype(bf16)
                y_copy(step, piece).start()

    pass_on(1, 0)
    for step in range(1, rows_size):
        fact_copy(step).start()
    place_all(lambda copy: copy.start())
    pass_on(1, 1)
    pass_on(2, 0)

    def normed(value, gain, shift):
        centred = value - jnp.mean(value, axis=1, keepdims=True)
        spread = jnp.mean(centred * centred, axis=1, keepdims=True)
        return (centred * lax.rsqrt(spread + 1e-05) * gain + shift).astype(bf16)

    def dot(left, right):
        return jnp.dot(left, right, preferred_element_type=f32)

    def rotated(value, rows):
        cosine, low, high = turn_ref[0, rows, :], turn_ref[1, rows, :], turn_ref[2, rows, :]
        parts = []
        for at in range(depth // PAIR):
            tile = value[:, at * PAIR : (at + 1) * PAIR]
            parts.append(
                tile * cosine + pltpu.roll(tile, PAIR - ROT // 2, 1) * low + pltpu.roll(tile, ROT // 2, 1) * high)
        return jnp.concatenate(parts, axis=1)

    for load in loads[1:]:
        load.wait()
    for block in range(tokens // ROWS):
        rows = pl.ds(block * ROWS, ROWS)
        for piece in range(block * ROWS // PIECE, (block + 1) * ROWS // PIECE):
            for step in range(1, y_size):
                y_copy(step, piece).wait_recv()
        embedded = base[rows, :]
        for step in range(1, y_size):
            embedded = embedded + from_y[step - 1, rows, :].astype(f32)
        attn_in = normed(embedded, norm_ref[0:1, :], norm_ref[1:2, :])
        joined = dot(attn_in, joined_ref[...]) + bias_ref[:, : 3 * depth]
        queries[rows, :] = (rotated(joined[:, :depth], rows).astype(bf16) * HEAD**-0.5).astype(bf16)
        keys[rows, :] = rotated(joined[:, depth : 2 * depth], rows).astype(bf16)
        values[rows, :] = joined[:, 2 * depth :].astype(bf16)
        mlp_in = normed(embedded, norm_ref[2:3, :], norm_ref[3:4, :])
        inner = dot(mlp_in, mlp_in_ref[...]) + bias_ref[:, 4 * depth : 4 * depth + hidden]
        inner = (0.5 * inner * (1.0 + lax.erf(inner * 0.5**0.5))).astype(bf16)
        base[rows, :] = embedded + (dot(inner, mlp_out_ref[...]) + bias_ref[:, 4 * depth + hidden :])
        if block == 0:
            pass_on(2, 1)
    pass_on(3, 0)

    def own_rows(y, which_core, piece):
        return pl.ds(pl.multiple_of((y * CORES + which_core) * tokens + piece * PIECE, PIECE), PIECE)

    def own_copy(step, piece):
        area = inputs_out.at[own_rows(my_y, core, piece)]
        return remote(ready.at[pl.ds(piece * PIECE, PIECE)], area, out_own.at[step - 1, piece], in_own.at[step - 1, piece], row, y_peer(step) * CORES + core)

    def near_copy(step, piece):
        area = inputs_out.at[own_rows(y_peer(step), core, piece)]
        source = area if step else ready.at[pl.ds(piece * PIECE, PIECE)]
        return remote(source, area, out_near.at[step, piece], in_near.at[step, piece], row, my_y * CORES + other)

    def keep_copy(piece):
        return pltpu.make_async_copy(
            ready.at[pl.ds(piece * PIECE, PIECE)], inputs_out.at[own_rows(my_y, core, piece)], place_sem.at[x_size + 2, piece])

    lanes = lax.broadcasted_iota(jnp.int32, (PIECE, PAIR), 1)
    for piece in range(pieces):
        here = pl.ds(piece * PIECE, PIECE)
        reach = (piece + 1) * PIECE
        visible = (
            lax.broadcasted_iota(jnp.int32, (PIECE, reach), 0) + piece * PIECE
            >= lax.broadcasted_iota(jnp.int32, (PIECE, reach), 1)
        )

        def attend(pair, carry):
            cols = pl.ds(pl.multiple_of(pair * PAIR, PAIR), PAIR)
            both = queries[here, cols]
            found = []
            for first in (True, False):
                chosen = jnp.where((lanes < HEAD) == first, both, jnp.zeros_like(both))
                scores = lax.dot_general(
                    chosen, keys[0:reach, cols], (((1,), (1,)), ((), ())), preferred_element_type=f32)
                scores = jnp.where(visible, scores, -1e30)
                powers = jnp.exp(scores - jnp.max(scores, axis=1, keepdims=True))
                probs = (powers * (1.0 / jnp.sum(powers, axis=1, keepdims=True))).astype(bf16)
                found.append(dot(probs, values[0:reach, cols]))
            context[here, cols] = jnp.where(lanes < HEAD, found[0], found[1]).astype(bf16)
            return carry

        lax.fori_loop(0, depth // PAIR, attend, 0)
        attended = dot(context[here, :], attn_ref[...]) + bias_ref[:, 3 * depth : 4 * depth]
        level = 0.5 + 0.25 * (code_rows(my_y, piece) & 15).astype(f32)
        ready[here, :] = ((base[here, :] + attended) * level).astype(bf16)
        keep_copy(piece).start()
        for step in range(1, y_size):
            own_copy(step, piece).start()
        near_copy(0, piece).start()
        if piece == 1:
            pass_on(3, 1)
        if piece >= 2:
            for step in range(1, y_size):
                own_copy(step, piece - 2).wait_recv()
                near_copy(step, piece - 2).start()

    total = facts[...]
    for step in range(1, rows_size):
        fact_copy(step).wait_recv()
        total = total + got_facts[step - 1]
    count = total[8:9, 0:1]
    norms = jnp.sqrt(total[0:8, :])
    norms = jnp.concatenate([norms[at : at + 1, :] for at in range(8)], axis=1)
    lasso_scale = lasso_coef / count
    norms_out[...] = norms
    lasso_out[...] = lasso_scale * norms
    pull_out[...] = lasso_scale / norms
    scale_out[0:1, :] = jnp.broadcast_to(2.0 / count, (1, depth))
    scale_out[1:8, :] = jnp.broadcast_to(count, (7, depth))
    for piece in range(pieces - 2, pieces):
        for step in range(1, y_size):
            own_copy(step, piece).wait_recv()
            near_copy(step, piece).start()
    place_all(lambda copy: copy.wait())

    for which in range(2):
        for hop in range(1, Z_CHIPS - 1):
            @pl.when((my_z < Z_CHIPS - 1) & (my_z >= hop))
            def _():
                right_copy(hop, which).wait_send()

            @pl.when((my_z > 0) & (my_z + hop <= Z_CHIPS - 1))
            def _():
                left_copy(hop, which).wait_send()

        for z in range(Z_CHIPS):
            @pl.when(z != my_z)
            def _():
                for step in range(1, x_size):
                    x_copy(z, which, step).wait_send()
                    x_copy(z, which, step).wait_recv()
    for step in range(1, rows_size):
        fact_copy(step).wait_send()
    for piece in range(pieces):
        keep_copy(piece).wait()
        for step in range(y_size):
            core_copy(step, piece).wait_send()
            near_copy(step, piece).wait_send()
            near_copy(step, piece).wait_recv()
        for step in range(1, y_size):
            y_copy(step, piece).wait_send()
            own_copy(step, piece).wait_send()


def front(rows_size, lat_size, picked, norm_params, bias_row, w_joined, w_attn_out, w_mlp_in, w_mlp_out,
          turns, code_lanes, mask_tiles, dec_shard, own, left, right, across):
    group, depth = picked.shape
    tokens = group // lat_size
    shard, latents = dec_shard.shape
    x_size = rows_size // Z_CHIPS
    y_size = lat_size // CORES
    pieces = tokens // PIECE
    dma = pltpu.SemaphoreType.DMA
    vmem = pl.BlockSpec(memory_space=pltpu.VMEM)
    hbm = pl.BlockSpec(memory_space=pl.ANY)
    hops = Z_CHIPS - 1
    return pl.pallas_call(
        functools.partial(front_kernel, rows_size, lat_size),
        out_shape=[
            jax.ShapeDtypeStruct((group, depth), bf16),
            jax.ShapeDtypeStruct((depth, latents), bf16),
            jax.ShapeDtypeStruct((depth, latents), bf16),
            jax.ShapeDtypeStruct((1, latents), f32),
            jax.ShapeDtypeStruct((1, latents), f32),
            jax.ShapeDtypeStruct((1, latents), f32),
            jax.ShapeDtypeStruct((8, depth), f32),
        ],
        in_specs=[vmem] * 5 + [hbm] * 6 + [vmem] * 4,
        out_specs=[hbm] * 3 + [vmem] * 4,
        scratch_shapes=[
            pltpu.VMEM((y_size, tokens, depth), bf16),
            pltpu.VMEM((y_size - 1, tokens, depth), bf16),
            pltpu.VMEM((tokens, depth), f32),
            pltpu.VMEM((tokens, depth), bf16),
            pltpu.VMEM((tokens, depth), bf16),
            pltpu.VMEM((tokens, depth), bf16),
            pltpu.VMEM((tokens, depth), bf16),
            pltpu.VMEM((tokens, depth), bf16),
            pltpu.VMEM((16, latents // 8), f32),
            pltpu.VMEM((rows_size - 1, 16, latents // 8), f32),
            *[pltpu.VMEM(a.shape, a.dtype) for a in (w_joined, w_attn_out, w_mlp_in, w_mlp_out, turns, code_lanes)],
            dma((6,)), dma((x_size + 3, max(pieces, 2))),
            dma((hops, 2)), dma((hops, 2)), dma((hops, 2)), dma((hops, 2)),
            dma((Z_CHIPS, 2, x_size - 1)), dma((Z_CHIPS, 2, x_size - 1)),
            dma((rows_size - 1,)), dma((rows_size - 1,)),
            dma((y_size, pieces)), dma((y_size, pieces)),
            dma((y_size - 1, pieces)), dma((y_size - 1, pieces)),
            dma((y_size - 1, pieces)), dma((y_size - 1, pieces)),
            dma((y_size, pieces)), dma((y_size, pieces)),
        ],
        compiler_params=pltpu.CompilerParams(
            collective_id=3, has_side_effects=True, vmem_limit_bytes=60 * 2**20),
        name="front",
    )(picked, norm_params, bias_row, mask_tiles, dec_shard,
      w_joined, w_attn_out, w_mlp_in, w_mlp_out, turns, code_lanes, own, left, right, across)


def turn_tables(length):
    half = ROT // 2
    freqs = np.float32(10000.0) ** (np.float32(-2.0) * np.arange(half, dtype=np.float32) / np.float32(ROT))
    angles = np.arange(length, dtype=np.float32)[:, None] * np.tile(freqs, PAIR // half)[None, :]
    place = np.arange(PAIR) % HEAD
    cosines, sines = np.cos(angles.astype(np.float64)), np.sin(angles.astype(np.float64))
    return np.stack([
        np.where(place < ROT, cosines, 1.0),
        np.where(place < half, -sines, 0.0),
        np.where((place >= half) & (place < ROT), sines, 0.0),
    ]).astype(np.float32)


def softplus_parts(value):
    power = jnp.exp(value)
    grown = jnp.log(1.0 + power)
    grown = jnp.where(power < 2.0**-8, power * (1.0 - 0.5 * power), grown)
    active = jnp.where(value > 30.0, value, grown)
    return active, jnp.exp(value - active)


def forward_kernel(
    lat_size,
    inputs_hbm, enc_hbm, dec_hbm, mask_hbm, enc_bias_ref, dec_bias_ref, scale_ref,
    active_hbm, slope_hbm, mass_out, back_out, stats_out,
    active_buf, slope_buf, product, partial, own, send_two, units_two, recv_one, recv_two, got_two,
    inputs_ref, enc_ref, dec_ref, mask_ref, load_sem,
    active_sem, slope_sem, out_one, in_one, out_two, in_two, outu_two, inu_two, out_three, in_three, out_four, in_four,
):
    tokens, depth = inputs_ref.shape
    latents = enc_ref.shape[1]
    chunk, span = product.shape[1:]
    halves = [pl.ds(at * span, span) for at in range(latents // span)]
    loads = [pltpu.make_async_copy(inputs_hbm, inputs_ref, load_sem.at[0]), pltpu.make_async_copy(mask_hbm, mask_ref, load_sem.at[1])]
    for at, cols in enumerate(halves):
        loads.append(pltpu.make_async_copy(enc_hbm.at[:, cols], enc_ref.at[:, cols], load_sem.at[2 + 2 * at]))
        loads.append(pltpu.make_async_copy(dec_hbm.at[:, cols], dec_ref.at[:, cols], load_sem.at[3 + 2 * at]))
    for load in loads:
        load.start()

    width = active_hbm.shape[2]
    chunks, spans = tokens // chunk, latents // span
    y_size = lat_size // CORES
    share = chunk // lat_size
    strip = 32
    row = lax.axis_index("rows")
    lat = lax.axis_index("lat")
    my_y, core = lat // CORES, lax.rem(lat, CORES)
    other = 1 - core

    def y_peer(step):
        return lax.rem(my_y + step, y_size)

    def share_rows(y, which_core):
        return pl.multiple_of((y * CORES + which_core) * share, share)

    def token_rows(block, y, which_core):
        return pl.ds(pl.multiple_of(block * chunk + (y * CORES + which_core) * share, share), share)

    def remote(src, dst, send, recv, target):
        return pltpu.make_async_remote_copy(
            src_ref=src, dst_ref=dst, send_sem=send, recv_sem=recv,
            device_id=(row, target), device_id_type=MESH)

    def copy_one(block, y):
        slot = lax.rem(block, 2)
        return remote(
            partial.at[slot, pl.ds(share_rows(y, other), share)], recv_one.at[block, y],
            out_one.at[slot, y], in_one.at[block, y], my_y * CORES + other)

    def copies_two(block, step):
        slot = lax.rem(block, 2)
        target = y_peer(step) * CORES + core
        return [
            remote(send_two.at[slot, step - 1], recv_two.at[block, step - 1],
                   out_two.at[slot, step - 1], in_two.at[block, step - 1], target),
            remote(units_two.at[slot, step - 1], got_two.at[block, step - 1],
                   outu_two.at[slot, step - 1], inu_two.at[block, step - 1], target),
        ]

    def copy_three(block, step):
        mine = back_out.at[token_rows(block, my_y, core)]
        return remote(
            mine, mine, out_three.at[block, step - 1], in_three.at[block, step - 1], y_peer(step) * CORES + core)

    def copy_four(block, y):
        mine = back_out.at[token_rows(block, y, core)]
        return remote(mine, mine, out_four.at[block, y], in_four.at[block, y], my_y * CORES + other)

    def stores(block, at, slot):
        rows = pl.ds(pl.multiple_of(block * chunk, chunk), chunk)
        copies = []
        for part in range(span // width):
            lanes = pl.ds(part * width, width)
            copies.append(pltpu.make_async_copy(
                active_buf.at[slot, :, lanes], active_hbm.at[at * (span // width) + part, rows], active_sem.at[slot, part]))
            copies.append(pltpu.make_async_copy(
                slope_buf.at[slot, :, lanes], slope_hbm.at[at * (span // width) + part, rows], slope_sem.at[slot, part]))
        return copies

    barrier = pltpu.get_barrier_semaphore()
    pl.semaphore_signal(barrier, inc=1, device_id=(row, my_y * CORES + other), device_id_type=MESH)
    for step in range(1, y_size):
        pl.semaphore_signal(barrier, inc=1, device_id=(row, y_peer(step) * CORES + core), device_id_type=MESH)
    mass_out[...] = jnp.zeros_like(mass_out)
    stats_out[...] = jnp.zeros_like(stats_out)
    pl.semaphore_wait(barrier, y_size)

    def compute(block):
        place = lax.rem(block, 2)
        first = pl.multiple_of(block * chunk, chunk)

        @pl.when(block >= 2)
        def _():
            for y in range(y_size):
                copy_one(block - 2, y).wait_send()

        for at in range(spans):
            slot = at % 2
            if at >= 2:
                for copy in stores(block, at - 2, slot):
                    copy.wait()
            else:
                @pl.when(block > 0)
                def _():
                    for copy in stores(block - 1, spans - 2 + at, slot):
                        copy.wait()

            @pl.when(block == 0)
            def _():
                for load in loads[2 * at + 2 : 2 * at + 4] + (loads[:2] if at == 0 else []):
                    load.wait()

            product[slot] = jnp.dot(
                inputs_ref[pl.ds(first, chunk), :], enc_ref[:, at * span : (at + 1) * span], preferred_element_type=f32)
            for left in range(0, span, width):
                lanes = pl.ds(left, width)
                cols = pl.ds(at * span + left, width)
                shift = enc_bias_ref[:, cols]
                total = mass_out[:, cols]
                for top in range(0, chunk, strip):
                    rows = pl.ds(top, strip)
                    mask = mask_ref[pl.ds(first + top, strip), :]
                    mask = jnp.concatenate([mask] * (width // 128), axis=1)
                    active, slope = softplus_parts(product[slot, rows, lanes] + shift)
                    active_buf[slot, rows, lanes] = active.astype(bf16)
                    slope_buf[slot, rows, lanes] = slope * mask
                    total = total + (active * mask).reshape(strip // 8, 8, width).sum(0)
                mass_out[:, cols] = total
            for copy in stores(block, at, slot):
                copy.start()
            part = lax.dot_general(
                active_buf[slot], dec_ref[:, at * span : (at + 1) * span], (((1,), (1,)), ((), ())),
                preferred_element_type=f32)
            partial[place] = part if at == 0 else partial[place] + part

    def exchange(block):
        slot = lax.rem(block, 2)
        for y in range(y_size):
            copy_one(block, y).wait_recv()
        for step in list(range(1, y_size)) + [0]:
            y = y_peer(step)
            total = partial[slot, pl.ds(share_rows(y, core), share), :] + recv_one[block, y]
            if step == 0:
                own[slot] = total
            else:
                @pl.when(block >= 2)
                def _():
                    for copy in copies_two(block - 2, step):
                        copy.wait_send()

                code, unit = encode(total)
                send_two[slot, step - 1] = code
                put_units(units_two, (slot, step - 1), unit)
                for copy in copies_two(block, step):
                    copy.start()

    def settle(block):
        slot = lax.rem(block, 2)
        rows = token_rows(block, my_y, core)
        total = own[slot]
        for step in range(1, y_size):
            for copy in copies_two(block, step):
                copy.wait_recv()
            total = total + decode(recv_two[block, step - 1], get_units(got_two, (block, step - 1), depth))
        error = total + dec_bias_ref[...] - inputs_ref[rows, :].astype(f32)
        mask = jnp.concatenate([mask_ref[rows, :]] * (depth // 128), axis=1)
        low = (scale_ref[0:1, :] * mask * error).astype(bf16)
        back_out[rows, :] = low
        stats_out[0:8, :] += (mask * error * error).reshape(share // 8, 8, depth).sum(0)
        stats_out[8:16, :] += low.astype(f32).reshape(share // 8, 8, depth).sum(0)
        for step in range(1, y_size):
            copy_three(block, step).start()

    def spread(block):
        for step in range(1, y_size):
            copy_three(block, step).wait_recv()
        for y in range(y_size):
            copy_four(block, y).start()

    def turn(block, carry):
        @pl.when(block < chunks)
        def _():
            compute(block)
            for y in range(y_size):
                copy_one(block, y).start()

        @pl.when((block >= 1) & (block <= chunks))
        def _():
            exchange(block - 1)

        @pl.when((block >= 2) & (block <= chunks + 1))
        def _():
            settle(block - 2)

        @pl.when(block >= 3)
        def _():
            spread(block - 3)

        return carry

    lax.fori_loop(0, chunks + 3, turn, 0)
    for slot in range(2):
        for copy in stores(chunks - 1, spans - 2 + slot, slot):
            copy.wait()
    for block in range(chunks - 2, chunks):
        for y in range(y_size):
            copy_one(block, y).wait_send()
        for step in range(1, y_size):
            for copy in copies_two(block, step):
                copy.wait_send()

    def drain(block, carry):
        for step in range(1, y_size):
            copy_three(block, step).wait_send()
        for y in range(y_size):
            copy_four(block, y).wait_send()
            copy_four(block, y).wait_recv()
        return carry

    lax.fori_loop(0, chunks, drain, 0)


def forward(lat_size, inputs, enc_low, dec_cols, enc_bias_row, mask_lanes, dec_bias_row, scale_rows):
    tokens, depth = inputs.shape
    latents = enc_low.shape[1]
    chunk, span, width = 512, 1024, (512 if tokens <= 4096 else 256)
    chunks = tokens // chunk
    y_size = lat_size // CORES
    share = chunk // lat_size
    dma = pltpu.SemaphoreType.DMA
    vmem = pl.BlockSpec(memory_space=pltpu.VMEM)
    hbm = pl.BlockSpec(memory_space=pl.ANY)
    return pl.pallas_call(
        functools.partial(forward_kernel, lat_size),
        out_shape=[
            jax.ShapeDtypeStruct((latents // width, tokens, width), bf16),
            jax.ShapeDtypeStruct((latents // width, tokens, width), f32),
            jax.ShapeDtypeStruct((8, latents), f32),
            jax.ShapeDtypeStruct((tokens, depth), bf16),
            jax.ShapeDtypeStruct((16, depth), f32),
        ],
        in_specs=[hbm] * 4 + [vmem] * 3,
        out_specs=[hbm, hbm, vmem, vmem, vmem],
        scratch_shapes=[
            pltpu.VMEM((2, chunk, span), bf16),
            pltpu.VMEM((2, chunk, span), f32),
            pltpu.VMEM((2, chunk, span), f32),
            pltpu.VMEM((2, chunk, depth), f32),
            pltpu.VMEM((2, share, depth), f32),
            pltpu.VMEM((2, y_size - 1, share, depth), jnp.int16),
            pltpu.VMEM((2, y_size - 1, 8, 128), f32),
            pltpu.VMEM((chunks, y_size, share, depth), f32),
            pltpu.VMEM((chunks, y_size - 1, share, depth), jnp.int16),
            pltpu.VMEM((chunks, y_size - 1, 8, 128), f32),
            *[pltpu.VMEM(a.shape, a.dtype) for a in (inputs, enc_low, dec_cols, mask_lanes)],
            dma((2 + 2 * (latents // span),)),
            dma((2, span // width)), dma((2, span // width)),
            dma((2, y_size)), dma((chunks, y_size)),
            dma((2, y_size - 1)), dma((chunks, y_size - 1)),
            dma((2, y_size - 1)), dma((chunks, y_size - 1)),
            dma((chunks, y_size - 1)), dma((chunks, y_size - 1)),
            dma((chunks, y_size)), dma((chunks, y_size)),
        ],
        compiler_params=pltpu.CompilerParams(
            collective_id=1, has_side_effects=True, vmem_limit_bytes=60 * 2**20),
        name="forward",
    )(inputs, enc_low, dec_cols, mask_lanes, enc_bias_row, dec_bias_row, scale_rows)


def encode(value):
    top = jnp.max(jnp.abs(value), axis=0, keepdims=True)
    unit = jnp.where(top > 0.0, 32766.0 / top, 0.0)
    shifted = value * unit + 12582912.0
    return (shifted - 12582912.0).astype(jnp.int32).astype(jnp.int16), top * (1.0 / 32766.0)


def decode(code, unit):
    return code.astype(jnp.int32).astype(f32) * unit


def put_units(ref, index, unit):
    for piece in range(unit.shape[1] // 128):
        ref[index + (pl.ds(piece, 1), slice(None))] = unit[:, piece * 128 : piece * 128 + 128]


def get_units(ref, index, width):
    return jnp.concatenate(
        [ref[index + (pl.ds(piece, 1), slice(None))] for piece in range(width // 128)], axis=1)


def backward_kernel(
    rows_size, lat_size,
    back_ref, norms_ref, lasso_ref, pull_ref, mass_ref, stats_ref,
    inputs_hbm, dec_hbm, master_hbm, active_hbm, slope_hbm,
    enc_out, dec_out, bias_out, center_out, totals_out,
    grad_low, active_buf, slope_buf, sums,
    send_one, units_one, recv_one, got_one,
    send_two, units_two, recv_two, got_two,
    bias_rows, pull_cols, facts, tiles, inputs_ref, dec_ref, master_ref, load_sem,
    active_sem, slope_sem,
    out_one, in_one, outu_one, inu_one, out_two, in_two, outu_two, inu_two, out_facts, in_facts, out_tiles, in_tiles,
):
    blocks, tokens, width = active_hbm.shape
    chunk = slope_buf.shape[1]
    chunks = tokens // chunk
    shard = enc_out.shape[0]
    x_size = rows_size // Z_CHIPS
    row = lax.axis_index("rows")
    lat = lax.axis_index("lat")
    my_z, my_x = row // x_size, lax.rem(row, x_size)

    def x_peer(step):
        return lax.rem(my_x + step, x_size)

    def z_peer(step):
        return lax.rem(my_z + step, Z_CHIPS)

    def active_copy(block):
        slot = lax.rem(block, 2)
        return pltpu.make_async_copy(active_hbm.at[block], active_buf.at[slot], active_sem.at[slot])

    def slope_copy(index):
        slot = lax.rem(index, slope_buf.shape[0])
        return pltpu.make_async_copy(
            slope_hbm.at[index // chunks, pl.ds(pl.multiple_of(lax.rem(index, chunks) * chunk, chunk), chunk)],
            slope_buf.at[slot],
            slope_sem.at[slot],
        )

    def copies(stage, block, which, step):
        slot = lax.rem(block, 2)
        if stage == 0:
            target = (my_z * x_size + x_peer(step), lat)
            refs = (send_one, recv_one, out_one, in_one, units_one, got_one, outu_one, inu_one)
        else:
            target = (z_peer(step) * x_size + my_x, lat)
            refs = (send_two, recv_two, out_two, in_two, units_two, got_two, outu_two, inu_two)
        return [
            pltpu.make_async_remote_copy(
                src_ref=refs[at].at[slot, which, step - 1], dst_ref=refs[at + 1].at[block, which, step - 1],
                send_sem=refs[at + 2].at[slot, which, step - 1], recv_sem=refs[at + 3].at[block, which, step - 1],
                device_id=target, device_id_type=MESH)
            for at in (0, 4)
        ]

    devices = rows_size * lat_size
    me = row * lat_size + lat
    latents = dec_ref.shape[1]
    depth = inputs_ref.shape[1]
    part = latents // 8

    def fact_copy(kind, step):
        area = facts.at[kind, row]
        return pltpu.make_async_remote_copy(
            src_ref=area, dst_ref=area, send_sem=out_facts.at[kind, step], recv_sem=in_facts.at[kind, row],
            device_id=(lax.rem(row + step, rows_size), lat), device_id_type=MESH)

    def fact_arrival(kind, step):
        source = lax.rem(row + step, rows_size)
        area = facts.at[kind, source]
        return pltpu.make_async_remote_copy(
            src_ref=area, dst_ref=area, send_sem=out_facts.at[kind, step], recv_sem=in_facts.at[kind, source],
            device_id=(source, lat), device_id_type=MESH)

    def tile_copy(kind, step):
        area = tiles.at[kind, me]
        target = lax.rem(me + step, devices)
        return pltpu.make_async_remote_copy(
            src_ref=area, dst_ref=area, send_sem=out_tiles.at[kind, step], recv_sem=in_tiles.at[kind, me],
            device_id=(target // lat_size, lax.rem(target, lat_size)), device_id_type=MESH)

    def tile_arrival(kind, step):
        source = lax.rem(me + step, devices)
        area = tiles.at[kind, source]
        return pltpu.make_async_remote_copy(
            src_ref=area, dst_ref=area, send_sem=out_tiles.at[kind, step], recv_sem=in_tiles.at[kind, source],
            device_id=(source // lat_size, lax.rem(source, lat_size)), device_id_type=MESH)

    def over_devices(action):
        def turn(step, carry):
            action(step)
            return carry

        lax.fori_loop(1, devices, turn, 0)

    def share_row(kind, value):
        for at in range(8):
            facts[kind, row, pl.ds(at, 1), :] = value[:, at * part : (at + 1) * part]
        for step in range(1, rows_size):
            fact_copy(kind, step).start()

    def shared_row(kind):
        for step in range(1, rows_size):
            fact_arrival(kind, step).wait_recv()
        total = facts[kind, 0]
        for source in range(1, rows_size):
            total = total + facts[kind, source]
        return jnp.concatenate([total[at : at + 1, :] for at in range(8)], axis=1)

    def share_tile(kind, value):
        tiles[kind, me] = value

        def start(step):
            tile_copy(kind, step).start()

        over_devices(start)

    def shared_tile(kind):
        def wait(step):
            tile_arrival(kind, step).wait_recv()

        over_devices(wait)
        return lax.fori_loop(1, devices, lambda source, total: total + tiles[kind, source], tiles[kind, 0])

    barrier = pltpu.get_barrier_semaphore()

    def greet(step):
        target = lax.rem(me + step, devices)
        pl.semaphore_signal(
            barrier, inc=1, device_id=(target // lat_size, lax.rem(target, lat_size)), device_id_type=MESH)

    over_devices(greet)
    loads = [
        pltpu.make_async_copy(source, target, load_sem.at[at])
        for at, (source, target) in enumerate(((dec_hbm, dec_ref), (inputs_hbm, inputs_ref), (master_hbm, master_ref)))
    ]
    active_copy(0).start()
    for load in loads:
        load.start()
    ahead = slope_buf.shape[0] - 1
    for index in range(ahead):
        slope_copy(index).start()
    pl.semaphore_wait(barrier, devices - 1)
    share_row(0, jnp.sum(mass_ref[...], axis=0, keepdims=True))
    center = jnp.sum(stats_ref[8:16, :], axis=0, keepdims=True)
    square = jnp.sum(stats_ref[0:8, :], keepdims=True)
    quarter = depth // 4
    share_tile(0, jnp.concatenate(
        [center[:, at * quarter : (at + 1) * quarter] for at in range(4)]
        + [jnp.broadcast_to(square, (4, quarter))], axis=0))

    def columns(block):
        return pl.ds(pl.multiple_of(block * width, width), width)

    over_tokens = (((0,), (0,)), ((), ()))

    def compute_dec(block):
        slot = lax.rem(block, 2)

        @pl.when(block + 1 < blocks)
        def _():
            active_copy(block + 1).start()

        active_copy(block).wait()
        sums[slot, 1] = lax.dot_general(back_ref[...], active_buf[slot], over_tokens, preferred_element_type=f32)

    def compute_enc(block):
        slot = lax.rem(block, 2)
        cols = columns(block)

        @pl.when(block == 0)
        def _():
            for load in loads:
                load.wait()

        def piece(index, total):
            at = block * chunks + index

            @pl.when(at + ahead < blocks * chunks)
            def _():
                slope_copy(at + ahead).start()

            slope_copy(at).wait()
            rows = pl.ds(pl.multiple_of(index * chunk, chunk), chunk)
            back = jnp.dot(back_ref[rows, :], dec_ref[:, cols], preferred_element_type=f32)
            low = ((back + lasso_ref[:, cols]) * slope_buf[lax.rem(at, ahead + 1)]).astype(bf16)
            grad_low[rows, :] = low
            return total + low.astype(f32).reshape(chunk // 8, 8, width).sum(0)

        bias_rows[:, cols] = lax.fori_loop(0, chunks, piece, jnp.zeros((8, width), f32))
        sums[slot, 0] = lax.dot_general(inputs_ref[...], grad_low[...], over_tokens, preferred_element_type=f32)

    def send_x(block, which):
        slot = lax.rem(block, 2)
        for step in range(1, x_size):
            @pl.when(block >= 2)
            def _():
                for copy in copies(0, block - 2, which, step):
                    copy.wait_send()

            parts = []
            for z in range(Z_CHIPS):
                first = pl.multiple_of((z * x_size + x_peer(step)) * shard, shard)
                parts.append(sums[slot, which, pl.ds(first, shard), :])
            code, unit = encode(jnp.concatenate(parts, axis=0))
            for z in range(Z_CHIPS):
                send_one[slot, which, step - 1, z] = code[z * shard : (z + 1) * shard]
            put_units(units_one, (slot, which, step - 1), unit)
            for copy in copies(0, block, which, step):
                copy.start()

    def send_z(block, which):
        slot = lax.rem(block, 2)
        for step in range(1, x_size):
            for copy in copies(0, block, which, step):
                copy.wait_recv()
        for step in range(Z_CHIPS):
            z = z_peer(step)
            if step:
                @pl.when(block >= 2)
                def _():
                    for copy in copies(1, block - 2, which, step):
                        copy.wait_send()

            first = pl.multiple_of((z * x_size + my_x) * shard, shard)
            total = sums[slot, which, pl.ds(first, shard), :]
            for x_step in range(1, x_size):
                total = total + decode(
                    recv_one[block, which, x_step - 1, z], get_units(got_one, (block, which, x_step - 1), width))
            if step == 0:
                (enc_out, dec_out)[which][:, columns(block)] = total
            else:
                code, unit = encode(total)
                send_two[slot, which, step - 1] = code
                put_units(units_two, (slot, which, step - 1), unit)
                for copy in copies(1, block, which, step):
                    copy.start()

    def finish(block, which):
        slot = lax.rem(block, 2)
        for step in range(1, Z_CHIPS):
            for copy in copies(1, block, which, step):
                copy.wait_recv()
        out, cols = (enc_out, dec_out)[which], columns(block)
        total = out[:, cols]
        for step in range(1, Z_CHIPS):
            total = total + decode(
                recv_two[block, which, step - 1], get_units(got_two, (block, which, step - 1), width))
        out[:, cols] = total

    def turn(block, carry):
        for which, compute in ((1, compute_dec), (0, compute_enc)):
            @pl.when(block < blocks)
            def _():
                compute(block)
                send_x(block, which)

            @pl.when((block >= 1) & (block <= blocks))
            def _():
                send_z(block - 1, which)

            @pl.when(block >= 2)
            def _():
                finish(block - 2, which)

        return carry

    lax.fori_loop(0, blocks, turn, 0)
    share_row(1, jnp.sum(bias_rows[...], axis=0, keepdims=True))
    lax.fori_loop(blocks, blocks + 2, turn, 0)

    mass = shared_row(0)
    bias = shared_row(1)
    bias_out[...] = bias
    pull = mass * pull_ref[...]

    def squares(block, total):
        cols = columns(block)
        gain = dec_out[:, cols] + pull_cols[:, cols] * master_ref[:, cols]
        dec_out[:, cols] = gain
        other = enc_out[:, cols]
        return total + gain * gain + other * other

    pull_cols[...] = pull
    total = jnp.sum(lax.fori_loop(0, blocks, squares, jnp.zeros((shard, width), f32)), keepdims=True)
    leads = jnp.where(row == 0, 1.0, 0.0)
    total = total + leads * jnp.sum(bias * bias, keepdims=True)
    lasso = leads * lasso_coef * jnp.sum(mass * norms_ref[...], keepdims=True)
    share_tile(1, jnp.concatenate(
        [jnp.broadcast_to(total, (4, quarter)), jnp.broadcast_to(lasso, (4, quarter))], axis=0))
    first = shared_tile(0)
    center = jnp.concatenate([first[at : at + 1, :] for at in range(4)], axis=1)
    center_out[...] = center
    second = shared_tile(1)
    squared = second[0:4, :] + jnp.sum(center * center, keepdims=True)
    totals_out[...] = jnp.concatenate([squared, first[4:8, :] + second[4:8, :]], axis=0)
    for kind in range(2):
        for step in range(1, rows_size):
            fact_copy(kind, step).wait_send()

        def sent(step, kind=kind):
            tile_copy(kind, step).wait_send()

        over_devices(sent)
    for block in range(max(blocks - 2, 0), blocks):
        for which in range(2):
            for stage, size in ((0, x_size), (1, Z_CHIPS)):
                for step in range(1, size):
                    for copy in copies(stage, block, which, step):
                        copy.wait_send()


def backward(rows_size, lat_size, inputs, back, dec_cols, norms_row, lasso_row, pull_row, mass_rows, stats, master,
             active, slope):
    blocks, tokens, width = active.shape
    depth = inputs.shape[1]
    shard = depth // rows_size
    latents = dec_cols.shape[1]
    x_size = rows_size // Z_CHIPS
    devices = rows_size * lat_size
    chunk = min(CHUNK, tokens)
    i16 = jnp.int16
    dma = pltpu.SemaphoreType.DMA
    vmem = pl.BlockSpec(memory_space=pltpu.VMEM)
    hbm = pl.BlockSpec(memory_space=pl.ANY)
    return pl.pallas_call(
        functools.partial(backward_kernel, rows_size, lat_size),
        out_shape=[
            jax.ShapeDtypeStruct((shard, latents), f32),
            jax.ShapeDtypeStruct((shard, latents), f32),
            jax.ShapeDtypeStruct((1, latents), f32),
            jax.ShapeDtypeStruct((1, depth), f32),
            jax.ShapeDtypeStruct((8, 128), f32),
        ],
        in_specs=[vmem] * 6 + [hbm] * 5,
        out_specs=[vmem] * 5,
        scratch_shapes=[
            pltpu.VMEM((tokens, width), bf16),
            pltpu.VMEM((2, tokens, width), bf16),
            pltpu.VMEM((SLOTS, chunk, width), f32),
            pltpu.VMEM((2, 2, depth, width), f32),
            pltpu.VMEM((2, 2, x_size - 1, Z_CHIPS, shard, width), i16),
            pltpu.VMEM((2, 2, x_size - 1, 8, 128), f32),
            pltpu.VMEM((blocks, 2, x_size - 1, Z_CHIPS, shard, width), i16),
            pltpu.VMEM((blocks, 2, x_size - 1, 8, 128), f32),
            pltpu.VMEM((2, 2, Z_CHIPS - 1, shard, width), i16),
            pltpu.VMEM((2, 2, Z_CHIPS - 1, 8, 128), f32),
            pltpu.VMEM((blocks, 2, Z_CHIPS - 1, shard, width), i16),
            pltpu.VMEM((blocks, 2, Z_CHIPS - 1, 8, 128), f32),
            pltpu.VMEM((8, latents), f32),
            pltpu.VMEM((1, latents), f32),
            pltpu.VMEM((2, rows_size, 8, latents // 8), f32),
            pltpu.VMEM((2, devices, 8, 128), f32),
            *[pltpu.VMEM(a.shape, a.dtype) for a in (inputs, dec_cols, master)],
            dma((3,)),
            dma((2,)), dma((SLOTS,)),
            dma((2, 2, x_size - 1)), dma((blocks, 2, x_size - 1)),
            dma((2, 2, x_size - 1)), dma((blocks, 2, x_size - 1)),
            dma((2, 2, Z_CHIPS - 1)), dma((blocks, 2, Z_CHIPS - 1)),
            dma((2, 2, Z_CHIPS - 1)), dma((blocks, 2, Z_CHIPS - 1)),
            dma((2, rows_size)), dma((2, rows_size)), dma((2, devices)), dma((2, devices)),
        ],
        compiler_params=pltpu.CompilerParams(
            collective_id=2, has_side_effects=True, vmem_limit_bytes=61 * 2**20),
        name="backward",
    )(back, norms_row, lasso_row, pull_row, mass_rows, stats, inputs, dec_cols, master, active, slope)


def update_kernel(
    totals_ref, counts_ref, enc_grad, dec_grad, enc_bias_grad, dec_bias_grad,
    enc_w, enc_m, enc_s, dec_w, dec_m, dec_s, enc_b, enc_bm, enc_bs, dec_b, dec_bm, dec_bs,
    enc_w_out, enc_m_out, enc_s_out, dec_w_out, dec_m_out, dec_s_out,
    enc_b_out, enc_bm_out, enc_bs_out, dec_b_out, dec_bm_out, dec_bs_out, scalars_out,
):
    norm = jnp.sqrt(totals_ref[0:1, 0:1])
    factor = clip_bound / jnp.maximum(norm, clip_bound)
    groups = (
        (enc_grad, (enc_w, enc_m, enc_s), (enc_w_out, enc_m_out, enc_s_out), weight_decay),
        (dec_grad, (dec_w, dec_m, dec_s), (dec_w_out, dec_m_out, dec_s_out), weight_decay),
        (enc_bias_grad, (enc_b, enc_bm, enc_bs), (enc_b_out, enc_bm_out, enc_bs_out), 0.0),
        (dec_bias_grad, (dec_b, dec_bm, dec_bs), (dec_b_out, dec_bm_out, dec_bs_out), 0.0),
    )
    for grad, olds, news, decay in groups:
        found = adam_update(*[old[...] for old in olds], grad[...] * factor, decay)
        for new, value in zip(news, found):
            new[...] = value
    scalars_out[0:1, :] = jnp.broadcast_to(norm, (1, 128))
    scalars_out[1:2, :] = totals_ref[4:5, :]
    scalars_out[2:8, :] = counts_ref[2:8, :]


def update(totals, counts, grads, states):
    shard, latents = grads[0].shape
    depth = grads[3].shape[1]
    span = latents // 8
    wide = pl.BlockSpec((shard, span), lambda i: (0, i))
    row = pl.BlockSpec((1, span), lambda i: (0, i))
    short = pl.BlockSpec((1, depth), lambda i: (0, 0))
    tile = pl.BlockSpec((8, 128), lambda i: (0, 0))
    state_specs = [wide] * 6 + [row] * 3 + [short] * 3
    return pl.pallas_call(
        update_kernel,
        grid=(latents // span,),
        out_shape=[jax.ShapeDtypeStruct(a.shape, f32) for a in states] + [jax.ShapeDtypeStruct((8, 128), f32)],
        in_specs=[tile, tile, wide, wide, row, short] + state_specs,
        out_specs=state_specs + [tile],
        compiler_params=pltpu.CompilerParams(vmem_limit_bytes=61 * 2**20),
        name="update",
    )(totals, counts, *grads, *states)


def body(
    token_ids,
    token_mask,
    scale_index,
    embed,
    norm_params,
    frozen_bias,
    w_joined,
    w_attn_out,
    w_mlp_in,
    w_mlp_out,
    enc_weight,
    enc_moment,
    enc_second,
    dec_weight,
    dec_moment,
    dec_second,
    enc_bias,
    enc_bias_moment,
    enc_bias_second,
    dec_bias,
    dec_bias_moment,
    dec_bias_second,
):
    lat_size = lax.axis_size("lat")
    lat_index = lax.axis_index("lat")
    group_tokens = token_ids.shape[0]
    tok_local = group_tokens // lat_size
    rows_size = lax.axis_size("rows")
    depth = enc_weight.shape[0] * rows_size
    mask_float = token_mask.astype(f32)
    dec_master = dec_weight.T
    bias_row = frozen_bias[None, :]
    vocab_local = embed.shape[0]
    vocab_first = lat_index * vocab_local
    local_ids = token_ids - vocab_first
    picked = jnp.take(embed, local_ids, axis=0, mode="clip")
    codes = (token_ids // vocab_local * 16 + scale_index).reshape(lat_size // CORES, CORES, tok_local)
    codes = lax.dynamic_index_in_dim(codes, lat_index % CORES, 1, keepdims=False).reshape(-1)
    code_lanes = jnp.broadcast_to(codes[:, None], (codes.shape[0], 128))
    own = jnp.stack([enc_weight.astype(bf16), dec_master.astype(bf16)])
    x_size = rows_size // Z_CHIPS
    right_pairs = [(i, i + x_size) for i in range(rows_size - x_size)]
    left_pairs = [(i + x_size, i) for i in range(rows_size - x_size)]
    from_left = lax.ppermute(own, "rows", right_pairs)
    from_right = lax.ppermute(own, "rows", left_pairs)
    across = []
    for step in range(1, x_size):
        pairs = [(i // x_size * x_size + (i + step) % x_size, i) for i in range(rows_size)]
        across.append(lax.ppermute(own, "rows", pairs))
    mask_lanes = jnp.broadcast_to(mask_float[:, None], (group_tokens, 128))
    all_inputs, enc_low, dec_cols, norms_row, lasso_row, pull_row, scale_rows = front(
        rows_size, lat_size, picked, norm_params, bias_row, w_joined, w_attn_out, w_mlp_in, w_mlp_out,
        turn_tables(tok_local), code_lanes, mask_float.reshape(-1, 128), dec_master,
        own, from_left, from_right, jnp.stack(across))
    active, slope, mass_rows, recon_grad, stats = forward(
        lat_size, all_inputs, enc_low, dec_cols, enc_bias[None, :], mask_lanes, dec_bias[None, :], scale_rows)
    grad_enc, grad_dec, bias_total, center, totals = backward(
        rows_size, lat_size, all_inputs, recon_grad, dec_cols, norms_row, lasso_row, pull_row, mass_rows, stats, dec_master, active, slope)
    states = [
        enc_weight, enc_moment, enc_second, dec_master, dec_moment.T, dec_second.T,
        enc_bias[None, :], enc_bias_moment[None, :], enc_bias_second[None, :],
        dec_bias[None, :], dec_bias_moment[None, :], dec_bias_second[None, :],
    ]
    *fresh, scalars = update(totals, scale_rows, (grad_enc, grad_dec, bias_total, center), states)
    return (
        *fresh[:3],
        *[value.T for value in fresh[3:6]],
        *[value[0] for value in fresh[6:]],
        scalars[0, 0],
        scalars[1, 0],
        scalars[2, 0],
    )


def solution(mesh):
    placed = (
        P("rows"),
        P("rows"),
        P("rows"),
        P("lat", None),
        P(),
        P(),
        P(),
        P(),
        P(),
        P(),
        P("rows", "lat"),
        P("rows", "lat"),
        P("rows", "lat"),
        P("lat", "rows"),
        P("lat", "rows"),
        P("lat", "rows"),
        P("lat"),
        P("lat"),
        P("lat"),
        P(),
        P(),
        P(),
    )
    return jax.shard_map(
        body,
        mesh=mesh,
        in_specs=placed,
        out_specs=(
            P("rows", "lat"),
            P("rows", "lat"),
            P("rows", "lat"),
            P("lat", "rows"),
            P("lat", "rows"),
            P("lat", "rows"),
            P("lat"),
            P("lat"),
            P("lat"),
            P(),
            P(),
            P(),
            P(),
            P(),
            P(),
        ),
        check_vma=False,
    )
```
